32 devices in a mesh: copies: 2 (over x), tensor: 8 (over z, y), dp: 2 (over core).
Axes of the slice: x: 2, y: 2, z: 4, core: 2. Of those that a mesh axis runs over, the one named last changes fastest.
Arguments:
- activations: bfloat16 [32768, 28672], P(('copies', 'dp'), 'tensor'), parts along dimension 0, may hold values from -6 to 6
- out_grads: bfloat16 [32768, 8192], P(('copies', 'dp'), 'tensor'), parts along dimension 0, may hold values from -6 to 6
- proj_in: int32 [28672, 64], P('tensor'), may hold values from 0 to 1
- proj_out: int32 [8192, 64], P('tensor'), may hold values from 0 to 1
- segment_ids: int32 [4, 8192], P(('copies', 'dp')), parts along dimension 0, may hold values from 0 to 63, never falling along the last dimension, each value on 1 to 256 neighbouring positions
- queries: bfloat16 [1024, 4096], P(('copies', 'dp'), 'tensor'), parts along dimension 0, may hold values from -0.0078125 to 0.0078125
Outputs:
- scores: float32 [256, 512], P(('copies', 'dp')), parts along dimension 0
The draws below stay inside these ranges and needn't reach their ends.
There are 2 independent parts, one for each index of `copies`. The reference program is written for one: setup_inputs(seed, part) draws one part's arguments, and reference() takes and returns one part's arrays. A program takes and returns all parts, laid end to end along the dimension named above; an argument that names none is the same for every part. Nothing has to cross between parts.
Inputs may be any that keep to these rules, and one draw needn't show every extreme that they name: `proj_in`: 0 or 1; the projection entry is 2 v - 1. `proj_out`: 0 or 1; the projection entry is 2 v - 1. `segment_ids`: in each row the ids never fall, every id 0 to 63 appears, each sequence has 1 to 256 tokens and one has exactly 256.
All inputs are finite; a program needn't handle non-finite values.
Results may differ from the reference program's by a relative error of at most 0.0052.
Values may be sent and summed in bfloat16 or wider, within the bound.
No kernel may reach another device: no remote copies, remote signals or barrier semaphores. Data moves between devices by JAX's collectives and lax.ppermute only.
A program may use at most 192 MiB of HBM per device.

```python
import math
import jax
import jax.numpy as jnp
import numpy as np

D = 8192
FF = 28672
R = 64
SK = 4096
TOK_DEV = 8192
SEQ_DEV = 64
MOST = 256
QUERIES = 512
TOKENS = 16384
SEQS = 128
N_DP = 2


def with_ends(array, stream_key, low, top_value):
    longest = array.shape.index(max(array.shape))
    spots = []
    for shift in (0, 1):
        where = [jax.random.randint(jax.random.fold_in(stream_key, axis), (), 0, length) for axis, length in enumerate(array.shape)]
        where[longest] = (where[longest] + shift) % array.shape[longest]
        spots.append(tuple(where))
    return array.at[spots[0]].set(low).at[spots[1]].set(top_value)


def block_scale(own_key, shape, shards, low, high):
    def one(dim, parts):
        heights = jax.random.uniform(jax.random.fold_in(jax.random.fold_in(own_key, 6), dim), (parts,), jnp.float32, low / len(shards), high / len(shards))
        return jnp.repeat(jnp.exp(heights), shape[dim] // parts).reshape((-1,) + (1,) * (len(shape) - dim - 1))

    gain = one(*shards[0])
    for cut in shards[1:]:
        gain = gain * one(*cut)
    return gain


def profile(count, total, limit, slope):
    portions = [(1 << 20) // math.isqrt(standing ** slope) + 1 for standing in range(2, count + 1)]
    spare, holding = total - limit - (count - 1), [1] * (count - 1)
    while spare > 0:
        free = [i for i in range(count - 1) if holding[i] < limit]
        pool, budget = sum([portions[i] for i in free]), spare
        for i in free:
            addition = min(limit - holding[i], max(1, budget * portions[i] // pool), spare)
            holding[i] = holding[i] + addition
            spare = spare - addition
    return np.array([limit] + holding)


def uneven_parts(own_key, number_of, total, most, lean):
    if number_of == 2:
        one = jax.random.randint(own_key, (), max(1, total - most), min(most, total - 1) + 1)
        return jnp.stack([one, total - one])
    sizes = jnp.asarray(profile(number_of, total, most, lean), jnp.int32)
    couples = (number_of - 1) // 2
    donor, taker = sizes[1:1 + 2 * couples:2], sizes[2:2 + 2 * couples:2]
    room = jnp.minimum(donor - 1, most - taker)
    shifted = jax.random.randint(jax.random.fold_in(own_key, 1), (couples,), 0, 1 << 20) % (room + 1)
    sizes = sizes.at[1:1 + 2 * couples:2].set(donor - shifted).at[2:2 + 2 * couples:2].set(taker + shifted)
    return sizes[jax.random.permutation(jax.random.fold_in(own_key, 2), number_of)]


def noise(stream_key, shape, spread, reach, pieces=(), kind=jnp.bfloat16):
    array = spread * jax.random.normal(stream_key, shape, jnp.float32)
    if pieces:
        array = array * block_scale(stream_key, shape, pieces, -0.22, 0.18)
    return jnp.clip(array, -reach, reach).astype(kind)


def setup_inputs(seed: int = 0, part: int = 0) -> dict:
    seeds = jax.random.split(jax.random.key(seed), 7)
    own_keys = jax.random.split(jax.random.fold_in(seeds[6], part), 7)
    return {
        "activations": noise(own_keys[0], (TOKENS, FF), 1.0, 6.0, ((0, 2), (1, 8))),
        "out_grads": noise(own_keys[1], (TOKENS, D), 1.0, 6.0, ((0, 2), (1, 8))),
        "proj_in": with_ends(jax.random.randint(seeds[2], (FF, R), 0, 2), jax.random.fold_in(seeds[2], 1), 0, 1).astype(jnp.int32),
        "proj_out": with_ends(jax.random.randint(seeds[3], (D, R), 0, 2), jax.random.fold_in(seeds[3], 1), 0, 1).astype(jnp.int32),
        "segment_ids": jax.vmap(lambda own: jnp.searchsorted(jnp.cumsum(uneven_parts(own, SEQ_DEV, TOK_DEV, MOST, 2)), jnp.arange(TOK_DEV), side="right"))(jax.random.split(own_keys[4], N_DP)).reshape((N_DP, TOK_DEV)).astype(jnp.int32),
        "queries": noise(own_keys[5], (QUERIES, SK), (SK * MOST // 2) ** -0.5, 0.0078125, ((0, 2), (1, 8))),
    }


def reference(activations, out_grads, proj_in, proj_out, segment_ids, queries):
    signs_in = (2 * proj_in - 1).astype(jnp.bfloat16)
    signs_out = (2 * proj_out - 1).astype(jnp.bfloat16)
    proj_a = (jnp.dot(activations, signs_in, preferred_element_type=jnp.float32) * (FF ** -0.5)).astype(jnp.bfloat16)
    proj_g = (jnp.dot(out_grads, signs_out, preferred_element_type=jnp.float32) * (D ** -0.5)).astype(jnp.bfloat16)
    offsets = (jnp.arange(N_DP, dtype=jnp.int32) * SEQ_DEV)[:, None]
    global_ids = (segment_ids + offsets).reshape(-1).astype(jnp.int32)
    outer = proj_a.astype(jnp.float32)[:, :, None] * proj_g.astype(jnp.float32)[:, None, :]
    sketch = jax.ops.segment_sum(outer.reshape(TOKENS, SK), global_ids, num_segments=SEQS)
    sketch = sketch.astype(jnp.bfloat16)
    return jnp.dot(sketch, queries.T, preferred_element_type=jnp.float32)
```

```python
import functools

import jax
import jax.numpy as jnp
from jax import lax
from jax.experimental import pallas as pl
from jax.experimental.pallas import tpu as pltpu
from jax.sharding import PartitionSpec as P

D = 8192
FF = 28672
R = 64
SEQ_DEV = 64
CHUNKS = 4
VMEM = 56 * 1024 * 1024


def project_kernel(quarters, half_ref, act_ref, grad_ref, sin_ref, sout_ref, sent_ref, kept_ref):
    step = pl.program_id(0)
    part_a = jnp.dot(act_ref[...], sin_ref[...], preferred_element_type=jnp.float32)
    part_g = jnp.dot(grad_ref[...], sout_ref[...], preferred_element_type=jnp.float32)
    part_a = (part_a * FF ** -0.5).T
    part_g = (part_g * D ** -0.5).T

    @pl.when(step < quarters)
    def _():
        sent_ref[0, :R, :] = part_a.astype(jnp.bfloat16)
        sent_ref[0, R:, :] = part_g.astype(jnp.bfloat16)

    @pl.when(step >= quarters)
    def _():
        kept_ref[0, :R, :] = part_a
        kept_ref[0, R:, :] = part_g


def project(chunk, quarters, half, activations, out_grads, signs_in, signs_out):
    tokens, width_in = activations.shape
    width_out = out_grads.shape[1]
    steps = 2 * quarters
    tile = tokens // (CHUNKS * steps)

    def rows(s, half_ref):
        mine = (s >= quarters).astype(jnp.int32)
        side = half_ref[0] * mine + (1 - half_ref[0]) * (1 - mine)
        return (chunk * steps + side * quarters + s - mine * quarters, 0)

    fixed = lambda s, half_ref: (0, 0)
    return pl.pallas_call(
        functools.partial(project_kernel, quarters),
        grid_spec=pltpu.PrefetchScalarGridSpec(
            num_scalar_prefetch=1,
            grid=(steps,),
            in_specs=[
                pl.BlockSpec((tile, width_in), rows),
                pl.BlockSpec((tile, width_out), rows),
                pl.BlockSpec((width_in, R), fixed),
                pl.BlockSpec((width_out, R), fixed),
            ],
            out_specs=[
                pl.BlockSpec((1, 2 * R, tile), lambda s, half_ref: (jnp.minimum(s, quarters - 1), 0, 0)),
                pl.BlockSpec((1, 2 * R, tile), lambda s, half_ref: (jnp.maximum(s - quarters, 0), 0, 0)),
            ],
        ),
        out_shape=[
            jax.ShapeDtypeStruct((quarters, 2 * R, tile), jnp.bfloat16),
            jax.ShapeDtypeStruct((quarters, 2 * R, tile), jnp.float32),
        ],
        compiler_params=pltpu.CompilerParams(vmem_limit_bytes=VMEM),
        cost_estimate=pl.CostEstimate(
            flops=2 * tile * steps * (width_in + width_out) * R,
            bytes_accessed=2 * tile * steps * (width_in + width_out),
            transcendentals=0,
        ),
        name="project",
    )(half, activations, out_grads, signs_in, signs_out)


def sketch_kernel(per_dest, ids_ref, *refs):
    piece_refs, out_ref, proj_ref, spread_ref = refs[:-3], refs[-3], refs[-2], refs[-1]
    dest = pl.program_id(0)
    tile = piece_refs[0].shape[-1]

    @pl.when(dest == 0)
    def _():
        for c, piece_ref in enumerate(piece_refs):
            proj_ref[:, c * tile:(c + 1) * tile] = jnp.sum(piece_ref[...].astype(jnp.float32), axis=0)

    for r in range(per_dest):
        row = proj_ref[pl.ds(dest * per_dest + r, 1), :]
        spread_ref[r * R:(r + 1) * R, :] = (row * proj_ref[R:, :]).astype(jnp.bfloat16)
    numbers = lax.broadcasted_iota(jnp.int32, (SEQ_DEV, 1), 0)
    member = (ids_ref[...] == numbers).astype(jnp.bfloat16)
    part = lax.dot_general(
        spread_ref[...], member, (((1,), (1,)), ((), ())), preferred_element_type=jnp.float32
    )
    out_ref[0] = part.T.astype(jnp.bfloat16)


def sketch(ids, pieces, dests):
    per_dest = R // dests
    sources, both, tile = pieces[0].shape
    owned = tile * len(pieces)
    return pl.pallas_call(
        functools.partial(sketch_kernel, per_dest),
        grid=(dests,),
        in_specs=[pl.BlockSpec((1, owned), lambda s: (0, 0))]
        + [pl.BlockSpec((sources, both, tile), lambda s: (0, 0, 0))] * len(pieces),
        out_specs=pl.BlockSpec((1, SEQ_DEV, per_dest * R), lambda s: (s, 0, 0)),
        out_shape=jax.ShapeDtypeStruct((dests, SEQ_DEV, per_dest * R), jnp.bfloat16),
        scratch_shapes=[
            pltpu.VMEM((both, owned), jnp.float32),
            pltpu.VMEM((per_dest * R, owned), jnp.bfloat16),
        ],
        compiler_params=pltpu.CompilerParams(vmem_limit_bytes=VMEM),
        name="sketch",
    )(ids, *pieces)


def body(n_tensor, activations, out_grads, proj_in, proj_out, segment_ids, queries):
    halves = 2
    quarters = n_tensor // halves
    me = lax.axis_index("tensor")
    swap = [(k, k + 1 - 2 * (k % 2)) for k in range(n_tensor)]
    half = (me % halves).reshape(1)
    by_quarter = [[q * halves + h for q in range(quarters)] for h in range(halves)]

    signs_in = (2 * proj_in - 1).astype(jnp.bfloat16)
    signs_out = (2 * proj_out - 1).astype(jnp.bfloat16)

    other = lax.ppermute(queries, "dp", [(0, 1), (1, 0)])
    first = lax.axis_index("dp") == 0
    queries_0 = jnp.where(first, queries, other)
    queries_1 = jnp.where(first, other, queries)
    all_queries = jnp.concatenate([queries_0, queries_1], axis=0)

    pieces = []
    for c in range(CHUNKS):
        sent, kept = project(c, quarters, half, activations, out_grads, signs_in, signs_out)
        pair = (kept + lax.ppermute(sent, "tensor", swap)).astype(jnp.bfloat16)
        pieces.append(lax.all_to_all(pair, "tensor", 0, 0, axis_index_groups=by_quarter))

    tile = pieces[0].shape[-1]
    ids = segment_ids.reshape(CHUNKS, halves, quarters, tile)
    ids = lax.dynamic_slice(ids, (0, me % halves, me // halves, 0), (CHUNKS, 1, 1, tile)).reshape(1, CHUNKS * tile)
    parts = sketch(ids, pieces, n_tensor)
    entries = jnp.sum(lax.all_to_all(parts, "tensor", 0, 0).astype(jnp.float32), axis=0)
    rounded = lax.reduce_precision(entries, 8, 7)
    high = rounded.astype(jnp.bfloat16)
    low = (entries - rounded).astype(jnp.bfloat16)
    along = (((1,), (1,)), ((), ()))
    scores = lax.dot_general(high, all_queries, along, preferred_element_type=jnp.float32)
    scores = scores + lax.dot_general(low, all_queries, along, preferred_element_type=jnp.float32)
    split = scores.reshape(n_tensor, SEQ_DEV // n_tensor, scores.shape[1])
    mine = jnp.sum(lax.all_to_all(split, "tensor", 0, 0), axis=0)
    spread = jnp.broadcast_to(mine[None], split.shape)
    return lax.all_to_all(spread, "tensor", 0, 0).reshape(scores.shape)


def solution(mesh):
    return jax.shard_map(
        functools.partial(body, mesh.shape["tensor"]),
        mesh=mesh,
        in_specs=(
            P(("copies", "dp"), "tensor"),
            P(("copies", "dp"), "tensor"),
            P("tensor", None),
            P("tensor", None),
            P(("copies", "dp"), None),
            P(("copies", "dp"), "tensor"),
        ),
        out_specs=P(("copies", "dp"), None),
        check_vma=False,
    )
```

```python
import functools

import jax
import jax.numpy as jnp
from jax import lax
from jax.experimental import pallas as pl
from jax.experimental.pallas import tpu as pltpu
from jax.sharding import PartitionSpec as P

D = 8192
FF = 28672
R = 64
SEQ_DEV = 64
CHUNKS = 4
GROUP = 512
VMEM = 56 * 1024 * 1024
LAST = (((1,), (1,)), ((), ()))


def project_kernel(first, quarters, piece, who_ref, act_hbm, grad_hbm, sin_ref, sout_ref, sent_ref, kept_ref, act_buf, grad_buf, sems):
    half, quarter = who_ref[0], who_ref[1]
    count = 2 * quarters

    def copies(p):
        side = 1 - half if p < quarters else half
        row = pl.multiple_of(first + (side * quarters + ((p % quarters) ^ quarter)) * piece, piece)
        here = pl.ds(p * piece, piece)
        return (
            pltpu.make_async_copy(act_hbm.at[pl.ds(row, piece)], act_buf.at[here], sems.at[0, p]),
            pltpu.make_async_copy(grad_hbm.at[pl.ds(row, piece)], grad_buf.at[here], sems.at[1, p]),
        )

    for p in range(count):
        for copy in copies(p):
            copy.start()
    signs_in = (2 * sin_ref[...] - 1).astype(jnp.bfloat16)
    signs_out = (2 * sout_ref[...] - 1).astype(jnp.bfloat16)
    per_group = max(1, min(GROUP, count * piece) // piece)
    for start in range(0, count, per_group):
        for p in range(start, start + per_group):
            for copy in copies(p):
                copy.wait()
        rows = pl.ds(start * piece, per_group * piece)
        part_a = lax.dot_general(act_buf[rows, :], signs_in, LAST, preferred_element_type=jnp.float32)
        part_g = lax.dot_general(grad_buf[rows, :], signs_out, LAST, preferred_element_type=jnp.float32)
        part_a = (part_a * FF ** -0.5).T
        part_g = (part_g * D ** -0.5).T
        for p in range(start, start + per_group):
            at = (p - start) * piece
            out_ref = sent_ref if p < quarters else kept_ref
            out_ref[p % quarters, :R, :] = part_a[:, at:at + piece].astype(out_ref.dtype)
            out_ref[p % quarters, R:, :] = part_g[:, at:at + piece].astype(out_ref.dtype)


def project(first, quarters, piece, who, activations, out_grads, signs_in, signs_out):
    count = 2 * quarters
    rows = count * piece
    width_in, width_out = activations.shape[1], out_grads.shape[1]
    whole = pl.BlockSpec(memory_space=pltpu.VMEM)
    hbm = pl.BlockSpec(memory_space=pl.ANY)
    return pl.pallas_call(
        functools.partial(project_kernel, first, quarters, piece),
        in_specs=[pl.BlockSpec(memory_space=pltpu.SMEM), hbm, hbm, whole, whole],
        out_specs=[whole, whole],
        out_shape=[
            jax.ShapeDtypeStruct((quarters, 2 * R, piece), jnp.bfloat16),
            jax.ShapeDtypeStruct((quarters, 2 * R, piece), jnp.float32),
        ],
        scratch_shapes=[
            pltpu.VMEM((rows, width_in), jnp.bfloat16),
            pltpu.VMEM((rows, width_out), jnp.bfloat16),
            pltpu.SemaphoreType.DMA((2, count)),
        ],
        compiler_params=pltpu.CompilerParams(vmem_limit_bytes=VMEM),
        cost_estimate=pl.CostEstimate(
            flops=2 * rows * (width_in + width_out) * R,
            bytes_accessed=2 * rows * (width_in + width_out),
            transcendentals=0,
        ),
        name="project",
    )(who, activations, out_grads, signs_in, signs_out)


def sketch_kernel(quarters, chunks, has_base, last, who_ref, ids_ref, *refs):
    pieces = refs[:chunks * quarters]
    refs = refs[chunks * quarters:]
    if has_base:
        base_ref, refs = refs[0], refs[1:]
    outs, proj_ref, spread_ref = refs[:-2], refs[-2], refs[-1]
    quarter = who_ref[1]
    piece = pieces[0].shape[1]
    per_dest = R // quarters
    group = min(per_dest, 8)
    width = group * R
    for c in range(chunks):
        total = pieces[c * quarters][...]
        for q in range(1, quarters):
            total = total + pieces[c * quarters + q][...].astype(jnp.float32)
        proj_ref[:, c * piece:(c + 1) * piece] = total
    numbers = lax.broadcasted_iota(jnp.int32, (SEQ_DEV, 1), 0)
    member = (ids_ref[...] == numbers).astype(jnp.float32).T.astype(jnp.bfloat16)
    right = proj_ref[R:, :]
    for d in list(range(1, quarters)) + [0]:
        for s in range(per_dest // group):
            at = (quarter ^ d) * per_dest + s * group
            for r in range(group):
                spread_ref[r * R:(r + 1) * R, :] = (proj_ref[pl.ds(at + r, 1), :] * right).astype(jnp.bfloat16)
            part = jnp.dot(spread_ref[...], member, preferred_element_type=jnp.float32).T
            if has_base:
                part = part + base_ref[d, :, s * width:(s + 1) * width]
            if last:
                outs[d][:, s * width:(s + 1) * width] = part.astype(outs[d].dtype)
            else:
                outs[0][d, :, s * width:(s + 1) * width] = part


def sketch(quarters, last, who, ids, pieces, base):
    chunks = len(pieces) // quarters
    owned = chunks * pieces[0].shape[1]
    width = R // quarters * R
    whole = pl.BlockSpec(memory_space=pltpu.VMEM)
    operands = [who, ids] + pieces + ([] if base is None else [base])
    if last:
        shapes = [jax.ShapeDtypeStruct((SEQ_DEV, width), jnp.bfloat16 if d else jnp.float32) for d in range(quarters)]
    else:
        shapes = [jax.ShapeDtypeStruct((quarters, SEQ_DEV, width), jnp.float32)]
    return pl.pallas_call(
        functools.partial(sketch_kernel, quarters, chunks, base is not None, last),
        in_specs=[pl.BlockSpec(memory_space=pltpu.SMEM)] + [whole] * (len(operands) - 1),
        out_specs=[whole] * len(shapes),
        out_shape=shapes,
        scratch_shapes=[
            pltpu.VMEM((2 * R, owned), jnp.float32),
            pltpu.VMEM((min(R // quarters, 8) * R, owned), jnp.bfloat16),
        ],
        compiler_params=pltpu.CompilerParams(vmem_limit_bytes=VMEM),
        cost_estimate=pl.CostEstimate(flops=2 * owned * R * R * SEQ_DEV, bytes_accessed=4 * quarters * SEQ_DEV * width, transcendentals=0),
        name="sketch",
    )(*operands)


def score_kernel(quarters, who_ref, *refs):
    pieces, query_refs = refs[:quarters], refs[quarters:quarters + 4]
    outs, total_ref = refs[quarters + 4:-1], refs[-1]
    half, quarter, data = who_ref[0], who_ref[1], who_ref[2]
    width = query_refs[0].shape[1]
    count = query_refs[0].shape[0]
    entries = pieces[0][...]
    for piece_ref in pieces[1:]:
        entries = entries + piece_ref[...].astype(jnp.float32)
    high = entries.astype(jnp.bfloat16)
    low = (entries - high.astype(jnp.float32)).astype(jnp.bfloat16)
    both = jnp.concatenate([high, low], axis=0)
    swapped = half == 1
    near = jnp.where(swapped, both[:, width:], both[:, :width])
    far = jnp.where(swapped, both[:, :width], both[:, width:])
    for side in range(2):
        part = lax.dot_general(near, query_refs[2 * side][...], LAST, preferred_element_type=jnp.float32)
        part = part + lax.dot_general(far, query_refs[2 * side + 1][...], LAST, preferred_element_type=jnp.float32)
        place = data if side == 0 else 1 - data
        total_ref[:, pl.ds(pl.multiple_of(place * count, count), count)] = part[:SEQ_DEV] + part[SEQ_DEV:]
    rows = SEQ_DEV // quarters
    for d, out_ref in enumerate(outs):
        out_ref[...] = total_ref[pl.ds(pl.multiple_of((quarter ^ d) * rows, rows), rows), :]


def score(quarters, who, pieces, queries):
    whole = pl.BlockSpec(memory_space=pltpu.VMEM)
    columns = 2 * queries[0].shape[0]
    return pl.pallas_call(
        functools.partial(score_kernel, quarters),
        in_specs=[pl.BlockSpec(memory_space=pltpu.SMEM)] + [whole] * (quarters + 4),
        out_specs=[whole] * quarters,
        out_shape=[jax.ShapeDtypeStruct((SEQ_DEV // quarters, columns), jnp.float32)] * quarters,
        scratch_shapes=[pltpu.VMEM((SEQ_DEV, columns), jnp.float32)],
        compiler_params=pltpu.CompilerParams(vmem_limit_bytes=VMEM),
        name="score",
    )(who, *pieces, *queries)


def place_kernel(quarters, who_ref, *refs):
    rows = refs[0].shape[0]
    for d in range(quarters):
        refs[-1][pl.ds(pl.multiple_of((who_ref[1] ^ d) * rows, rows), rows), :] = refs[d][...]


def place(quarters, who, blocks):
    whole = pl.BlockSpec(memory_space=pltpu.VMEM)
    return pl.pallas_call(
        functools.partial(place_kernel, quarters),
        in_specs=[pl.BlockSpec(memory_space=pltpu.SMEM)] + [whole] * quarters,
        out_specs=whole,
        out_shape=jax.ShapeDtypeStruct((SEQ_DEV, blocks[0].shape[1]), jnp.float32),
        name="place",
    )(who, *blocks)


def plain_scores(half, first, pieces, queries):
    entries = sum([piece.astype(jnp.float32) for piece in pieces])
    near, near_far, far, far_far = queries
    mine = jnp.where(half == 0, jnp.concatenate([near, near_far], 1), jnp.concatenate([near_far, near], 1))
    other = jnp.where(half == 0, jnp.concatenate([far, far_far], 1), jnp.concatenate([far_far, far], 1))
    every = jnp.where(first, jnp.concatenate([mine, other], 0), jnp.concatenate([other, mine], 0))
    rounded = lax.reduce_precision(entries, 8, 7)
    high, low = rounded.astype(jnp.bfloat16), (entries - rounded).astype(jnp.bfloat16)
    total = lax.dot_general(high, every, LAST, preferred_element_type=jnp.float32)
    return lax.psum(total + lax.dot_general(low, every, LAST, preferred_element_type=jnp.float32), "tensor")


def body(n_tensor, activations, out_grads, proj_in, proj_out, segment_ids, queries):
    halves = 2
    quarters = n_tensor // halves
    me = lax.axis_index("tensor")
    half, quarter, data = me % halves, me // halves, lax.axis_index("dp")
    who = jnp.stack([half, quarter, data]).astype(jnp.int32)
    swap = [(k, k ^ 1) for k in range(n_tensor)]

    def across(array):
        return lax.ppermute(array, "tensor", swap)

    def along(array, d):
        return lax.ppermute(array, "tensor", [(k, k ^ (halves * d)) for k in range(n_tensor)])

    signs_in, signs_out = proj_in.T, proj_out.T
    near = across(queries)
    cores = [(0, 1), (1, 0)]
    all_queries = [queries, near, lax.ppermute(queries, "dp", cores), lax.ppermute(near, "dp", cores)]

    tokens = activations.shape[0]
    piece = tokens // (CHUNKS * n_tensor)
    pieces = []
    for c in range(CHUNKS):
        first = c * n_tensor * piece
        sent, kept = project(first, quarters, piece, who, activations, out_grads, signs_in, signs_out)
        got = across(sent)
        pieces.append(kept[0] + got[0].astype(jnp.float32))
        for d in range(1, quarters):
            pieces.append(along((kept[d] + got[d].astype(jnp.float32)).astype(jnp.bfloat16), d))

    ids = segment_ids.reshape(CHUNKS, halves, quarters, piece)
    ids = lax.dynamic_slice(ids, (0, half, quarter, 0), (CHUNKS, 1, 1, piece)).reshape(1, CHUNKS * piece)
    early = (CHUNKS - 1) * piece
    base = sketch(quarters, False, who, ids[:, :early], pieces[:(CHUNKS - 1) * quarters], None)[0]
    parts = sketch(quarters, True, who, ids[:, early:], pieces[(CHUNKS - 1) * quarters:], base)
    entries = [parts[0]] + [along(parts[d], d) for d in range(1, quarters)]
    if queries.shape[1] % 128 or SEQ_DEV % (8 * quarters):
        return plain_scores(half, data == 0, entries, all_queries)
    blocks = score(quarters, who, entries, all_queries)
    mine = blocks[0]
    for d in range(1, quarters):
        mine = mine + along(blocks[d], d)
    mine = mine + across(mine)
    return place(quarters, who, [mine] + [along(mine, d) for d in range(1, quarters)])


def solution(mesh):
    return jax.shard_map(
        functools.partial(body, mesh.shape["tensor"]),
        mesh=mesh,
        in_specs=(
            P(("copies", "dp"), "tensor"),
            P(("copies", "dp"), "tensor"),
            P("tensor", None),
            P("tensor", None),
            P(("copies", "dp"), None),
            P(("copies", "dp"), "tensor"),
        ),
        out_specs=P(("copies", "dp"), None),
        check_vma=False,
    )
```

```python
import functools

import jax
import jax.numpy as jnp
from jax import lax
from jax.experimental import pallas as pl
from jax.experimental.pallas import tpu as pltpu
from jax.sharding import PartitionSpec as P

D = 8192
FF = 28672
R = 64
SEQ_DEV = 64
VMEM = 56 * 1024 * 1024
LAST = (((1,), (1,)), ((), ()))


def project_kernel(scale, by_column, x_ref, bits_ref, out_ref, signs_ref):
    @pl.when(pl.program_id(0) == 0)
    def _():
        signs_ref[...] = (2 * bits_ref[...] - 1).astype(jnp.bfloat16)

    part = lax.dot_general(signs_ref[...], x_ref[...], LAST, preferred_element_type=jnp.float32)
    part = (part * scale).astype(jnp.bfloat16)
    if by_column:
        out_ref[:, 0] = part.reshape(out_ref.shape[0], out_ref.shape[2], part.shape[1])
    else:
        across = out_ref.shape[0]
        tokens = part.shape[1] // across
        for q in range(across):
            out_ref[q, 0] = part[:, q * tokens:(q + 1) * tokens]


def project(x, bits, scale, quarters, by_column, tile):
    tokens, width = x.shape
    per_half = tokens // 2 // tile
    if by_column:
        shape = (quarters, 2, R // quarters, tokens // 2)
        block = (quarters, 1, R // quarters, tile)
        place = lambda s: (0, s // per_half, 0, s % per_half)
    else:
        piece = tokens // 2 // quarters
        shape = (quarters, 2, R, piece)
        across = max(1, tile // piece)
        block = (across, 1, R, min(tile, piece))
        split = max(1, piece // tile)
        place = lambda s: ((s % per_half) // split, s // per_half, 0, (s % per_half) % split)
    out = pl.pallas_call(
        functools.partial(project_kernel, scale, by_column),
        grid=(tokens // tile,),
        in_specs=[pl.BlockSpec((tile, width), lambda s: (s, 0)), pl.BlockSpec((R, width), lambda s: (0, 0))],
        out_specs=pl.BlockSpec(block, place),
        out_shape=jax.ShapeDtypeStruct(shape, jnp.bfloat16),
        scratch_shapes=[pltpu.VMEM((R, width), jnp.bfloat16)],
        compiler_params=pltpu.CompilerParams(vmem_limit_bytes=VMEM),
        cost_estimate=pl.CostEstimate(flops=2 * tokens * width * R, bytes_accessed=2 * tokens * width, transcendentals=0),
        name="project",
    )(x, bits)
    return out.reshape((2 * quarters,) + shape[2:])


def score_kernel(width, ids_ref, left_ref, right_ref, query_ref, out_ref, row_ref, col_ref, member_ref, spread_ref, sketch_ref):
    total = left_ref[0].astype(jnp.float32)
    for source in range(1, left_ref.shape[0]):
        total = total + left_ref[source].astype(jnp.float32)
    row_ref[...] = total
    piece = right_ref.shape[2]
    for q in range(right_ref.shape[0]):
        col_ref[:, q * piece:(q + 1) * piece] = right_ref[q].astype(jnp.float32)
    numbers = lax.broadcasted_iota(jnp.int32, (SEQ_DEV, 1), 0)
    member_ref[...] = (ids_ref[...] == numbers).astype(jnp.bfloat16)
    rows = spread_ref.shape[0] // R
    for first in range(0, row_ref.shape[0], rows):
        for at in range(0, col_ref.shape[1], width):
            right = col_ref[:, at:at + width]
            for r in range(rows):
                spread_ref[r * R:(r + 1) * R, at:at + width] = (row_ref[first + r:first + r + 1, at:at + width] * right).astype(jnp.bfloat16)
        sketch_ref[:, first * R:(first + rows) * R] = lax.dot_general(
            member_ref[...], spread_ref[...], LAST, preferred_element_type=jnp.float32
        )
    entries = sketch_ref[...]
    high = entries.astype(jnp.bfloat16)
    low = (entries - high.astype(jnp.float32)).astype(jnp.bfloat16)
    out_ref[...] = lax.dot_general(high, query_ref[...], LAST, preferred_element_type=jnp.float32) + lax.dot_general(
        low, query_ref[...], LAST, preferred_element_type=jnp.float32
    )


def score(ids, left, right, queries):
    whole = pl.BlockSpec(memory_space=pltpu.VMEM)
    sources, columns, tokens = left.shape
    rows = min(4, columns)
    return pl.pallas_call(
        functools.partial(score_kernel, min(512, tokens)),
        in_specs=[whole] * 4,
        out_specs=whole,
        out_shape=jax.ShapeDtypeStruct((SEQ_DEV, queries.shape[0]), jnp.float32),
        scratch_shapes=[
            pltpu.VMEM((columns, tokens), jnp.float32),
            pltpu.VMEM((R, tokens), jnp.float32),
            pltpu.VMEM((SEQ_DEV, tokens), jnp.bfloat16),
            pltpu.VMEM((rows * R, tokens), jnp.bfloat16),
            pltpu.VMEM((SEQ_DEV, columns * R), jnp.float32),
        ],
        compiler_params=pltpu.CompilerParams(vmem_limit_bytes=VMEM),
        cost_estimate=pl.CostEstimate(flops=2 * tokens * columns * R * SEQ_DEV, bytes_accessed=2 * left.size, transcendentals=0),
        name="score",
    )(ids, left, right, queries)


def body(n_tensor, activations, out_grads, proj_in, proj_out, segment_ids, queries):
    quarters = n_tensor // 2
    by_half = [[2 * q, 2 * q + 1] for q in range(quarters)]
    by_quarter = [[2 * q + h for q in range(quarters)] for h in range(2)]
    half = lax.axis_index("tensor") % 2
    tokens = activations.shape[0]

    part_g = project(out_grads, proj_out.T, D ** -0.5, quarters, False, 1024)
    got_g = lax.all_to_all(part_g, "tensor", 0, 0)
    part_a = project(activations, proj_in.T, FF ** -0.5, quarters, True, 512)
    own_g = jnp.sum(got_g.astype(jnp.float32), axis=0).astype(jnp.bfloat16)
    right = lax.all_gather(own_g, "tensor", axis=0, axis_index_groups=by_quarter)
    left = lax.all_to_all(part_a, "tensor", 0, 0)

    all_queries = lax.all_gather(queries, "dp", axis=0, tiled=True)
    all_queries = lax.all_gather(all_queries, "tensor", axis=1, tiled=True, axis_index_groups=by_half)
    ids = lax.dynamic_slice(segment_ids, (0, half * (tokens // 2)), (1, tokens // 2))
    return lax.psum(score(ids, left, right, all_queries), "tensor")


def solution(mesh):
    return jax.shard_map(
        functools.partial(body, mesh.shape["tensor"]),
        mesh=mesh,
        in_specs=(
            P(("copies", "dp"), "tensor"),
            P(("copies", "dp"), "tensor"),
            P("tensor", None),
            P("tensor", None),
            P(("copies", "dp"), None),
            P(("copies", "dp"), "tensor"),
        ),
        out_specs=P(("copies", "dp"), None),
        check_vma=False,
    )
```

```python
import functools
import math

import jax
import jax.numpy as jnp
from jax import lax
from jax.experimental import pallas as pl
from jax.experimental.pallas import tpu as pltpu
from jax.sharding import PartitionSpec as P

D = 8192
FF = 28672
R = 64
SEQ_DEV = 64
VMEM = 56 * 1024 * 1024
LAST = (((1,), (1,)), ((), ()))


def project_kernel(scale, per, depth, by_column, half_ref, x_ref, bits_ref, *refs):
    sent_ref, kept_ref, signs_ref, total_ref = refs[-4:]
    step = pl.program_id(0)

    @pl.when(step == 0)
    def _():
        signs_ref[...] = (2 * bits_ref[...] - 1).astype(jnp.bfloat16)

    for at in range(0, x_ref.shape[1], depth):
        here = slice(at, at + depth)
        part = lax.dot_general(x_ref[:, here], signs_ref[:, here], LAST, preferred_element_type=jnp.float32)
        total_ref[...] = part if at == 0 else total_ref[...] + part
    part = (total_ref[...] * scale).T

    def store(out_ref):
        if by_column:
            out_ref[...] = part.astype(out_ref.dtype).reshape(out_ref.shape)
        else:
            tokens = out_ref.shape[2]
            for q in range(out_ref.shape[0]):
                out_ref[q] = part[:, q * tokens:(q + 1) * tokens].astype(out_ref.dtype)

    @pl.when(step < per)
    def _():
        store(sent_ref)

    @pl.when(step >= per)
    def _():
        store(kept_ref)


def project(x, bits, half, scale, quarters, by_column, first, count, tile, after=()):
    tokens, width = x.shape
    depth = math.gcd(width, 256)
    per = count // tile
    if by_column:
        shape = (quarters, R // quarters, count)
        block = (quarters, R // quarters, tile)
        place = lambda s: (0, 0, s)
    else:
        piece = count // quarters
        across = max(1, tile // piece)
        split = max(1, piece // tile)
        shape = (quarters, R, piece)
        block = (across, R, min(tile, piece))
        place = lambda s: (s // split, 0, s % split)

    def rows(s, half_ref):
        mine = (s >= per).astype(jnp.int32)
        side = half_ref[0] * mine + (1 - half_ref[0]) * (1 - mine)
        return (side * (tokens // 2 // tile) + first // tile + s - mine * per, 0)

    return pl.pallas_call(
        functools.partial(project_kernel, scale, per, depth, by_column),
        grid_spec=pltpu.PrefetchScalarGridSpec(
            num_scalar_prefetch=1,
            grid=(2 * per,),
            in_specs=[pl.BlockSpec((tile, width), rows), pl.BlockSpec((R, width), lambda s, half_ref: (0, 0))]
            + [pl.BlockSpec(memory_space=pl.ANY)] * len(after),
            out_specs=[
                pl.BlockSpec(block, lambda s, half_ref: place(jnp.minimum(s, per - 1))),
                pl.BlockSpec(block, lambda s, half_ref: place(jnp.maximum(s - per, 0))),
            ],
            scratch_shapes=[pltpu.VMEM((R, width), jnp.bfloat16), pltpu.VMEM((tile, R), jnp.float32)],
        ),
        out_shape=[jax.ShapeDtypeStruct(shape, jnp.bfloat16), jax.ShapeDtypeStruct(shape, jnp.float32)],
        compiler_params=pltpu.CompilerParams(vmem_limit_bytes=VMEM),
        cost_estimate=pl.CostEstimate(flops=4 * count * width * R, bytes_accessed=4 * count * width, transcendentals=0),
        name="project",
    )(half, x, bits, *after)


def score_kernel(width, half_ref, ids_ref, left_ref, right_ref, near_ref, far_ref, out_ref, row_ref, col_ref, member_ref, spread_ref, sketch_ref):
    total = left_ref[0].astype(jnp.float32)
    for source in range(1, left_ref.shape[0]):
        total = total + left_ref[source].astype(jnp.float32)
    row_ref[...] = total
    piece = right_ref.shape[2]
    for q in range(right_ref.shape[0]):
        col_ref[:, q * piece:(q + 1) * piece] = right_ref[q].astype(jnp.float32)
    numbers = lax.broadcasted_iota(jnp.int32, (SEQ_DEV, 1), 0)
    member_ref[...] = (ids_ref[...] == numbers).astype(jnp.bfloat16)
    rows = spread_ref.shape[0] // R
    for first in range(0, row_ref.shape[0], rows):
        for at in range(0, col_ref.shape[1], width):
            right = col_ref[:, at:at + width]
            for r in range(rows):
                spread_ref[r * R:(r + 1) * R, at:at + width] = (row_ref[first + r:first + r + 1, at:at + width] * right).astype(jnp.bfloat16)
        sketch_ref[:, first * R:(first + rows) * R] = lax.dot_general(
            member_ref[...], spread_ref[...], LAST, preferred_element_type=jnp.float32
        )
    entries = sketch_ref[...]
    high = entries.astype(jnp.bfloat16)
    low = (entries - high.astype(jnp.float32)).astype(jnp.bfloat16)
    both = jnp.concatenate([high, low], axis=0)
    middle = both.shape[1] // 2
    swapped = half_ref[0] == 1
    near = jnp.where(swapped, both[:, middle:], both[:, :middle])
    far = jnp.where(swapped, both[:, :middle], both[:, middle:])
    part = lax.dot_general(near, near_ref[...], LAST, preferred_element_type=jnp.float32)
    part = part + lax.dot_general(far, far_ref[...], LAST, preferred_element_type=jnp.float32)
    out_ref[...] = part[:SEQ_DEV] + part[SEQ_DEV:]


def score(half, ids, left, right, near, far):
    whole = pl.BlockSpec(memory_space=pltpu.VMEM)
    sources, columns, tokens = left.shape
    rows = min(4, columns)
    return pl.pallas_call(
        functools.partial(score_kernel, min(512, tokens)),
        in_specs=[pl.BlockSpec(memory_space=pltpu.SMEM)] + [whole] * 5,
        out_specs=whole,
        out_shape=jax.ShapeDtypeStruct((SEQ_DEV, near.shape[0]), jnp.float32),
        scratch_shapes=[
            pltpu.VMEM((columns, tokens), jnp.float32),
            pltpu.VMEM((R, tokens), jnp.float32),
            pltpu.VMEM((SEQ_DEV, tokens), jnp.bfloat16),
            pltpu.VMEM((rows * R, tokens), jnp.bfloat16),
            pltpu.VMEM((SEQ_DEV, columns * R), jnp.float32),
        ],
        compiler_params=pltpu.CompilerParams(vmem_limit_bytes=VMEM),
        cost_estimate=pl.CostEstimate(flops=2 * tokens * columns * R * SEQ_DEV, bytes_accessed=2 * left.size, transcendentals=0),
        name="score",
    )(half, ids, left, right, near, far)


def body(n_tensor, activations, out_grads, proj_in, proj_out, segment_ids, queries):
    quarters = n_tensor // 2
    by_quarter = [[2 * q + h for q in range(quarters)] for h in range(2)]
    half = (lax.axis_index("tensor") % 2).astype(jnp.int32)
    side = half.reshape(1)
    owned = activations.shape[0] // 2

    def swap(array, distance):
        return lax.ppermute(array, "tensor", [(k, k ^ distance) for k in range(n_tensor)])

    def along(array):
        return lax.all_to_all(array, "tensor", 0, 0, axis_index_groups=by_quarter)

    near = lax.all_gather(queries, "dp", axis=0, tiled=True)
    far = swap(near, 1)

    bits_in, bits_out = proj_in.T, proj_out.T
    sent_g, kept_g = project(out_grads, bits_out, side, D ** -0.5, quarters, False, 0, owned, 1024)
    got_g = swap(sent_g, 1)
    sent_0, kept_0 = project(activations, bits_in, side, FF ** -0.5, quarters, True, 0, owned // 2, 1024)
    got_0 = swap(sent_0, 1)
    pair_g = (kept_g + got_g.astype(jnp.float32)).astype(jnp.bfloat16)
    pieces_g = along(pair_g)
    sent_1, kept_1 = project(activations, bits_in, side, FF ** -0.5, quarters, True, owned // 2, owned // 2, 1024, (pair_g,))
    got_1 = swap(sent_1, 1)
    own_g = jnp.sum(pieces_g.astype(jnp.float32), axis=0).astype(jnp.bfloat16)
    right = along(jnp.broadcast_to(own_g[None], pieces_g.shape))
    pair_0 = (kept_0 + got_0.astype(jnp.float32)).astype(jnp.bfloat16)
    pair_1 = (kept_1 + got_1.astype(jnp.float32)).astype(jnp.bfloat16)
    left = along(jnp.concatenate([pair_0, pair_1], axis=2))

    ids = lax.dynamic_slice(segment_ids, (0, half * owned), (1, owned))
    total = score(side, ids, left, right, near, far)
    distance = 1
    while 2 * distance < n_tensor:
        total = total + swap(total, distance)
        distance = 2 * distance
    rounded = total.astype(jnp.bfloat16)
    return rounded.astype(jnp.float32) + swap(rounded, distance).astype(jnp.float32)


def solution(mesh):
    return jax.shard_map(
        functools.partial(body, mesh.shape["tensor"]),
        mesh=mesh,
        in_specs=(
            P(("copies", "dp"), "tensor"),
            P(("copies", "dp"), "tensor"),
            P("tensor", None),
            P("tensor", None),
            P(("copies", "dp"), None),
            P(("copies", "dp"), "tensor"),
        ),
        out_specs=P(("copies", "dp"), None),
        check_vma=False,
    )
```

```python
import functools

import jax
import jax.numpy as jnp
from jax import lax
from jax.experimental import pallas as pl
from jax.experimental.pallas import tpu as pltpu
from jax.sharding import PartitionSpec as P

D = 8192
FF = 28672
R = 64
SEQ_DEV = 64
BUFFERS = 4
VMEM = 56 * 1024 * 1024
LAST = (((1,), (1,)), ((), ()))


def project_kernel(scale, per, order, start, who_ref, x_hbm, bits_ref, *refs):
    sent_ref, kept_ref, signs_ref, x_buf, sems = refs[-5:]
    step = pl.program_id(0)
    steps = 2 * per
    buffers, tile = x_buf.shape[0], x_buf.shape[1]
    slot = lax.rem(step, buffers)

    def copy(s, slot):
        mine = (s >= per).astype(jnp.int32) if isinstance(s, jax.Array) else int(s >= per)
        side = who_ref[0] * mine + (1 - who_ref[0]) * (1 - mine)
        row = pl.multiple_of(side * (x_hbm.shape[0] // 2) + start + (s - mine * per) * tile, tile)
        return pltpu.make_async_copy(x_hbm.at[pl.ds(row, tile)], x_buf.at[slot], sems.at[slot])

    @pl.when(step == 0)
    def _():
        for s in range(min(buffers, steps)):
            copy(s, s).start()
        if order:
            for q in range(order):
                rows = R // order
                bits = bits_ref[pl.ds(pl.multiple_of((q ^ who_ref[1]) * rows, rows), rows), :]
                signs_ref[q * rows:(q + 1) * rows, :] = (2 * bits - 1).astype(jnp.bfloat16)
        else:
            signs_ref[...] = (2 * bits_ref[...] - 1).astype(jnp.bfloat16)

    copy(step, slot).wait()
    part = lax.dot_general(signs_ref[...], x_buf[slot], LAST, preferred_element_type=jnp.float32) * scale

    @pl.when(step + buffers < steps)
    def _():
        copy(step + buffers, slot).start()

    def store(out_ref):
        out_ref[...] = part.astype(out_ref.dtype).reshape(out_ref.shape)

    @pl.when(step < per)
    def _():
        store(sent_ref)

    @pl.when(step >= per)
    def _():
        store(kept_ref)


def project(x, bits, who, scale, quarters, by_column, first, count, tile, after=()):
    tokens, width = x.shape
    piece = count // quarters
    if not by_column:
        tile = min(tile, piece)
    per = count // tile
    order = quarters if by_column and (R // quarters) % 8 == 0 else 0
    if by_column and not order:
        rows = jnp.arange(R, dtype=jnp.int32)
        bits = jnp.take(bits, rows ^ (who[1] * (R // quarters)), axis=0)
    if by_column:
        shape = (quarters, R // quarters, count)
        block = (quarters, R // quarters, tile)
        place = lambda s, who_ref: (0, 0, s)
    else:
        split = piece // tile
        shape = (quarters, R, piece)
        block = (1, R, tile)
        place = lambda s, who_ref: ((s // split) ^ who_ref[1], 0, s % split)

    return pl.pallas_call(
        functools.partial(project_kernel, scale, per, order, first),
        grid_spec=pltpu.PrefetchScalarGridSpec(
            num_scalar_prefetch=1,
            grid=(2 * per,),
            in_specs=[
                pl.BlockSpec(memory_space=pl.ANY),
                pl.BlockSpec((R, width), lambda s, who_ref: (0, 0)),
            ]
            + [pl.BlockSpec(memory_space=pl.ANY)] * len(after),
            out_specs=[
                pl.BlockSpec(block, lambda s, who_ref: place(jnp.minimum(s, per - 1), who_ref)),
                pl.BlockSpec(block, lambda s, who_ref: place(jnp.maximum(s - per, 0), who_ref)),
            ],
            scratch_shapes=[
                pltpu.VMEM((R, width), jnp.bfloat16),
                pltpu.VMEM((BUFFERS, tile, width), jnp.bfloat16),
                pltpu.SemaphoreType.DMA((BUFFERS,)),
            ],
        ),
        out_shape=[jax.ShapeDtypeStruct(shape, jnp.bfloat16), jax.ShapeDtypeStruct(shape, jnp.float32)],
        compiler_params=pltpu.CompilerParams(vmem_limit_bytes=VMEM),
        cost_estimate=pl.CostEstimate(flops=4 * count * width * R, bytes_accessed=4 * count * width, transcendentals=0),
        name="project",
    )(who, x, bits, *after)


def score_kernel(quarters, width, who_ref, ids_ref, near_ref, far_ref, *refs):
    left_refs, right_refs = refs[:quarters], refs[quarters:2 * quarters]
    out_ref, row_ref, col_ref, member_ref, spread_ref, sketch_ref = refs[2 * quarters:]
    half, quarter = who_ref[0], who_ref[1]
    total = left_refs[0][...]
    for left_ref in left_refs[1:]:
        total = total + left_ref[...].astype(jnp.float32)
    row_ref[...] = total
    piece = right_refs[0].shape[1]
    for d, right_ref in enumerate(right_refs):
        col_ref[:, pl.ds(pl.multiple_of((quarter ^ d) * piece, piece), piece)] = right_ref[...].astype(jnp.float32)
    numbers = lax.broadcasted_iota(jnp.int32, (SEQ_DEV, 1), 0)
    member_ref[...] = (ids_ref[...] == numbers).astype(jnp.bfloat16)
    rows = spread_ref.shape[0] // R
    for first in range(0, row_ref.shape[0], rows):
        for at in range(0, col_ref.shape[1], width):
            right = col_ref[:, at:at + width]
            for r in range(rows):
                spread_ref[r * R:(r + 1) * R, at:at + width] = (row_ref[first + r:first + r + 1, at:at + width] * right).astype(jnp.bfloat16)
        sketch_ref[:, first * R:(first + rows) * R] = lax.dot_general(
            member_ref[...], spread_ref[...], LAST, preferred_element_type=jnp.float32
        )
    entries = sketch_ref[...]
    high = entries.astype(jnp.bfloat16)
    low = (entries - high.astype(jnp.float32)).astype(jnp.bfloat16)
    both = jnp.concatenate([high, low], axis=0)
    middle = both.shape[1] // 2
    swapped = half == 1
    near = jnp.where(swapped, both[:, middle:], both[:, :middle])
    far = jnp.where(swapped, both[:, :middle], both[:, middle:])
    part = lax.dot_general(near, near_ref[...], LAST, preferred_element_type=jnp.float32)
    part = part + lax.dot_general(far, far_ref[...], LAST, preferred_element_type=jnp.float32)
    out_ref[...] = part[:SEQ_DEV] + part[SEQ_DEV:]


def score(who, ids, near, far, left, right):
    whole = pl.BlockSpec(memory_space=pltpu.VMEM)
    columns, tokens = left[0].shape
    rows = min(4, columns)
    return pl.pallas_call(
        functools.partial(score_kernel, len(left), min(512, tokens)),
        in_specs=[pl.BlockSpec(memory_space=pltpu.SMEM)] + [whole] * (3 + len(left) + len(right)),
        out_specs=whole,
        out_shape=jax.ShapeDtypeStruct((SEQ_DEV, near.shape[0]), jnp.float32),
        scratch_shapes=[
            pltpu.VMEM((columns, tokens), jnp.float32),
            pltpu.VMEM((R, tokens), jnp.float32),
            pltpu.VMEM((SEQ_DEV, tokens), jnp.bfloat16),
            pltpu.VMEM((rows * R, tokens), jnp.bfloat16),
            pltpu.VMEM((SEQ_DEV, columns * R), jnp.float32),
        ],
        compiler_params=pltpu.CompilerParams(vmem_limit_bytes=VMEM),
        cost_estimate=pl.CostEstimate(flops=2 * tokens * columns * R * SEQ_DEV, bytes_accessed=4 * columns * tokens, transcendentals=0),
        name="score",
    )(who, ids, near, far, *left, *right)


def body(n_tensor, activations, out_grads, proj_in, proj_out, segment_ids, queries):
    quarters = n_tensor // 2
    me = lax.axis_index("tensor").astype(jnp.int32)
    half = me % 2
    who = jnp.stack([half, me // 2])
    owned = activations.shape[0] // 2
    early = owned * 5 // 8

    def swap(array, distance):
        return lax.ppermute(array, "tensor", [(k, k ^ distance) for k in range(n_tensor)])

    near = lax.all_gather(queries, "dp", axis=0, tiled=True)
    far = swap(near, 1)

    bits_in, bits_out = proj_in.T, proj_out.T
    scale_in, scale_out = FF ** -0.5, D ** -0.5
    sent_g, kept_g = project(out_grads, bits_out, who, scale_out, quarters, False, 0, owned, 1024)
    got_g = swap(sent_g, 1)
    sent_0, kept_0 = project(activations, bits_in, who, scale_in, quarters, True, 0, early, 512)
    got_0 = swap(sent_0, 1)
    pair_g = [kept_g[d] + got_g[d].astype(jnp.float32) for d in range(quarters)]
    pair_g = [pair_g[0]] + [pair.astype(jnp.bfloat16) for pair in pair_g[1:]]
    moved_g = [swap(pair_g[d], 2 * d) for d in range(1, quarters)]
    sent_1, kept_1 = project(activations, bits_in, who, scale_in, quarters, True, early, owned - early, 512, pair_g[1:2])
    got_1 = swap(sent_1, 1)
    own_g = sum([moved.astype(jnp.float32) for moved in moved_g], pair_g[0]).astype(jnp.bfloat16)
    right = [own_g] + [swap(own_g, 2 * d) for d in range(1, quarters)]
    left = []
    for d in range(quarters):
        parts = [kept_0[d] + got_0[d].astype(jnp.float32), kept_1[d] + got_1[d].astype(jnp.float32)]
        if d:
            left.append(swap(jnp.concatenate([part.astype(jnp.bfloat16) for part in parts], axis=1), 2 * d))
        else:
            left.append(jnp.concatenate(parts, axis=1))

    ids = lax.dynamic_slice(segment_ids, (0, half * owned), (1, owned))
    total = score(who, ids, near, far, left, right)
    distance = 1
    while 2 * distance < n_tensor:
        total = total + swap(total, distance)
        distance = 2 * distance
    rounded = total.astype(jnp.bfloat16)
    return rounded.astype(jnp.float32) + swap(rounded, distance).astype(jnp.float32)


def solution(mesh):
    return jax.shard_map(
        functools.partial(body, mesh.shape["tensor"]),
        mesh=mesh,
        in_specs=(
            P(("copies", "dp"), "tensor"),
            P(("copies", "dp"), "tensor"),
            P("tensor", None),
            P("tensor", None),
            P(("copies", "dp"), None),
            P(("copies", "dp"), "tensor"),
        ),
        out_specs=P(("copies", "dp"), None),
        check_vma=False,
    )
```

```python
import functools

import jax
import jax.numpy as jnp
from jax import lax
from jax.experimental import pallas as pl
from jax.experimental.pallas import tpu as pltpu
from jax.sharding import PartitionSpec as P

D = 8192
FF = 28672
R = 64
SEQ_DEV = 64
BUFFERS = 4
VMEM = 48 * 1024 * 1024
LAST = (((1,), (1,)), ((), ()))


def project_kernel(scale, order, first, split, who_ref, x_hbm, bits_hbm, *refs):
    sent_ref, kept_ref, bits_ref, signs_ref, x_buf, bits_sem, sems = refs[-7:]
    half, quarter = who_ref[0], who_ref[1]
    buffers, tile = x_buf.shape[0], x_buf.shape[1]
    steps = sent_ref.size // R // tile

    def copy(s, mine):
        slot = lax.rem(s + mine * steps, buffers)
        row = pl.multiple_of((half ^ 1 ^ mine) * (x_hbm.shape[0] // 2) + first + s * tile, tile)
        return pltpu.make_async_copy(x_hbm.at[pl.ds(row, tile)], x_buf.at[slot], sems.at[slot])

    bits_copy = pltpu.make_async_copy(bits_hbm, bits_ref, bits_sem)
    bits_copy.start()
    ahead = min(buffers, steps)
    for s in range(ahead):
        copy(s, 0).start()
    bits_copy.wait()
    for q in range(max(order, 1)):
        rows = R // max(order, 1)
        at = pl.multiple_of((q ^ quarter) * rows, rows) if order else 0
        signs_ref[q * rows:(q + 1) * rows, :] = (2 * bits_ref[pl.ds(at, rows), :] - 1).astype(jnp.bfloat16)

    for mine, out_ref in enumerate((sent_ref, kept_ref)):
        def one(s, carry):
            copy(s, mine).wait()
            slot = lax.rem(s + mine * steps, buffers)
            part = lax.dot_general(signs_ref[...], x_buf[slot], LAST, preferred_element_type=jnp.float32) * scale
            part = part.astype(out_ref.dtype)
            if split:
                here = pl.ds(pl.multiple_of(lax.rem(s, split) * tile, tile), tile)
                out_ref[(s // split) ^ quarter, :, here] = part
            else:
                here = pl.ds(pl.multiple_of(s * tile, tile), tile)
                out_ref[:, :, here] = part.reshape(out_ref.shape[0], out_ref.shape[1], tile)

            @pl.when(s + ahead < steps)
            def _():
                copy(s + ahead, mine).start()

            if not mine:
                @pl.when(s + ahead >= steps)
                def _():
                    copy(s + ahead - steps, 1).start()

            return carry

        lax.fori_loop(0, steps, one, 0)


def project(x, bits, who, scale, quarters, by_column, first, count, tile, after=()):
    width = x.shape[1]
    piece = count // quarters
    order, split = 0, 0
    if not by_column:
        tile = min(tile, piece)
        split = piece // tile
        shape = (quarters, R, piece)
    else:
        shape = (quarters, R // quarters, count)
        if (R // quarters) % 8:
            rows = jnp.arange(R, dtype=jnp.int32)
            bits = jnp.take(bits, rows ^ (who[1] * (R // quarters)), axis=0)
        else:
            order = quarters
    whole = pl.BlockSpec(memory_space=pltpu.VMEM)
    buffers = min(BUFFERS, count // tile)
    return pl.pallas_call(
        functools.partial(project_kernel, scale, order, first, split),
        in_specs=[pl.BlockSpec(memory_space=pltpu.SMEM)] + [pl.BlockSpec(memory_space=pl.ANY)] * (2 + len(after)),
        out_specs=[whole, whole],
        scratch_shapes=[
            pltpu.VMEM((R, width), jnp.int32),
            pltpu.VMEM((R, width), jnp.bfloat16),
            pltpu.VMEM((buffers, tile, width), jnp.bfloat16),
            pltpu.SemaphoreType.DMA,
            pltpu.SemaphoreType.DMA((buffers,)),
        ],
        out_shape=[jax.ShapeDtypeStruct(shape, jnp.bfloat16), jax.ShapeDtypeStruct(shape, jnp.float32)],
        compiler_params=pltpu.CompilerParams(vmem_limit_bytes=VMEM),
        cost_estimate=pl.CostEstimate(flops=4 * count * width * R, bytes_accessed=4 * count * width, transcendentals=0),
        name="project",
    )(who, x, bits, *after)


def fetch_all(sources, targets, sems):
    copies = [pltpu.make_async_copy(source, target, sems.at[k]) for k, (source, target) in enumerate(zip(sources, targets))]
    for copy in copies:
        copy.start()
    return copies


def merge_kernel(chunks, *refs):
    sources, outs = refs[:2 * chunks], refs[2 * chunks:-2 * chunks - 1]
    targets, sems = refs[-2 * chunks - 1:-1], refs[-1]
    copies = fetch_all(sources, targets, sems)
    at = 0
    for c in range(chunks):
        kept_ref, got_ref = targets[2 * c], targets[2 * c + 1]
        copies[2 * c].wait()
        copies[2 * c + 1].wait()
        width = kept_ref.shape[2]
        for d, out_ref in enumerate(outs):
            out_ref[:, at:at + width] = (kept_ref[d] + got_ref[d].astype(jnp.float32)).astype(out_ref.dtype)
        at = at + width


def merge(arrays):
    quarters, rows = arrays[0].shape[:2]
    tokens = sum(array.shape[2] for array in arrays[::2])
    whole = pl.BlockSpec(memory_space=pltpu.VMEM)
    return pl.pallas_call(
        functools.partial(merge_kernel, len(arrays) // 2),
        in_specs=[pl.BlockSpec(memory_space=pl.ANY)] * len(arrays),
        out_specs=[whole] * quarters,
        out_shape=[jax.ShapeDtypeStruct((rows, tokens), jnp.bfloat16 if d else jnp.float32) for d in range(quarters)],
        scratch_shapes=[pltpu.VMEM(array.shape, array.dtype) for array in arrays] + [pltpu.SemaphoreType.DMA((len(arrays),))],
        compiler_params=pltpu.CompilerParams(vmem_limit_bytes=VMEM // 6),
        cost_estimate=pl.CostEstimate(flops=quarters * rows * tokens, bytes_accessed=8 * quarters * rows * tokens, transcendentals=0),
        name="merge",
    )(*arrays)


def score_kernel(quarters, width, who_ref, *refs):
    count = 2 * quarters + 5
    sources, out_ref, targets = refs[:count], refs[count], refs[count + 1:2 * count + 1]
    sems, row_ref, col_ref, member_ref, spread_ref, sketch_ref = refs[2 * count + 1:]
    copies = fetch_all(sources, targets, sems)
    left_refs, right_refs = targets[:quarters], targets[quarters:2 * quarters]
    ids_ref, query_refs = targets[2 * quarters], targets[2 * quarters + 1:]
    half, quarter, data = who_ref[0], who_ref[1], who_ref[2]
    for copy in copies[:2 * quarters + 1]:
        copy.wait()
    total = left_refs[0][...]
    for left_ref in left_refs[1:]:
        total = total + left_ref[...].astype(jnp.float32)
    row_ref[...] = total
    piece = right_refs[0].shape[1]
    for d, right_ref in enumerate(right_refs):
        col_ref[:, pl.ds(pl.multiple_of((quarter ^ d) * piece, piece), piece)] = right_ref[...].astype(jnp.float32)
    numbers = lax.broadcasted_iota(jnp.int32, (SEQ_DEV, 1), 0)
    member_ref[...] = (ids_ref[...] == numbers).astype(jnp.bfloat16)
    rows = spread_ref.shape[0] // R
    for first in range(0, row_ref.shape[0], rows):
        for at in range(0, col_ref.shape[1], width):
            right = col_ref[:, at:at + width]
            for r in range(rows):
                spread_ref[r * R:(r + 1) * R, at:at + width] = (row_ref[first + r:first + r + 1, at:at + width] * right).astype(jnp.bfloat16)
        sketch_ref[:, first * R:(first + rows) * R] = lax.dot_general(
            member_ref[...], spread_ref[...], LAST, preferred_element_type=jnp.float32
        )
    entries = sketch_ref[...]
    high = entries.astype(jnp.bfloat16)
    low = (entries - high.astype(jnp.float32)).astype(jnp.bfloat16)
    both = jnp.concatenate([high, low], axis=0)
    middle = both.shape[1] // 2
    swapped = half == 1
    near = jnp.where(swapped, both[:, middle:], both[:, :middle])
    far = jnp.where(swapped, both[:, :middle], both[:, middle:])
    for copy in copies[2 * quarters + 1:]:
        copy.wait()
    rows = query_refs[0].shape[0]
    for side in range(2):
        part = lax.dot_general(near, query_refs[2 * side][...], LAST, preferred_element_type=jnp.float32)
        part = part + lax.dot_general(far, query_refs[2 * side + 1][...], LAST, preferred_element_type=jnp.float32)
        out_ref[:, pl.ds(pl.multiple_of((data ^ side) * rows, rows), rows)] = part[:SEQ_DEV] + part[SEQ_DEV:]


def score(who, left, right, ids, queries):
    operands = left + right + [ids] + queries
    columns, tokens = left[0].shape
    rows = min(4, columns)
    shape = (SEQ_DEV, 2 * queries[0].shape[0])
    return pl.pallas_call(
        functools.partial(score_kernel, len(left), min(512, tokens)),
        in_specs=[pl.BlockSpec(memory_space=pltpu.SMEM)] + [pl.BlockSpec(memory_space=pl.ANY)] * len(operands),
        out_specs=pl.BlockSpec(memory_space=pltpu.VMEM),
        out_shape=jax.ShapeDtypeStruct(shape, jnp.float32),
        scratch_shapes=[pltpu.VMEM(operand.shape, operand.dtype) for operand in operands]
        + [
            pltpu.SemaphoreType.DMA((len(operands),)),
            pltpu.VMEM((columns, tokens), jnp.float32),
            pltpu.VMEM((R, tokens), jnp.float32),
            pltpu.VMEM((SEQ_DEV, tokens), jnp.bfloat16),
            pltpu.VMEM((rows * R, tokens), jnp.bfloat16),
            pltpu.VMEM((SEQ_DEV, columns * R), jnp.float32),
        ],
        compiler_params=pltpu.CompilerParams(vmem_limit_bytes=VMEM // 3),
        cost_estimate=pl.CostEstimate(flops=2 * tokens * columns * R * SEQ_DEV, bytes_accessed=4 * columns * tokens, transcendentals=0),
        name="score",
    )(who, *operands)


def body(n_tensor, activations, out_grads, proj_in, proj_out, segment_ids, queries):
    quarters = n_tensor // 2
    me = lax.axis_index("tensor").astype(jnp.int32)
    half = me % 2
    who = jnp.stack([half, me // 2, lax.axis_index("dp").astype(jnp.int32)])
    owned = activations.shape[0] // 2
    early = owned * 5 // 8

    def swap(array, distance):
        return lax.ppermute(array, "tensor", [(k, k ^ distance) for k in range(n_tensor)])

    def cross(array):
        return lax.ppermute(array, "dp", [(0, 1), (1, 0)])

    far = swap(queries, 1)
    every = [queries, far, cross(queries), cross(far)]

    bits_in, bits_out = proj_in.T, proj_out.T
    scale_in, scale_out = FF ** -0.5, D ** -0.5
    sent_g, kept_g = project(out_grads, bits_out, who, scale_out, quarters, False, 0, owned, 1024)
    got_g = swap(sent_g, 1)
    sent_0, kept_0 = project(activations, bits_in, who, scale_in, quarters, True, 0, early, 512)
    got_0 = swap(sent_0, 1)
    pair_g = [kept_g[d] + got_g[d].astype(jnp.float32) for d in range(quarters)]
    pair_g = [pair_g[0]] + [pair.astype(jnp.bfloat16) for pair in pair_g[1:]]
    moved_g = [swap(pair_g[d], 2 * d) for d in range(1, quarters)]
    sent_1, kept_1 = project(activations, bits_in, who, scale_in, quarters, True, early, owned - early, 512, [pair_g[1], far])
    got_1 = swap(sent_1, 1)
    own_g = sum([moved.astype(jnp.float32) for moved in moved_g], pair_g[0]).astype(jnp.bfloat16)
    right = [own_g] + [swap(own_g, 2 * d) for d in range(1, quarters)]
    pair_a = merge([kept_0, got_0, kept_1, got_1])
    left = [pair_a[0]] + [swap(pair_a[d], 2 * d) for d in range(1, quarters)]

    ids = lax.dynamic_slice(segment_ids, (0, half * owned), (1, owned))
    total = score(who, left, right, ids, every)
    distance = 1
    while 2 * distance < n_tensor:
        total = total + swap(total, distance)
        distance = 2 * distance
    rounded = total.astype(jnp.bfloat16)
    return rounded.astype(jnp.float32) + swap(rounded, distance).astype(jnp.float32)


def solution(mesh):
    return jax.shard_map(
        functools.partial(body, mesh.shape["tensor"]),
        mesh=mesh,
        in_specs=(
            P(("copies", "dp"), "tensor"),
            P(("copies", "dp"), "tensor"),
            P("tensor", None),
            P("tensor", None),
            P(("copies", "dp"), None),
            P(("copies", "dp"), "tensor"),
        ),
        out_specs=P(("copies", "dp"), None),
        check_vma=False,
    )
```

```python
import functools
import math

import jax
import jax.numpy as jnp
from jax import lax
from jax.experimental import pallas as pl
from jax.experimental.pallas import tpu as pltpu
from jax.sharding import PartitionSpec as P

D = 8192
FF = 28672
R = 64
SEQ_DEV = 64
BUFFERS = 4
VMEM = 48 * 1024 * 1024
LAST = (((1,), (1,)), ((), ()))


def project_kernel(scale, first, split, order, direct, makes, waits, who_ref, x_hbm, sign_source, *refs):
    outs = 1 if direct else 2
    other_source, refs = refs[0], refs[makes + waits:]
    out_refs, refs = refs[:outs], refs[outs:]
    made_ref, refs = refs[0], refs[makes:]
    bits_ref, other_ref = refs[0], refs[1]
    signs_ref, x_buf, sign_sem, sems = refs[-4:]
    half, quarter = who_ref[0], who_ref[1]
    buffers, tile = x_buf.shape[0], x_buf.shape[1]
    subs = sems.shape[1]
    sub = tile // subs
    steps = out_refs[0].size // (R * tile) // (2 if direct else 1)

    def copies(p):
        mine = (p >= steps).astype(jnp.int32) if isinstance(p, jax.Array) else int(p >= steps)
        side = mine if direct else half ^ 1 ^ mine
        slot = lax.rem(p, buffers)
        row = pl.multiple_of(side * (x_hbm.shape[0] // 2) + first + (p - mine * steps) * tile, sub)
        return [
            pltpu.make_async_copy(x_hbm.at[pl.ds(row + h * sub, sub)], x_buf.at[slot, pl.ds(h * sub, sub)], sems.at[slot, h])
            for h in range(subs)
        ]

    sign_copy = pltpu.make_async_copy(sign_source, bits_ref, sign_sem.at[0])
    if makes:
        other_copy = pltpu.make_async_copy(other_source, other_ref, sign_sem.at[1])
    sign_copy.start()
    for p in range(min(buffers, 2 * steps)):
        for copy in copies(p):
            copy.start()
    if makes:
        other_copy.start()
    sign_copy.wait()
    if makes:
        signs_ref[...] = (2 * bits_ref[...] - 1).astype(jnp.bfloat16)
    else:
        rows = R // max(order, 1)
        for q in range(max(order, 1)):
            at = pl.multiple_of((q ^ quarter) * rows, rows) if order else 0
            signs_ref[q * rows:(q + 1) * rows, :] = bits_ref[pl.ds(at, rows), :]

    def product(p, mine, at, size):
        s = p - mine * steps
        slot = lax.rem(p, buffers)
        part = lax.dot_general(
            signs_ref[...], x_buf[slot, at:at + size, :], LAST, preferred_element_type=jnp.float32
        ) * scale
        out_ref = out_refs[0] if direct else out_refs[mine]
        part = part.astype(out_ref.dtype)
        if split:
            here = pl.ds(pl.multiple_of(lax.rem(s, split) * tile + at, size), size)
            out_ref[s // split, mine, :, here] = part
        else:
            here = pl.ds(pl.multiple_of(s * tile + at, size), size)
            if direct:
                out_ref[:, mine, :, here] = part.reshape(out_ref.shape[0], out_ref.shape[2], size)
            else:
                out_ref[:, :, here] = part.reshape(out_ref.shape[0], out_ref.shape[1], size)

    def one(p, mine):
        for copy in copies(p):
            copy.wait()
        product(p, mine, 0, tile)

        @pl.when(p + buffers < 2 * steps)
        def _():
            for copy in copies(p + buffers):
                copy.start()

    def halves(p, mine):
        for h, copy in enumerate(copies(p)):
            copy.wait()
            product(p, mine, h * sub, sub)
        if p + buffers < 2 * steps:
            for copy in copies(p + buffers):
                copy.start()

    def run(low, high, mine):
        def loop(p, carry):
            one(p, mine)
            return carry

        lax.fori_loop(low, high, loop, 0)

    halves(0, 0)
    run(1, steps, 0)
    run(steps, 2 * steps - 1, 1)
    halves(2 * steps - 1, 1)
    if makes:
        other_copy.wait()
        made_ref[...] = (2 * other_ref[...] - 1).astype(jnp.bfloat16)


def project(x, signs, who, scale, quarters, by_column, direct, first, count, tile, other=None, after=()):
    width = x.shape[1]
    piece = count // quarters
    order, split = 0, 0
    makes = other is not None
    if by_column:
        shape = (quarters, R // quarters, count)
        if not direct and (R // quarters) % 16:
            rows = jnp.arange(R, dtype=jnp.int32)
            signs = jnp.take(signs, rows ^ (who[1] * (R // quarters)), axis=0)
        elif not direct:
            order = quarters
    else:
        tile = min(tile, piece)
        split = piece // tile
        shape = (quarters, R, piece)
    if direct:
        shapes = [jax.ShapeDtypeStruct((quarters, 2) + shape[1:], jnp.bfloat16)]
    else:
        shapes = [jax.ShapeDtypeStruct(shape, jnp.bfloat16), jax.ShapeDtypeStruct(shape, jnp.float32)]
    scratch = [pltpu.VMEM(signs.shape, signs.dtype)]
    if makes:
        shapes.append(jax.ShapeDtypeStruct(other.shape, jnp.bfloat16))
        scratch.append(pltpu.VMEM(other.shape, other.dtype))
    hbm = pl.BlockSpec(memory_space=pltpu.HBM)
    buffers = min(BUFFERS, 2 * (count // tile))
    subs = 2 if tile % 256 == 0 else 1
    operands = [x, signs] + ([other] if makes else []) + list(after)
    specs = [hbm, hbm if makes else pl.BlockSpec(memory_space=pl.ANY)] + ([hbm] if makes else [])
    return pl.pallas_call(
        functools.partial(project_kernel, scale, first, split, order, direct, int(makes), len(after)),
        in_specs=[pl.BlockSpec(memory_space=pltpu.SMEM)] + specs + [pl.BlockSpec(memory_space=pl.ANY)] * len(after),
        out_specs=[pl.BlockSpec(memory_space=pltpu.VMEM)] * len(shapes),
        scratch_shapes=scratch
        + [
            pltpu.VMEM(signs.shape, jnp.bfloat16),
            pltpu.VMEM((buffers, tile, width), jnp.bfloat16),
            pltpu.SemaphoreType.DMA((2,)),
            pltpu.SemaphoreType.DMA((buffers, subs)),
        ],
        out_shape=shapes,
        compiler_params=pltpu.CompilerParams(vmem_limit_bytes=VMEM),
        cost_estimate=pl.CostEstimate(flops=4 * count * width * R, bytes_accessed=4 * count * width, transcendentals=0),
        name="project",
    )(who, *operands)


def fetch_all(sources, targets, sems):
    copies = [pltpu.make_async_copy(source, target, sems.at[k]) for k, (source, target) in enumerate(zip(sources, targets))]
    for copy in copies:
        copy.start()
    return copies


def merge_kernel(chunks, *refs):
    sources, outs = refs[:2 * chunks], refs[2 * chunks:-2 * chunks - 1]
    targets, sems = refs[-2 * chunks - 1:-1], refs[-1]
    copies = fetch_all(sources, targets, sems)
    at = 0
    for c in range(chunks):
        kept_ref, got_ref = targets[2 * c], targets[2 * c + 1]
        copies[2 * c].wait()
        copies[2 * c + 1].wait()
        width = kept_ref.shape[2]
        for d, out_ref in enumerate(outs):
            out_ref[:, at:at + width] = (kept_ref[d] + got_ref[d].astype(jnp.float32)).astype(out_ref.dtype)
        at = at + width


def merge(arrays):
    quarters, rows = arrays[0].shape[:2]
    tokens = sum(array.shape[2] for array in arrays[::2])
    whole = pl.BlockSpec(memory_space=pltpu.VMEM)
    return pl.pallas_call(
        functools.partial(merge_kernel, len(arrays) // 2),
        in_specs=[pl.BlockSpec(memory_space=pl.ANY)] * len(arrays),
        out_specs=[whole] * quarters,
        out_shape=[jax.ShapeDtypeStruct((rows, tokens), jnp.bfloat16 if d else jnp.float32) for d in range(quarters)],
        scratch_shapes=[pltpu.VMEM(array.shape, array.dtype) for array in arrays] + [pltpu.SemaphoreType.DMA((len(arrays),))],
        compiler_params=pltpu.CompilerParams(vmem_limit_bytes=VMEM // 6),
        cost_estimate=pl.CostEstimate(flops=quarters * rows * tokens, bytes_accessed=8 * quarters * rows * tokens, transcendentals=0),
        name="merge",
    )(*arrays)


def add_sources(refs, stacked):
    parts = [refs[0][k] for k in range(refs[0].shape[0])] if stacked else [ref[...] for ref in refs]
    return sum([part.astype(jnp.float32) for part in parts[1:]], parts[0].astype(jnp.float32))


def sketch_rows(half, quarter, first, left_refs, right_refs, ids_ref, base_ref, stores, scratch):
    row_ref, col_ref, member_ref, spread_ref = scratch
    owned = ids_ref.shape[1] // 2
    tokens = row_ref.shape[1]
    width = math.gcd(tokens, 512)
    row_ref[...] = add_sources(left_refs, len(left_refs) == 1)
    piece = right_refs[0].shape[1]
    for d, right_ref in enumerate(right_refs):
        col_ref[:, pl.ds(pl.multiple_of((quarter ^ d) * piece, piece), piece)] = right_ref[...].astype(jnp.float32)
    numbers = lax.broadcasted_iota(jnp.int32, (SEQ_DEV, 1), 0)
    ids = ids_ref[:, pl.ds(pl.multiple_of(half * owned + first, 128), tokens)]
    member_ref[...] = (ids == numbers).astype(jnp.bfloat16)
    rows = spread_ref.shape[0] // R
    for top in range(0, row_ref.shape[0], rows):
        for at in range(0, tokens, width):
            right = col_ref[:, first + at:first + at + width]
            for r in range(rows):
                spread_ref[r * R:(r + 1) * R, at:at + width] = (row_ref[top + r:top + r + 1, at:at + width] * right).astype(jnp.bfloat16)
        part = lax.dot_general(member_ref[...], spread_ref[...], LAST, preferred_element_type=jnp.float32)
        here = slice(top * R, (top + rows) * R)
        stores[:, here] = part if base_ref is None else base_ref[:, here] + part


def sketch_kernel(quarters, lefts, first, who_ref, *refs):
    count = lefts + quarters + 1
    sources, out_ref, targets = refs[:count], refs[count], refs[count + 1:2 * count + 1]
    copies = fetch_all(sources, targets, refs[2 * count + 1])
    for copy in copies:
        copy.wait()
    sketch_rows(who_ref[0], who_ref[1], first, targets[:lefts], targets[lefts:-1], targets[-1], None, out_ref, refs[2 * count + 2:])


def score_kernel(quarters, lefts, first, who_ref, *refs):
    count = lefts + quarters + 6
    sources, out_ref, targets = refs[:count], refs[count], refs[count + 1:2 * count + 1]
    sketch_ref, scratch = refs[2 * count + 2], refs[2 * count + 3:]
    copies = fetch_all(sources, targets, refs[2 * count + 1])
    half, quarter, data = who_ref[0], who_ref[1], who_ref[2]
    for copy in copies[:-4]:
        copy.wait()
    sketch_rows(half, quarter, first, targets[:lefts], targets[lefts:-6], targets[-6], targets[-5], sketch_ref, scratch)
    entries = sketch_ref[...]
    high = entries.astype(jnp.bfloat16)
    low = (entries - high.astype(jnp.float32)).astype(jnp.bfloat16)
    both = jnp.concatenate([high, low], axis=0)
    middle = both.shape[1] // 2
    swapped = half == 1
    near = jnp.where(swapped, both[:, middle:], both[:, :middle])
    far = jnp.where(swapped, both[:, :middle], both[:, middle:])
    for copy in copies[-4:]:
        copy.wait()
    query_refs = targets[-4:]
    rows = query_refs[0].shape[0]
    for side in range(2):
        part = lax.dot_general(near, query_refs[2 * side][...], LAST, preferred_element_type=jnp.float32)
        part = part + lax.dot_general(far, query_refs[2 * side + 1][...], LAST, preferred_element_type=jnp.float32)
        out_ref[:, pl.ds(pl.multiple_of((data ^ side) * rows, rows), rows)] = part[:SEQ_DEV] + part[SEQ_DEV:]


def call_sketch(kernel, first, who, left, right, rest, shape, extra):
    operands = left + right + rest
    columns, tokens = left[0].shape[-2:]
    rows = min(4, columns)
    return pl.pallas_call(
        functools.partial(kernel, len(right), len(left), first),
        in_specs=[pl.BlockSpec(memory_space=pltpu.SMEM)] + [pl.BlockSpec(memory_space=pl.ANY)] * len(operands),
        out_specs=pl.BlockSpec(memory_space=pltpu.VMEM),
        out_shape=jax.ShapeDtypeStruct(shape, jnp.float32),
        scratch_shapes=[pltpu.VMEM(operand.shape, operand.dtype) for operand in operands]
        + [pltpu.SemaphoreType.DMA((len(operands),))]
        + extra
        + [
            pltpu.VMEM((columns, tokens), jnp.float32),
            pltpu.VMEM((R, rest[0].shape[1] // 2), jnp.float32),
            pltpu.VMEM((SEQ_DEV, tokens), jnp.bfloat16),
            pltpu.VMEM((rows * R, tokens), jnp.bfloat16),
        ],
        compiler_params=pltpu.CompilerParams(vmem_limit_bytes=VMEM // 3),
        cost_estimate=pl.CostEstimate(flops=2 * tokens * columns * R * SEQ_DEV, bytes_accessed=4 * columns * tokens, transcendentals=0),
        name="sketch" if not extra else "score",
    )(who, *operands)


def body(n_tensor, activations, out_grads, proj_in, proj_out, segment_ids, queries):
    quarters = n_tensor // 2
    me = lax.axis_index("tensor").astype(jnp.int32)
    half = me % 2
    who = jnp.stack([half, me // 2, lax.axis_index("dp").astype(jnp.int32)])
    owned = activations.shape[0] // 2
    early = owned * 3 // 4

    def swap(array, distance):
        return lax.ppermute(array, "tensor", [(k, k ^ distance) for k in range(n_tensor)])

    def cross(array):
        return lax.ppermute(array, "dp", [(0, 1), (1, 0)])

    far = swap(queries, 1)
    every = [queries, far, cross(queries), cross(far)]

    bits_in, bits_out = proj_in.T, proj_out.T
    scale_in, scale_out = FF ** -0.5, D ** -0.5
    part_g, signs_in = project(out_grads, bits_out, who, scale_out, quarters, False, True, 0, owned, 1024, bits_in)
    moved_g = lax.all_to_all(part_g.reshape((n_tensor,) + part_g.shape[2:]), "tensor", 0, 0)
    sent_0, kept_0 = project(activations, signs_in, who, scale_in, quarters, True, False, 0, early, 512)
    got_0 = swap(sent_0, 1)
    own_g = sum([moved_g[k].astype(jnp.float32) for k in range(1, n_tensor)], moved_g[0].astype(jnp.float32)).astype(jnp.bfloat16)
    right = [own_g] + [swap(own_g, 2 * d) for d in range(1, quarters)]
    late = owned - early
    part_1 = project(activations, signs_in, who, scale_in, quarters, True, True, early, late, 512, None, [own_g, far])[0]
    pair_0 = merge([kept_0, got_0])
    left_0 = [pair_0[0]] + [swap(pair_0[d], 2 * d) for d in range(1, quarters)]
    left_1 = [lax.all_to_all(part_1.reshape((n_tensor,) + part_1.shape[2:]), "tensor", 0, 0)]

    entries = R // quarters * R
    base = call_sketch(sketch_kernel, 0, who, left_0, right, [segment_ids], (SEQ_DEV, entries), [])
    rest = [segment_ids, base] + every
    shape = (SEQ_DEV, 2 * queries.shape[0])
    total = call_sketch(score_kernel, early, who, left_1, right, rest, shape, [pltpu.VMEM((SEQ_DEV, entries), jnp.float32)])
    distance = 1
    while 2 * distance < n_tensor:
        total = total + swap(total, distance)
        distance = 2 * distance
    rounded = total.astype(jnp.bfloat16)
    return rounded.astype(jnp.float32) + swap(rounded, distance).astype(jnp.float32)


def solution(mesh):
    return jax.shard_map(
        functools.partial(body, mesh.shape["tensor"]),
        mesh=mesh,
        in_specs=(
            P(("copies", "dp"), "tensor"),
            P(("copies", "dp"), "tensor"),
            P("tensor", None),
            P("tensor", None),
            P(("copies", "dp"), None),
            P(("copies", "dp"), "tensor"),
        ),
        out_specs=P(("copies", "dp"), None),
        check_vma=False,
    )
```

```python
import functools

import jax
import jax.numpy as jnp
from jax import lax
from jax.experimental import pallas as pl
from jax.experimental.pallas import tpu as pltpu
from jax.sharding import PartitionSpec as P

D = 8192
FF = 28672
R = 64
SEQ_DEV = 64
BUFFERS = 4
VMEM = 48 * 1024 * 1024
LAST = (((1,), (1,)), ((), ()))


def project_kernel(scale, first, split, order, makes, waits, who_ref, x_hbm, sign_source, *refs):
    other_source, refs = refs[0], refs[makes + waits:]
    sent_ref, kept_ref, made_ref, refs = refs[0], refs[1], refs[2], refs[2 + makes:]
    bits_ref, other_ref = refs[0], refs[1]
    signs_ref, x_buf, sign_sem, sems = refs[-4:]
    half, quarter = who_ref[0], who_ref[1]
    buffers, tile = x_buf.shape[0], x_buf.shape[1]
    steps = sent_ref.size // (R * tile)

    def copy(p):
        mine = (p >= steps).astype(jnp.int32)
        row = pl.multiple_of((half ^ 1 ^ mine) * (x_hbm.shape[0] // 2) + first + (p - mine * steps) * tile, tile)
        slot = lax.rem(p, buffers)
        return pltpu.make_async_copy(x_hbm.at[pl.ds(row, tile)], x_buf.at[slot], sems.at[slot])

    sign_copy = pltpu.make_async_copy(sign_source, bits_ref, sign_sem.at[0])
    sign_copy.start()

    def begin(p, carry):
        copy(p).start()
        return carry

    lax.fori_loop(0, buffers, begin, 0)
    if makes:
        other_copy = pltpu.make_async_copy(other_source, other_ref, sign_sem.at[1])
        other_copy.start()
    sign_copy.wait()
    if makes:
        signs_ref[...] = (2 * bits_ref[...] - 1).astype(jnp.bfloat16)
    else:
        rows = R // max(order, 1)
        for q in range(max(order, 1)):
            at = pl.multiple_of((q ^ quarter) * rows, rows) if order else 0
            signs_ref[q * rows:(q + 1) * rows, :] = bits_ref[pl.ds(at, rows), :]

    def one(p, carry):
        copy(p).wait()
        mine = (p >= steps).astype(jnp.int32)
        s = p - mine * steps
        part = lax.dot_general(
            signs_ref[...], x_buf[lax.rem(p, buffers)], LAST, preferred_element_type=jnp.float32
        ) * scale

        def store(out_ref):
            value = part.astype(out_ref.dtype)
            if split:
                here = pl.ds(pl.multiple_of(lax.rem(s, split) * tile, tile), tile)
                out_ref[(s // split) ^ quarter, :, here] = value
            else:
                here = pl.ds(pl.multiple_of(s * tile, tile), tile)
                out_ref[:, :, here] = value.reshape(out_ref.shape[0], out_ref.shape[1], tile)

        @pl.when(p < steps)
        def _():
            store(sent_ref)

        @pl.when(p >= steps)
        def _():
            store(kept_ref)

        @pl.when(p + buffers < 2 * steps)
        def _():
            copy(p + buffers).start()

        return carry

    lax.fori_loop(0, 2 * steps, one, 0)
    if makes:
        other_copy.wait()
        made_ref[...] = (2 * other_ref[...] - 1).astype(jnp.bfloat16)


def project(x, signs, who, scale, quarters, by_column, first, count, tile, other=None, after=()):
    width = x.shape[1]
    piece = count // quarters
    order, split = 0, 0
    makes = other is not None
    if by_column:
        shape = (quarters, R // quarters, count)
        if (R // quarters) % 16:
            rows = jnp.arange(R, dtype=jnp.int32)
            signs = jnp.take(signs, rows ^ (who[1] * (R // quarters)), axis=0)
        else:
            order = quarters
    else:
        tile = min(tile, piece)
        split = piece // tile
        shape = (quarters, R, piece)
    shapes = [jax.ShapeDtypeStruct(shape, jnp.bfloat16), jax.ShapeDtypeStruct(shape, jnp.float32)]
    scratch = [pltpu.VMEM(signs.shape, signs.dtype)]
    if makes:
        shapes.append(jax.ShapeDtypeStruct(other.shape, jnp.bfloat16))
        scratch.append(pltpu.VMEM(other.shape, other.dtype))
    buffers = min(BUFFERS, 2 * (count // tile))
    operands = [x, signs] + ([other] if makes else []) + list(after)
    return pl.pallas_call(
        functools.partial(project_kernel, scale, first, split, order, int(makes), len(after)),
        in_specs=[pl.BlockSpec(memory_space=pltpu.SMEM)] + [pl.BlockSpec(memory_space=pl.ANY)] * len(operands),
        out_specs=[pl.BlockSpec(memory_space=pltpu.VMEM)] * len(shapes),
        scratch_shapes=scratch
        + [
            pltpu.VMEM(signs.shape, jnp.bfloat16),
            pltpu.VMEM((buffers, tile, width), jnp.bfloat16),
            pltpu.SemaphoreType.DMA((2,)),
            pltpu.SemaphoreType.DMA((buffers,)),
        ],
        out_shape=shapes,
        compiler_params=pltpu.CompilerParams(vmem_limit_bytes=VMEM),
        cost_estimate=pl.CostEstimate(flops=4 * count * width * R, bytes_accessed=4 * count * width, transcendentals=0),
        name="project",
    )(who, *operands)


def fetch_all(sources, targets, sems):
    copies = [pltpu.make_async_copy(source, target, sems.at[k]) for k, (source, target) in enumerate(zip(sources, targets))]
    for copy in copies:
        copy.start()
    return copies


def merge_kernel(quarters, bases, pairs, waits, *refs):
    count = bases + 2 * pairs
    sources, outs = refs[:count], refs[count + waits:count + waits + quarters]
    targets, sems = refs[count + waits + quarters:-1], refs[-1]
    copies = fetch_all(sources, targets, sems)
    for copy in copies:
        copy.wait()
    for d, out_ref in enumerate(outs):
        at = 0
        if bases:
            at = targets[d].shape[1]
            out_ref[:, :at] = targets[d][...]
        for c in range(bases, count, 2):
            kept_ref, got_ref = targets[c], targets[c + 1]
            width = kept_ref.shape[2]
            out_ref[:, at:at + width] = (kept_ref[d] + got_ref[d].astype(jnp.float32)).astype(out_ref.dtype)
            at = at + width


def merge(base, arrays, after):
    quarters, rows = arrays[0].shape[:2]
    tokens = sum(array.shape[2] for array in arrays[::2]) + (base[0].shape[1] if base else 0)
    operands = list(base) + list(arrays)
    return pl.pallas_call(
        functools.partial(merge_kernel, quarters, len(base), len(arrays) // 2, len(after)),
        in_specs=[pl.BlockSpec(memory_space=pl.ANY)] * (len(operands) + len(after)),
        out_specs=[pl.BlockSpec(memory_space=pltpu.VMEM)] * quarters,
        out_shape=[jax.ShapeDtypeStruct((rows, tokens), jnp.bfloat16 if d else jnp.float32) for d in range(quarters)],
        scratch_shapes=[pltpu.VMEM(operand.shape, operand.dtype) for operand in operands] + [pltpu.SemaphoreType.DMA((len(operands),))],
        compiler_params=pltpu.CompilerParams(vmem_limit_bytes=VMEM // 6),
        cost_estimate=pl.CostEstimate(flops=quarters * rows * tokens, bytes_accessed=8 * quarters * rows * tokens, transcendentals=0),
        name="merge",
    )(*operands, *after)


def total_kernel(count, waits, *refs):
    sources, out_ref, targets, sems = refs[:count], refs[count + waits], refs[count + waits + 1:-1], refs[-1]
    for copy in fetch_all(sources, targets, sems):
        copy.wait()
    total = targets[0][...]
    for target in targets[1:]:
        total = total + target[...].astype(jnp.float32)
    out_ref[...] = total.astype(out_ref.dtype)


def total_of(parts, after):
    return pl.pallas_call(
        functools.partial(total_kernel, len(parts), len(after)),
        in_specs=[pl.BlockSpec(memory_space=pl.ANY)] * (len(parts) + len(after)),
        out_specs=pl.BlockSpec(memory_space=pltpu.VMEM),
        out_shape=jax.ShapeDtypeStruct(parts[0].shape, jnp.bfloat16),
        scratch_shapes=[pltpu.VMEM(part.shape, part.dtype) for part in parts] + [pltpu.SemaphoreType.DMA((len(parts),))],
        compiler_params=pltpu.CompilerParams(vmem_limit_bytes=VMEM // 6),
        cost_estimate=pl.CostEstimate(flops=parts[0].size * len(parts), bytes_accessed=2 * parts[0].size * len(parts), transcendentals=0),
        name="total",
    )(*parts, *after)


def score_kernel(quarters, width, who_ref, *refs):
    count = 2 * quarters + 5
    sources, out_ref, targets = refs[:count], refs[count], refs[count + 1:2 * count + 1]
    sems, row_ref, col_ref, member_ref, spread_ref, sketch_ref = refs[2 * count + 1:]
    copies = fetch_all(sources, targets, sems)
    left_refs, right_refs = targets[:quarters], targets[quarters:2 * quarters]
    ids_ref, query_refs = targets[2 * quarters], targets[2 * quarters + 1:]
    half, quarter, data = who_ref[0], who_ref[1], who_ref[2]
    for copy in copies[:2 * quarters + 1]:
        copy.wait()
    total = left_refs[0][...]
    for left_ref in left_refs[1:]:
        total = total + left_ref[...].astype(jnp.float32)
    row_ref[...] = total
    piece = right_refs[0].shape[1]
    for d, right_ref in enumerate(right_refs):
        col_ref[:, pl.ds(pl.multiple_of((quarter ^ d) * piece, piece), piece)] = right_ref[...].astype(jnp.float32)
    numbers = lax.broadcasted_iota(jnp.int32, (SEQ_DEV, 1), 0)
    owned = col_ref.shape[1]
    ids = ids_ref[:, pl.ds(pl.multiple_of(half * owned, 128), owned)]
    member_ref[...] = (ids == numbers).astype(jnp.bfloat16)
    rows = spread_ref.shape[0] // R

    def group(g, carry):
        for at in range(0, owned, width):
            right = col_ref[:, at:at + width]
            for r in range(rows):
                row = row_ref[pl.ds(g * rows + r, 1), at:at + width]
                spread_ref[r * R:(r + 1) * R, at:at + width] = (row * right).astype(jnp.bfloat16)
        here = pl.ds(pl.multiple_of(g * rows * R, rows * R), rows * R)
        sketch_ref[:, here] = lax.dot_general(member_ref[...], spread_ref[...], LAST, preferred_element_type=jnp.float32)
        return carry

    lax.fori_loop(0, row_ref.shape[0] // rows, group, 0)
    entries = sketch_ref[...]
    high = entries.astype(jnp.bfloat16)
    low = (entries - high.astype(jnp.float32)).astype(jnp.bfloat16)
    both = jnp.concatenate([high, low], axis=0)
    middle = both.shape[1] // 2
    swapped = half == 1
    near = jnp.where(swapped, both[:, middle:], both[:, :middle])
    far = jnp.where(swapped, both[:, :middle], both[:, middle:])
    for copy in copies[2 * quarters + 1:]:
        copy.wait()
    rows = query_refs[0].shape[0]
    for side in range(2):
        part = lax.dot_general(near, query_refs[2 * side][...], LAST, preferred_element_type=jnp.float32)
        part = part + lax.dot_general(far, query_refs[2 * side + 1][...], LAST, preferred_element_type=jnp.float32)
        out_ref[:, pl.ds(pl.multiple_of((data ^ side) * rows, rows), rows)] = part[:SEQ_DEV] + part[SEQ_DEV:]


def score(who, left, right, ids, queries):
    operands = left + right + [ids] + queries
    columns, tokens = left[0].shape
    rows = min(4, columns)
    shape = (SEQ_DEV, 2 * queries[0].shape[0])
    return pl.pallas_call(
        functools.partial(score_kernel, len(left), min(512, tokens)),
        in_specs=[pl.BlockSpec(memory_space=pltpu.SMEM)] + [pl.BlockSpec(memory_space=pl.ANY)] * len(operands),
        out_specs=pl.BlockSpec(memory_space=pltpu.VMEM),
        out_shape=jax.ShapeDtypeStruct(shape, jnp.float32),
        scratch_shapes=[pltpu.VMEM(operand.shape, operand.dtype) for operand in operands]
        + [
            pltpu.SemaphoreType.DMA((len(operands),)),
            pltpu.VMEM((columns, tokens), jnp.float32),
            pltpu.VMEM((R, tokens), jnp.float32),
            pltpu.VMEM((SEQ_DEV, tokens), jnp.bfloat16),
            pltpu.VMEM((rows * R, tokens), jnp.bfloat16),
            pltpu.VMEM((SEQ_DEV, columns * R), jnp.float32),
        ],
        compiler_params=pltpu.CompilerParams(vmem_limit_bytes=VMEM // 3),
        cost_estimate=pl.CostEstimate(flops=2 * tokens * columns * R * SEQ_DEV, bytes_accessed=4 * columns * tokens, transcendentals=0),
        name="score",
    )(who, *operands)


def body(n_tensor, activations, out_grads, proj_in, proj_out, segment_ids, queries):
    quarters = n_tensor // 2
    me = lax.axis_index("tensor").astype(jnp.int32)
    half = me % 2
    who = jnp.stack([half, me // 2, lax.axis_index("dp").astype(jnp.int32)])
    owned = activations.shape[0] // 2
    def swap(array, distance):
        return lax.ppermute(array, "tensor", [(k, k ^ distance) for k in range(n_tensor)])

    def cross(array):
        return lax.ppermute(array, "dp", [(0, 1), (1, 0)])

    far = swap(queries, 1)
    every = [queries, far, cross(queries), cross(far)]

    scale_in, scale_out = FF ** -0.5, D ** -0.5
    sent_g, kept_g, signs = project(out_grads, proj_out.T, who, scale_out, quarters, False, 0, owned, 1024, proj_in.T)
    got_g = swap(sent_g, 1)

    def chunk(eighth, eighths, after):
        first, count = owned * eighth // 8, owned * eighths // 8
        sent, kept = project(activations, signs, who, scale_in, quarters, True, first, count, 512, None, after)
        return sent, [kept, swap(sent, 1)]

    sent_0, chunk_0 = chunk(0, 4, [])
    pair_g = merge([], [kept_g, got_g], [sent_0])
    moved_g = [swap(pair_g[d], 2 * d) for d in range(1, quarters)]
    sent_1, chunk_1 = chunk(4, 3, [pair_g[1]])
    own_g = total_of([pair_g[0]] + moved_g, [sent_1])
    right = [own_g] + [swap(own_g, 2 * d) for d in range(1, quarters)]
    sent_2, chunk_2 = chunk(7, 1, [own_g, far])
    pair_a = merge([], chunk_0, right[1:])
    pair_a = merge(pair_a, chunk_1 + chunk_2, [])
    left = [pair_a[0]] + [swap(pair_a[d], 2 * d) for d in range(1, quarters)]

    total = score(who, left, right, segment_ids, every)
    total = (total + swap(total, 1)).astype(jnp.bfloat16)
    parts = [total] + [swap(total, 2 * d) for d in range(1, quarters)]
    parts = [part.astype(jnp.float32) for part in parts]
    while len(parts) > 1:
        parts = [parts[k] + parts[k + 1] for k in range(0, len(parts), 2)]
    return parts[0]


def solution(mesh):
    return jax.shard_map(
        functools.partial(body, mesh.shape["tensor"]),
        mesh=mesh,
        in_specs=(
            P(("copies", "dp"), "tensor"),
            P(("copies", "dp"), "tensor"),
            P("tensor", None),
            P("tensor", None),
            P(("copies", "dp"), None),
            P(("copies", "dp"), "tensor"),
        ),
        out_specs=P(("copies", "dp"), None),
        check_vma=False,
    )
```

```python
import functools
import math

import jax
import jax.numpy as jnp
from jax import lax
from jax.experimental import pallas as pl
from jax.experimental.pallas import tpu as pltpu
from jax.sharding import PartitionSpec as P

D = 8192
FF = 28672
R = 64
SEQ_DEV = 64
BUFFERS = 4
VMEM = 48 * 1024 * 1024
LAST = (((1,), (1,)), ((), ()))


def project_kernel(scale, first, split, order, makes, waits, who_ref, x_hbm, sign_source, *refs):
    other_source, refs = refs[0], refs[makes + waits:]
    sent_ref, kept_ref, made_ref, refs = refs[0], refs[1], refs[2], refs[2 + makes:]
    bits_ref, other_ref = refs[0], refs[1]
    signs_ref, x_buf, sign_sem, sems = refs[-4:]
    half, quarter = who_ref[0], who_ref[1]
    buffers, tile = x_buf.shape[0], x_buf.shape[1]
    steps = sent_ref.size // (R * tile)

    def copy(p):
        mine = (p >= steps).astype(jnp.int32)
        row = pl.multiple_of((half ^ 1 ^ mine) * (x_hbm.shape[0] // 2) + first + (p - mine * steps) * tile, tile)
        slot = lax.rem(p, buffers)
        return pltpu.make_async_copy(x_hbm.at[pl.ds(row, tile)], x_buf.at[slot], sems.at[slot])

    sign_copy = pltpu.make_async_copy(sign_source, bits_ref, sign_sem.at[0])
    sign_copy.start()

    def begin(p, carry):
        copy(p).start()
        return carry

    lax.fori_loop(0, buffers, begin, 0)
    if makes:
        other_copy = pltpu.make_async_copy(other_source, other_ref, sign_sem.at[1])
        other_copy.start()
    sign_copy.wait()
    if makes:
        signs_ref[...] = (2 * bits_ref[...] - 1).astype(jnp.bfloat16)
    else:
        rows = R // max(order, 1)
        for q in range(max(order, 1)):
            at = pl.multiple_of((q ^ quarter) * rows, rows) if order else 0
            signs_ref[q * rows:(q + 1) * rows, :] = bits_ref[pl.ds(at, rows), :]

    def one(p, carry):
        copy(p).wait()
        mine = (p >= steps).astype(jnp.int32)
        s = p - mine * steps
        part = lax.dot_general(
            signs_ref[...], x_buf[lax.rem(p, buffers)], LAST, preferred_element_type=jnp.float32
        ) * scale

        def store(out_ref):
            value = part.astype(out_ref.dtype)
            if split:
                here = pl.ds(pl.multiple_of(lax.rem(s, split) * tile, tile), tile)
                out_ref[(s // split) ^ quarter, :, here] = value
            else:
                here = pl.ds(pl.multiple_of(s * tile, tile), tile)
                out_ref[:, :, here] = value.reshape(out_ref.shape[0], out_ref.shape[1], tile)

        @pl.when(p < steps)
        def _():
            store(sent_ref)

        @pl.when(p >= steps)
        def _():
            store(kept_ref)

        @pl.when(p + buffers < 2 * steps)
        def _():
            copy(p + buffers).start()

        return carry

    lax.fori_loop(0, 2 * steps, one, 0)
    if makes:
        other_copy.wait()
        made_ref[...] = (2 * other_ref[...] - 1).astype(jnp.bfloat16)


def project(x, signs, who, scale, quarters, by_column, first, count, tile, other=None, after=()):
    width = x.shape[1]
    piece = count // quarters
    order, split = 0, 0
    makes = other is not None
    if by_column:
        shape = (quarters, R // quarters, count)
        if (R // quarters) % 16:
            rows = jnp.arange(R, dtype=jnp.int32)
            signs = jnp.take(signs, rows ^ (who[1] * (R // quarters)), axis=0)
        else:
            order = quarters
    else:
        tile = min(tile, piece)
        split = piece // tile
        shape = (quarters, R, piece)
    shapes = [jax.ShapeDtypeStruct(shape, jnp.bfloat16), jax.ShapeDtypeStruct(shape, jnp.float32)]
    scratch = [pltpu.VMEM(signs.shape, signs.dtype)]
    if makes:
        shapes.append(jax.ShapeDtypeStruct(other.shape, jnp.bfloat16))
        scratch.append(pltpu.VMEM(other.shape, other.dtype))
    buffers = min(BUFFERS, 2 * (count // tile))
    operands = [x, signs] + ([other] if makes else []) + list(after)
    return pl.pallas_call(
        functools.partial(project_kernel, scale, first, split, order, int(makes), len(after)),
        in_specs=[pl.BlockSpec(memory_space=pltpu.SMEM)] + [pl.BlockSpec(memory_space=pl.ANY)] * len(operands),
        out_specs=[pl.BlockSpec(memory_space=pltpu.VMEM)] * len(shapes),
        scratch_shapes=scratch
        + [
            pltpu.VMEM(signs.shape, jnp.bfloat16),
            pltpu.VMEM((buffers, tile, width), jnp.bfloat16),
            pltpu.SemaphoreType.DMA((2,)),
            pltpu.SemaphoreType.DMA((buffers,)),
        ],
        out_shape=shapes,
        compiler_params=pltpu.CompilerParams(vmem_limit_bytes=VMEM),
        cost_estimate=pl.CostEstimate(flops=4 * count * width * R, bytes_accessed=4 * count * width, transcendentals=0),
        name="project",
    )(who, *operands)


def fetch_all(sources, targets, sems):
    copies = [pltpu.make_async_copy(source, target, sems.at[k]) for k, (source, target) in enumerate(zip(sources, targets))]
    for copy in copies:
        copy.start()
    return copies


def merge_kernel(quarters, bases, pairs, waits, *refs):
    count = bases + 2 * pairs
    sources, outs = refs[:count], refs[count + waits:count + waits + quarters]
    targets, sems = refs[count + waits + quarters:-1], refs[-1]
    copies = fetch_all(sources, targets, sems)
    for copy in copies:
        copy.wait()
    for d, out_ref in enumerate(outs):
        at = 0
        if bases:
            at = targets[d].shape[1]
            out_ref[:, :at] = targets[d][...]
        for c in range(bases, count, 2):
            kept_ref, got_ref = targets[c], targets[c + 1]
            width = kept_ref.shape[2]
            out_ref[:, at:at + width] = (kept_ref[d] + got_ref[d].astype(jnp.float32)).astype(out_ref.dtype)
            at = at + width


def merge(base, arrays, after):
    quarters, rows = arrays[0].shape[:2]
    tokens = sum(array.shape[2] for array in arrays[::2]) + (base[0].shape[1] if base else 0)
    operands = list(base) + list(arrays)
    return pl.pallas_call(
        functools.partial(merge_kernel, quarters, len(base), len(arrays) // 2, len(after)),
        in_specs=[pl.BlockSpec(memory_space=pl.ANY)] * (len(operands) + len(after)),
        out_specs=[pl.BlockSpec(memory_space=pltpu.VMEM)] * quarters,
        out_shape=[jax.ShapeDtypeStruct((rows, tokens), jnp.bfloat16 if d else jnp.float32) for d in range(quarters)],
        scratch_shapes=[pltpu.VMEM(operand.shape, operand.dtype) for operand in operands] + [pltpu.SemaphoreType.DMA((len(operands),))],
        compiler_params=pltpu.CompilerParams(vmem_limit_bytes=VMEM // 6),
        cost_estimate=pl.CostEstimate(flops=quarters * rows * tokens, bytes_accessed=8 * quarters * rows * tokens, transcendentals=0),
        name="merge",
    )(*operands, *after)


def total_kernel(count, waits, *refs):
    sources, out_ref, targets, sems = refs[:count], refs[count + waits], refs[count + waits + 1:-1], refs[-1]
    for copy in fetch_all(sources, targets, sems):
        copy.wait()
    total = targets[0][...]
    for target in targets[1:]:
        total = total + target[...].astype(jnp.float32)
    out_ref[...] = total.astype(out_ref.dtype)


def total_of(parts, after):
    return pl.pallas_call(
        functools.partial(total_kernel, len(parts), len(after)),
        in_specs=[pl.BlockSpec(memory_space=pl.ANY)] * (len(parts) + len(after)),
        out_specs=pl.BlockSpec(memory_space=pltpu.VMEM),
        out_shape=jax.ShapeDtypeStruct(parts[0].shape, jnp.bfloat16),
        scratch_shapes=[pltpu.VMEM(part.shape, part.dtype) for part in parts] + [pltpu.SemaphoreType.DMA((len(parts),))],
        compiler_params=pltpu.CompilerParams(vmem_limit_bytes=VMEM // 6),
        cost_estimate=pl.CostEstimate(flops=parts[0].size * len(parts), bytes_accessed=2 * parts[0].size * len(parts), transcendentals=0),
        name="total",
    )(*parts, *after)


def pack_kernel(quarters, waits, *refs):
    count = quarters + 2
    sources, refs = refs[:count], refs[count + waits:]
    own_g_ref, own_a_ref, outs, refs = refs[0], refs[1], refs[2:quarters + 1], refs[quarters + 1:]
    targets, sems = refs[:-1], refs[-1]
    for copy in fetch_all(sources, targets, sems):
        copy.wait()
    total = targets[0][...]
    for target in targets[1:quarters]:
        total = total + target[...].astype(jnp.float32)
    own = total.astype(jnp.bfloat16)
    own_g_ref[...] = own
    kept_ref, got_ref = targets[quarters], targets[quarters + 1]
    own_a_ref[...] = kept_ref[0] + got_ref[0].astype(jnp.float32)
    rows, at = kept_ref.shape[1], own.shape[1]
    width = kept_ref.shape[2] * rows // R
    for d, out_ref in enumerate(outs, 1):
        out_ref[:, :at] = own
        for f in range(R // rows):
            here = slice(f * width, (f + 1) * width)
            out_ref[f * rows:(f + 1) * rows, at:] = (kept_ref[d, :, here] + got_ref[d, :, here].astype(jnp.float32)).astype(jnp.bfloat16)


def pack(parts, kept, got, after):
    quarters, rows, tokens = kept.shape
    operands = list(parts) + [kept, got]
    packed = jax.ShapeDtypeStruct((R, parts[0].shape[1] + tokens * rows // R), jnp.bfloat16)
    shapes = [jax.ShapeDtypeStruct(parts[0].shape, jnp.bfloat16), jax.ShapeDtypeStruct((rows, tokens), jnp.float32)]
    shapes = shapes + [packed] * (quarters - 1)
    return pl.pallas_call(
        functools.partial(pack_kernel, quarters, len(after)),
        in_specs=[pl.BlockSpec(memory_space=pl.ANY)] * (len(operands) + len(after)),
        out_specs=[pl.BlockSpec(memory_space=pltpu.VMEM)] * len(shapes),
        out_shape=shapes,
        scratch_shapes=[pltpu.VMEM(operand.shape, operand.dtype) for operand in operands] + [pltpu.SemaphoreType.DMA((len(operands),))],
        compiler_params=pltpu.CompilerParams(vmem_limit_bytes=VMEM // 6),
        cost_estimate=pl.CostEstimate(flops=4 * kept.size, bytes_accessed=8 * kept.size, transcendentals=0),
        name="pack",
    )(*operands, *after)


def touch_kernel(*refs):
    refs[-1][...] = jnp.zeros(refs[-1].shape, refs[-1].dtype)


def touch(after):
    return pl.pallas_call(
        touch_kernel,
        in_specs=[pl.BlockSpec(memory_space=pl.ANY)] * len(after),
        out_specs=pl.BlockSpec(memory_space=pltpu.VMEM),
        out_shape=jax.ShapeDtypeStruct((8, 128), jnp.float32),
        compiler_params=pltpu.CompilerParams(vmem_limit_bytes=VMEM // 6),
        name="touch",
    )(*after)


def sketch_rows(half, first, row_ref, col_ref, ids_ref, member_ref, spread_refs, sink):
    columns, tokens = row_ref.shape
    owned = ids_ref.shape[1] // 2
    width = math.gcd(tokens, 512)
    numbers = lax.broadcasted_iota(jnp.int32, (SEQ_DEV, 1), 0)
    ids = ids_ref[:, pl.ds(pl.multiple_of(half * owned + first, 128), tokens)]
    member_ref[...] = (ids == numbers).astype(jnp.bfloat16)
    rows = spread_refs[0].shape[0] // R
    for g in range(columns // rows):
        spread_ref = spread_refs[g % 2]
        for at in range(0, tokens, width):
            right = col_ref[:, first + at:first + at + width].astype(jnp.float32)
            for r in range(rows):
                row = row_ref[g * rows + r:g * rows + r + 1, at:at + width]
                spread_ref[r * R:(r + 1) * R, at:at + width] = (row * right).astype(jnp.bfloat16)
        part = lax.dot_general(member_ref[...], spread_ref[...], LAST, preferred_element_type=jnp.float32)
        sink(slice(g * rows * R, (g + 1) * rows * R), part)


def sketch_kernel(quarters, packed, who_ref, *refs):
    count = quarters + 2 if packed else 2 * quarters + 1
    sources, base_ref, col_ref, targets = refs[:count], refs[count], refs[count + 1], refs[count + 2:2 * count + 2]
    sems, row_ref, member_ref, spread_0, spread_1 = refs[2 * count + 2:]
    half, quarter = who_ref[0], who_ref[1]
    for copy in fetch_all(sources, targets, sems):
        copy.wait()
    ids_ref, own_ref, right_refs = targets[0], targets[1], targets[2:2 + quarters]
    piece = right_refs[0].shape[1]
    for d, right_ref in enumerate(right_refs):
        here = pl.ds(pl.multiple_of((quarter ^ d) * piece, piece), piece)
        col_ref[:, here] = right_ref[:, :piece]
    if packed:
        rows, tokens = row_ref.shape
        width = tokens * rows // R
        for f in range(R // rows):
            here = slice(f * width, (f + 1) * width)
            total = own_ref[:, here]
            for right_ref in right_refs[1:]:
                total = total + right_ref[f * rows:(f + 1) * rows, piece:].astype(jnp.float32)
            row_ref[:, here] = total
    else:
        row_ref[...] = sum([ref[...].astype(jnp.float32) for ref in targets[2 + quarters:]], own_ref[...])

    def sink(here, part):
        base_ref[:, here] = part

    sketch_rows(half, 0, row_ref, col_ref, ids_ref, member_ref, (spread_0, spread_1), sink)


def score_kernel(lefts, first, who_ref, *refs):
    count = lefts + 7
    sources, out_ref, targets = refs[:count], refs[count], refs[count + 1:2 * count + 1]
    sems, sketch_ref, row_ref, member_ref, spread_0, spread_1 = refs[2 * count + 1:]
    copies = fetch_all(sources, targets, sems)
    half, data = who_ref[0], who_ref[2]
    ids_ref, col_ref, base_ref, left_refs, query_refs = targets[0], targets[1], targets[2], targets[3:-4], targets[-4:]
    for copy in copies[:-4]:
        copy.wait()
    row_ref[...] = sum([ref[...].astype(jnp.float32) for ref in left_refs[1:]], left_refs[0][...])

    def sink(here, part):
        sketch_ref[:, here] = base_ref[:, here] + part

    sketch_rows(half, first, row_ref, col_ref, ids_ref, member_ref, (spread_0, spread_1), sink)
    entries = sketch_ref[...]
    high = entries.astype(jnp.bfloat16)
    low = (entries - high.astype(jnp.float32)).astype(jnp.bfloat16)
    both = jnp.concatenate([high, low], axis=0)
    middle = both.shape[1] // 2
    swapped = half == 1
    near = jnp.where(swapped, both[:, middle:], both[:, :middle])
    far = jnp.where(swapped, both[:, :middle], both[:, middle:])
    for copy in copies[-4:]:
        copy.wait()
    rows = query_refs[0].shape[0]
    for side in range(2):
        part = lax.dot_general(near, query_refs[2 * side][...], LAST, preferred_element_type=jnp.float32)
        part = part + lax.dot_general(far, query_refs[2 * side + 1][...], LAST, preferred_element_type=jnp.float32)
        out_ref[:, pl.ds(pl.multiple_of((data ^ side) * rows, rows), rows)] = part[:SEQ_DEV] + part[SEQ_DEV:]


def call_sketch(kernel, who, operands, columns, tokens, shapes, extra, name):
    rows = min(4, columns)
    return pl.pallas_call(
        kernel,
        in_specs=[pl.BlockSpec(memory_space=pltpu.SMEM)] + [pl.BlockSpec(memory_space=pl.ANY)] * len(operands),
        out_specs=[pl.BlockSpec(memory_space=pltpu.VMEM)] * len(shapes),
        out_shape=shapes,
        scratch_shapes=[pltpu.VMEM(operand.shape, operand.dtype) for operand in operands]
        + [pltpu.SemaphoreType.DMA((len(operands),))]
        + extra
        + [
            pltpu.VMEM((columns, tokens), jnp.float32),
            pltpu.VMEM((SEQ_DEV, tokens), jnp.bfloat16),
            pltpu.VMEM((rows * R, tokens), jnp.bfloat16),
            pltpu.VMEM((rows * R, tokens), jnp.bfloat16),
        ],
        compiler_params=pltpu.CompilerParams(vmem_limit_bytes=VMEM // 3),
        cost_estimate=pl.CostEstimate(flops=2 * tokens * columns * R * SEQ_DEV, bytes_accessed=4 * columns * tokens, transcendentals=0),
        name=name,
    )(who, *operands)


def body(n_tensor, activations, out_grads, proj_in, proj_out, segment_ids, queries):
    quarters = n_tensor // 2
    me = lax.axis_index("tensor").astype(jnp.int32)
    half = me % 2
    who = jnp.stack([half, me // 2, lax.axis_index("dp").astype(jnp.int32)])
    owned = activations.shape[0] // 2
    def swap(array, distance):
        return lax.ppermute(array, "tensor", [(k, k ^ distance) for k in range(n_tensor)])

    def cross(array):
        return lax.ppermute(array, "dp", [(0, 1), (1, 0)])

    far = swap(queries, 1)
    every = [queries, far, cross(queries), cross(far)]

    scale_in, scale_out = FF ** -0.5, D ** -0.5
    sent_g, kept_g, signs = project(out_grads, proj_out.T, who, scale_out, quarters, False, 0, owned, 1024, proj_in.T)
    got_g = swap(sent_g, 1)

    def chunk(eighth, eighths, after):
        first, count = owned * eighth // 8, owned * eighths // 8
        sent, kept = project(activations, signs, who, scale_in, quarters, True, first, count, 512, None, after)
        return sent, [kept, swap(sent, 1)]

    sent_0, chunk_0 = chunk(0, 4, [])
    pair_g = merge([], [kept_g, got_g], [sent_0])
    moved_g = [swap(pair_g[d], 2 * d) for d in range(1, quarters)]
    sent_1, chunk_1 = chunk(4, 3, [pair_g[1]])
    columns = R // quarters
    packed = columns % 16 == 0
    if packed:
        sums = pack([pair_g[0]] + moved_g, chunk_0[0], chunk_0[1], [sent_1])
        own_g, own_a = sums[:2]
        right = [own_g] + [swap(sums[d + 1], 2 * d) for d in range(1, quarters)]
        first = [segment_ids, own_a] + right
    else:
        own_g = total_of([pair_g[0]] + moved_g, [sent_1])
        right = [own_g] + [swap(own_g, 2 * d) for d in range(1, quarters)]
        pair_0 = merge([], chunk_0, [])
        first = [segment_ids, pair_0[0]] + right + [swap(pair_0[d], 2 * d) for d in range(1, quarters)]
    sent_2, chunk_2 = chunk(7, 1, [own_g, far])
    pair_1 = merge([], chunk_1 + chunk_2, [touch(right[1:])])
    left = [pair_1[0]] + [swap(pair_1[d], 2 * d) for d in range(1, quarters)]

    early, entries = owned // 2, columns * R
    shapes = [jax.ShapeDtypeStruct((SEQ_DEV, entries), jnp.float32), jax.ShapeDtypeStruct((R, owned), jnp.bfloat16)]
    base, col = call_sketch(functools.partial(sketch_kernel, quarters, packed), who, first, columns, early, shapes, [], "sketch")
    shapes = [jax.ShapeDtypeStruct((SEQ_DEV, 2 * queries.shape[0]), jnp.float32)]
    extra = [pltpu.VMEM((SEQ_DEV, entries), jnp.float32)]
    rest = [segment_ids, col, base] + left + every
    total = call_sketch(functools.partial(score_kernel, quarters, early), who, rest, columns, owned - early, shapes, extra, "score")[0]
    total = (total + swap(total, 1)).astype(jnp.bfloat16)
    parts = [total] + [swap(total, 2 * d) for d in range(1, quarters)]
    parts = [part.astype(jnp.float32) for part in parts]
    while len(parts) > 1:
        parts = [parts[k] + parts[k + 1] for k in range(0, len(parts), 2)]
    return parts[0]


def solution(mesh):
    return jax.shard_map(
        functools.partial(body, mesh.shape["tensor"]),
        mesh=mesh,
        in_specs=(
            P(("copies", "dp"), "tensor"),
            P(("copies", "dp"), "tensor"),
            P("tensor", None),
            P("tensor", None),
            P(("copies", "dp"), None),
            P(("copies", "dp"), "tensor"),
        ),
        out_specs=P(("copies", "dp"), None),
        check_vma=False,
    )
```

```python
import functools
import math

import jax
import jax.numpy as jnp
from jax import lax
from jax.experimental import pallas as pl
from jax.experimental.pallas import tpu as pltpu
from jax.sharding import PartitionSpec as P

D = 8192
FF = 28672
R = 64
SEQ_DEV = 64
BUFFERS = 4
VMEM = 48 * 1024 * 1024
LAST = (((1,), (1,)), ((), ()))


def project_kernel(scale, first, split, order, makes, waits, who_ref, x_hbm, sign_source, *refs):
    other_source, refs = refs[0], refs[makes + waits:]
    sent_ref, kept_ref, made_ref, refs = refs[0], refs[1], refs[2], refs[2 + makes:]
    bits_ref, other_ref = refs[0], refs[1]
    signs_ref, x_buf, sign_sem, sems = refs[-4:]
    half, quarter = who_ref[0], who_ref[1]
    buffers, tile = x_buf.shape[0], x_buf.shape[1]
    steps = sent_ref.size // (R * tile)

    def copy(p):
        mine = (p >= steps).astype(jnp.int32)
        row = pl.multiple_of((half ^ 1 ^ mine) * (x_hbm.shape[0] // 2) + first + (p - mine * steps) * tile, tile)
        slot = lax.rem(p, buffers)
        return pltpu.make_async_copy(x_hbm.at[pl.ds(row, tile)], x_buf.at[slot], sems.at[slot])

    sign_copy = pltpu.make_async_copy(sign_source, bits_ref, sign_sem.at[0])
    sign_copy.start()

    def begin(p, carry):
        copy(p).start()
        return carry

    lax.fori_loop(0, buffers, begin, 0)
    if makes:
        other_copy = pltpu.make_async_copy(other_source, other_ref, sign_sem.at[1])
        other_copy.start()
    sign_copy.wait()
    if makes:
        signs_ref[...] = (2 * bits_ref[...] - 1).astype(jnp.bfloat16)
    else:
        rows = R // max(order, 1)
        for q in range(max(order, 1)):
            at = pl.multiple_of((q ^ quarter) * rows, rows) if order else 0
            signs_ref[q * rows:(q + 1) * rows, :] = bits_ref[pl.ds(at, rows), :]

    def one(p, carry):
        copy(p).wait()
        mine = (p >= steps).astype(jnp.int32)
        s = p - mine * steps
        part = lax.dot_general(
            signs_ref[...], x_buf[lax.rem(p, buffers)], LAST, preferred_element_type=jnp.float32
        ) * scale

        def store(out_ref):
            value = part.astype(out_ref.dtype)
            if split:
                here = pl.ds(pl.multiple_of(lax.rem(s, split) * tile, tile), tile)
                out_ref[(s // split) ^ quarter, :, here] = value
            else:
                here = pl.ds(pl.multiple_of(s * tile, tile), tile)
                out_ref[:, :, here] = value.reshape(out_ref.shape[0], out_ref.shape[1], tile)

        @pl.when(p < steps)
        def _():
            store(sent_ref)

        @pl.when(p >= steps)
        def _():
            store(kept_ref)

        @pl.when(p + buffers < 2 * steps)
        def _():
            copy(p + buffers).start()

        return carry

    lax.fori_loop(0, 2 * steps, one, 0)
    if makes:
        other_copy.wait()
        made_ref[...] = (2 * other_ref[...] - 1).astype(jnp.bfloat16)


def project(x, signs, who, scale, quarters, by_column, first, count, tile, other=None, after=()):
    width = x.shape[1]
    piece = count // quarters
    order, split = 0, 0
    makes = other is not None
    if by_column:
        shape = (quarters, R // quarters, count)
        if (R // quarters) % 16:
            rows = jnp.arange(R, dtype=jnp.int32)
            signs = jnp.take(signs, rows ^ (who[1] * (R // quarters)), axis=0)
        else:
            order = quarters
    else:
        tile = min(tile, piece)
        split = piece // tile
        shape = (quarters, R, piece)
    shapes = [jax.ShapeDtypeStruct(shape, jnp.bfloat16), jax.ShapeDtypeStruct(shape, jnp.float32)]
    scratch = [pltpu.VMEM(signs.shape, signs.dtype)]
    if makes:
        shapes.append(jax.ShapeDtypeStruct(other.shape, jnp.bfloat16))
        scratch.append(pltpu.VMEM(other.shape, other.dtype))
    buffers = min(BUFFERS, 2 * (count // tile))
    operands = [x, signs] + ([other] if makes else []) + list(after)
    return pl.pallas_call(
        functools.partial(project_kernel, scale, first, split, order, int(makes), len(after)),
        in_specs=[pl.BlockSpec(memory_space=pltpu.SMEM)] + [pl.BlockSpec(memory_space=pl.ANY)] * len(operands),
        out_specs=[pl.BlockSpec(memory_space=pltpu.VMEM)] * len(shapes),
        scratch_shapes=scratch
        + [
            pltpu.VMEM(signs.shape, jnp.bfloat16),
            pltpu.VMEM((buffers, tile, width), jnp.bfloat16),
            pltpu.SemaphoreType.DMA((2,)),
            pltpu.SemaphoreType.DMA((buffers,)),
        ],
        out_shape=shapes,
        compiler_params=pltpu.CompilerParams(vmem_limit_bytes=VMEM),
        cost_estimate=pl.CostEstimate(flops=4 * count * width * R, bytes_accessed=4 * count * width, transcendentals=0),
        name="project",
    )(who, *operands)


def fetch_all(sources, targets, sems):
    copies = [pltpu.make_async_copy(source, target, sems.at[k]) for k, (source, target) in enumerate(zip(sources, targets))]
    for copy in copies:
        copy.start()
    return copies


def merge_kernel(quarters, bases, pairs, carried, waits, *refs):
    count = bases + 2 * pairs
    sources, refs = refs[:count + carried], refs[count + carried + waits:]
    outs, carries, refs = refs[:quarters], refs[quarters:quarters + carried], refs[quarters + carried:]
    targets, sems = refs[:-1], refs[-1]
    copies = fetch_all(sources, targets, sems)
    for copy in copies:
        copy.wait()
    for k, carry_ref in enumerate(carries):
        carry_ref[...] = targets[count + k][...]
    for d, out_ref in enumerate(outs):
        at = 0
        if bases:
            at = targets[d].shape[1]
            out_ref[:, :at] = targets[d][...]
        for c in range(bases, count, 2):
            kept_ref, got_ref = targets[c], targets[c + 1]
            width = kept_ref.shape[2]
            out_ref[:, at:at + width] = (kept_ref[d] + got_ref[d].astype(jnp.float32)).astype(out_ref.dtype)
            at = at + width


def merge(base, arrays, after, carry=()):
    quarters, rows = arrays[0].shape[:2]
    tokens = sum(array.shape[2] for array in arrays[::2]) + (base[0].shape[1] if base else 0)
    operands = list(base) + list(arrays) + list(carry)
    return pl.pallas_call(
        functools.partial(merge_kernel, quarters, len(base), len(arrays) // 2, len(carry), len(after)),
        in_specs=[pl.BlockSpec(memory_space=pl.ANY)] * (len(operands) + len(after)),
        out_specs=[pl.BlockSpec(memory_space=pltpu.VMEM)] * (quarters + len(carry)),
        out_shape=[jax.ShapeDtypeStruct((rows, tokens), jnp.bfloat16 if d else jnp.float32) for d in range(quarters)]
        + [jax.ShapeDtypeStruct(array.shape, array.dtype) for array in carry],
        scratch_shapes=[pltpu.VMEM(operand.shape, operand.dtype) for operand in operands] + [pltpu.SemaphoreType.DMA((len(operands),))],
        compiler_params=pltpu.CompilerParams(vmem_limit_bytes=VMEM // 6),
        cost_estimate=pl.CostEstimate(flops=quarters * rows * tokens, bytes_accessed=8 * quarters * rows * tokens, transcendentals=0),
        name="merge",
    )(*operands, *after)


def total_kernel(count, waits, *refs):
    sources, out_ref, targets, sems = refs[:count], refs[count + waits], refs[count + waits + 1:-1], refs[-1]
    for copy in fetch_all(sources, targets, sems):
        copy.wait()
    total = targets[0][...]
    for target in targets[1:]:
        total = total + target[...].astype(jnp.float32)
    out_ref[...] = total.astype(out_ref.dtype)


def total_of(parts, after):
    return pl.pallas_call(
        functools.partial(total_kernel, len(parts), len(after)),
        in_specs=[pl.BlockSpec(memory_space=pl.ANY)] * (len(parts) + len(after)),
        out_specs=pl.BlockSpec(memory_space=pltpu.VMEM),
        out_shape=jax.ShapeDtypeStruct(parts[0].shape, jnp.bfloat16),
        scratch_shapes=[pltpu.VMEM(part.shape, part.dtype) for part in parts] + [pltpu.SemaphoreType.DMA((len(parts),))],
        compiler_params=pltpu.CompilerParams(vmem_limit_bytes=VMEM // 6),
        cost_estimate=pl.CostEstimate(flops=parts[0].size * len(parts), bytes_accessed=2 * parts[0].size * len(parts), transcendentals=0),
        name="total",
    )(*parts, *after)


def pack_kernel(quarters, waits, *refs):
    count = quarters + 2
    sources, refs = refs[:count], refs[count + waits:]
    own_g_ref, own_a_ref, outs, refs = refs[0], refs[1], refs[2:quarters + 1], refs[quarters + 1:]
    targets, sems = refs[:-1], refs[-1]
    for copy in fetch_all(sources, targets, sems):
        copy.wait()
    total = targets[0][...]
    for target in targets[1:quarters]:
        total = total + target[...].astype(jnp.float32)
    own = total.astype(jnp.bfloat16)
    own_g_ref[...] = own
    kept_ref, got_ref = targets[quarters], targets[quarters + 1]
    own_a_ref[...] = kept_ref[0] + got_ref[0].astype(jnp.float32)
    rows, at = kept_ref.shape[1], own.shape[1]
    width = kept_ref.shape[2] * rows // R
    for d, out_ref in enumerate(outs, 1):
        out_ref[:, :at] = own
        for f in range(R // rows):
            here = slice(f * width, (f + 1) * width)
            out_ref[f * rows:(f + 1) * rows, at:] = (kept_ref[d, :, here] + got_ref[d, :, here].astype(jnp.float32)).astype(jnp.bfloat16)


def pack(parts, kept, got, after):
    quarters, rows, tokens = kept.shape
    operands = list(parts) + [kept, got]
    packed = jax.ShapeDtypeStruct((R, parts[0].shape[1] + tokens * rows // R), jnp.bfloat16)
    shapes = [jax.ShapeDtypeStruct(parts[0].shape, jnp.bfloat16), jax.ShapeDtypeStruct((rows, tokens), jnp.float32)]
    shapes = shapes + [packed] * (quarters - 1)
    return pl.pallas_call(
        functools.partial(pack_kernel, quarters, len(after)),
        in_specs=[pl.BlockSpec(memory_space=pl.ANY)] * (len(operands) + len(after)),
        out_specs=[pl.BlockSpec(memory_space=pltpu.VMEM)] * len(shapes),
        out_shape=shapes,
        scratch_shapes=[pltpu.VMEM(operand.shape, operand.dtype) for operand in operands] + [pltpu.SemaphoreType.DMA((len(operands),))],
        compiler_params=pltpu.CompilerParams(vmem_limit_bytes=VMEM // 6),
        cost_estimate=pl.CostEstimate(flops=4 * kept.size, bytes_accessed=8 * kept.size, transcendentals=0),
        name="pack",
    )(*operands, *after)


def touch_kernel(*refs):
    refs[-1][...] = jnp.zeros(refs[-1].shape, refs[-1].dtype)


def touch(after):
    return pl.pallas_call(
        touch_kernel,
        in_specs=[pl.BlockSpec(memory_space=pl.ANY)] * len(after),
        out_specs=pl.BlockSpec(memory_space=pltpu.VMEM),
        out_shape=jax.ShapeDtypeStruct((8, 128), jnp.float32),
        compiler_params=pltpu.CompilerParams(vmem_limit_bytes=VMEM // 6),
        name="touch",
    )(*after)


def sketch_rows(half, first, row_ref, col_ref, ids_ref, member_ref, spread_refs, sink):
    columns, tokens = row_ref.shape
    owned = ids_ref.shape[1] // 2
    width = math.gcd(tokens, 512)
    numbers = lax.broadcasted_iota(jnp.int32, (SEQ_DEV, 1), 0)
    ids = ids_ref[:, pl.ds(pl.multiple_of(half * owned + first, 128), tokens)]
    member_ref[...] = (ids == numbers).astype(jnp.bfloat16)
    rows = spread_refs[0].shape[0] // R
    for g in range(columns // rows):
        spread_ref = spread_refs[g % 2]
        for at in range(0, tokens, width):
            right = col_ref[:, first + at:first + at + width].astype(jnp.float32)
            for r in range(rows):
                row = row_ref[g * rows + r:g * rows + r + 1, at:at + width]
                spread_ref[r * R:(r + 1) * R, at:at + width] = (row * right).astype(jnp.bfloat16)
        part = lax.dot_general(member_ref[...], spread_ref[...], LAST, preferred_element_type=jnp.float32)
        sink(slice(g * rows * R, (g + 1) * rows * R), part)


def sketch_kernel(quarters, packed, who_ref, *refs):
    count = quarters + 2 if packed else 2 * quarters + 1
    sources, base_ref, col_ref, targets = refs[:count], refs[count], refs[count + 1], refs[count + 2:2 * count + 2]
    sems, row_ref, member_ref, spread_0, spread_1 = refs[2 * count + 2:]
    half, quarter = who_ref[0], who_ref[1]
    for copy in fetch_all(sources, targets, sems):
        copy.wait()
    ids_ref, own_ref, right_refs = targets[0], targets[1], targets[2:2 + quarters]
    piece = right_refs[0].shape[1]
    for d, right_ref in enumerate(right_refs):
        here = pl.ds(pl.multiple_of((quarter ^ d) * piece, piece), piece)
        col_ref[:, here] = right_ref[:, :piece]
    if packed:
        rows, tokens = row_ref.shape
        width = tokens * rows // R
        for f in range(R // rows):
            here = slice(f * width, (f + 1) * width)
            total = own_ref[:, here]
            for right_ref in right_refs[1:]:
                total = total + right_ref[f * rows:(f + 1) * rows, piece:].astype(jnp.float32)
            row_ref[:, here] = total
    else:
        row_ref[...] = sum([ref[...].astype(jnp.float32) for ref in targets[2 + quarters:]], own_ref[...])

    def sink(here, part):
        base_ref[:, here] = part

    sketch_rows(half, 0, row_ref, col_ref, ids_ref, member_ref, (spread_0, spread_1), sink)


def score_kernel(lefts, first, who_ref, *refs):
    count = lefts + 7
    sources, out_ref, targets = refs[:count], refs[count], refs[count + 1:2 * count + 1]
    sems, sketch_ref, row_ref, member_ref, spread_0, spread_1 = refs[2 * count + 1:]
    copies = fetch_all(sources, targets, sems)
    half, data = who_ref[0], who_ref[2]
    ids_ref, col_ref, base_ref, left_refs, query_refs = targets[0], targets[1], targets[2], targets[3:-4], targets[-4:]
    for copy in copies[:-4]:
        copy.wait()
    row_ref[...] = sum([ref[...].astype(jnp.float32) for ref in left_refs[1:]], left_refs[0][...])

    def sink(here, part):
        sketch_ref[:, here] = base_ref[:, here] + part

    sketch_rows(half, first, row_ref, col_ref, ids_ref, member_ref, (spread_0, spread_1), sink)
    entries = sketch_ref[...]
    high = entries.astype(jnp.bfloat16)
    low = (entries - high.astype(jnp.float32)).astype(jnp.bfloat16)
    both = jnp.concatenate([high, low], axis=0)
    middle = both.shape[1] // 2
    swapped = half == 1
    near = jnp.where(swapped, both[:, middle:], both[:, :middle])
    far = jnp.where(swapped, both[:, :middle], both[:, middle:])
    for copy in copies[-4:]:
        copy.wait()
    rows = query_refs[0].shape[0]
    for side in range(2):
        part = lax.dot_general(near, query_refs[2 * side][...], LAST, preferred_element_type=jnp.float32)
        part = part + lax.dot_general(far, query_refs[2 * side + 1][...], LAST, preferred_element_type=jnp.float32)
        out_ref[:, pl.ds(pl.multiple_of((data ^ side) * rows, rows), rows)] = part[:SEQ_DEV] + part[SEQ_DEV:]


def call_sketch(kernel, who, operands, columns, tokens, shapes, extra, name):
    rows = min(4, columns)
    return pl.pallas_call(
        kernel,
        in_specs=[pl.BlockSpec(memory_space=pltpu.SMEM)] + [pl.BlockSpec(memory_space=pl.ANY)] * len(operands),
        out_specs=[pl.BlockSpec(memory_space=pltpu.VMEM)] * len(shapes),
        out_shape=shapes,
        scratch_shapes=[pltpu.VMEM(operand.shape, operand.dtype) for operand in operands]
        + [pltpu.SemaphoreType.DMA((len(operands),))]
        + extra
        + [
            pltpu.VMEM((columns, tokens), jnp.float32),
            pltpu.VMEM((SEQ_DEV, tokens), jnp.bfloat16),
            pltpu.VMEM((rows * R, tokens), jnp.bfloat16),
            pltpu.VMEM((rows * R, tokens), jnp.bfloat16),
        ],
        compiler_params=pltpu.CompilerParams(vmem_limit_bytes=VMEM // 3),
        cost_estimate=pl.CostEstimate(flops=2 * tokens * columns * R * SEQ_DEV, bytes_accessed=4 * columns * tokens, transcendentals=0),
        name=name,
    )(who, *operands)


def body(n_tensor, activations, out_grads, proj_in, proj_out, segment_ids, queries):
    quarters = n_tensor // 2
    me = lax.axis_index("tensor").astype(jnp.int32)
    half = me % 2
    who = jnp.stack([half, me // 2, lax.axis_index("dp").astype(jnp.int32)])
    owned = activations.shape[0] // 2
    def swap(array, distance):
        return lax.ppermute(array, "tensor", [(k, k ^ distance) for k in range(n_tensor)])

    def cross(array):
        return lax.ppermute(array, "dp", [(0, 1), (1, 0)])

    far = swap(queries, 1)
    cross_near = cross(queries)

    scale_in, scale_out = FF ** -0.5, D ** -0.5
    sent_g, kept_g, signs = project(out_grads, proj_out.T, who, scale_out, quarters, False, 0, owned, 1024, proj_in.T)
    got_g = swap(sent_g, 1)

    def chunk(eighth, eighths, after):
        first, count = owned * eighth // 8, owned * eighths // 8
        sent, kept = project(activations, signs, who, scale_in, quarters, True, first, count, 512, None, after)
        return sent, [kept, swap(sent, 1)]

    sent_0, chunk_0 = chunk(0, 4, [])
    pair_g = merge([], [kept_g, got_g], [sent_0])
    moved_g = [swap(pair_g[d], 2 * d) for d in range(1, quarters)]
    sent_1, chunk_1 = chunk(4, 3, [pair_g[1], far, cross_near])
    columns = R // quarters
    packed = columns % 16 == 0
    if packed:
        sums = pack([pair_g[0]] + moved_g, chunk_0[0], chunk_0[1], [sent_1])
        own_g, own_a = sums[:2]
        right = [own_g] + [swap(sums[d + 1], 2 * d) for d in range(1, quarters)]
        first = [segment_ids, own_a] + right
    else:
        own_g = total_of([pair_g[0]] + moved_g, [sent_1])
        right = [own_g] + [swap(own_g, 2 * d) for d in range(1, quarters)]
        pair_0 = merge([], chunk_0, [])
        first = [segment_ids, pair_0[0]] + right + [swap(pair_0[d], 2 * d) for d in range(1, quarters)]
    sent_2, chunk_2 = chunk(7, 1, [own_g])
    pair_1 = merge([], chunk_1 + chunk_2, [touch(right[1:])], [far])
    every = [queries, far, cross_near, cross(pair_1[quarters])]
    left = [pair_1[0]] + [swap(pair_1[d], 2 * d) for d in range(1, quarters)]

    early, entries = owned // 2, columns * R
    shapes = [jax.ShapeDtypeStruct((SEQ_DEV, entries), jnp.float32), jax.ShapeDtypeStruct((R, owned), jnp.bfloat16)]
    base, col = call_sketch(functools.partial(sketch_kernel, quarters, packed), who, first, columns, early, shapes, [], "sketch")
    shapes = [jax.ShapeDtypeStruct((SEQ_DEV, 2 * queries.shape[0]), jnp.float32)]
    extra = [pltpu.VMEM((SEQ_DEV, entries), jnp.float32)]
    rest = [segment_ids, col, base] + left + every
    total = call_sketch(functools.partial(score_kernel, quarters, early), who, rest, columns, owned - early, shapes, extra, "score")[0]
    total = (total + swap(total, 1)).astype(jnp.bfloat16)
    parts = [total] + [swap(total, 2 * d) for d in range(1, quarters)]
    parts = [part.astype(jnp.float32) for part in parts]
    while len(parts) > 1:
        parts = [parts[k] + parts[k + 1] for k in range(0, len(parts), 2)]
    return parts[0]


def solution(mesh):
    return jax.shard_map(
        functools.partial(body, mesh.shape["tensor"]),
        mesh=mesh,
        in_specs=(
            P(("copies", "dp"), "tensor"),
            P(("copies", "dp"), "tensor"),
            P("tensor", None),
            P("tensor", None),
            P(("copies", "dp"), None),
            P(("copies", "dp"), "tensor"),
        ),
        out_specs=P(("copies", "dp"), None),
        check_vma=False,
    )
```

```python
import functools
import math

import jax
import jax.numpy as jnp
from jax import lax
from jax.experimental import pallas as pl
from jax.experimental.pallas import tpu as pltpu
from jax.sharding import PartitionSpec as P

D = 8192
FF = 28672
R = 64
SEQ_DEV = 64
BUFFERS = 4
VMEM = 48 * 1024 * 1024
FULL = 60600000
LAST = (((1,), (1,)), ((), ()))


def project_kernel(scale, first, split, order, makes, waits, who_ref, x_hbm, sign_source, *refs):
    other_source, refs = refs[0], refs[makes + waits:]
    sent_ref, kept_ref, made_ref, refs = refs[0], refs[1], refs[2], refs[2 + makes:]
    bits_ref, other_ref = refs[0], refs[1]
    signs_ref, x_buf, sign_sem, sems = refs[-4:]
    half, quarter = who_ref[0], who_ref[1]
    buffers, tile = x_buf.shape[0], x_buf.shape[1]
    steps = sent_ref.size // (R * tile)

    def copy(p):
        mine = (p >= steps).astype(jnp.int32)
        row = pl.multiple_of((half ^ 1 ^ mine) * (x_hbm.shape[0] // 2) + first + (p - mine * steps) * tile, tile)
        slot = lax.rem(p, buffers)
        return pltpu.make_async_copy(x_hbm.at[pl.ds(row, tile)], x_buf.at[slot], sems.at[slot])

    sign_copy = pltpu.make_async_copy(sign_source, bits_ref, sign_sem.at[0])
    sign_copy.start()

    def begin(p, carry):
        copy(p).start()
        return carry

    lax.fori_loop(0, buffers, begin, 0)
    if makes:
        other_copy = pltpu.make_async_copy(other_source, other_ref, sign_sem.at[1])
        other_copy.start()
    sign_copy.wait()
    if makes:
        signs_ref[...] = (2 * bits_ref[...] - 1).astype(jnp.bfloat16)
    else:
        rows = R // max(order, 1)
        for q in range(max(order, 1)):
            at = pl.multiple_of((q ^ quarter) * rows, rows) if order else 0
            signs_ref[q * rows:(q + 1) * rows, :] = bits_ref[pl.ds(at, rows), :]

    def one(p, carry):
        copy(p).wait()
        mine = (p >= steps).astype(jnp.int32)
        s = p - mine * steps
        part = lax.dot_general(
            signs_ref[...], x_buf[lax.rem(p, buffers)], LAST, preferred_element_type=jnp.float32
        ) * scale

        def store(out_ref):
            value = part.astype(out_ref.dtype)
            if split:
                here = pl.ds(pl.multiple_of(lax.rem(s, split) * tile, tile), tile)
                out_ref[(s // split) ^ quarter, :, here] = value
            else:
                here = pl.ds(pl.multiple_of(s * tile, tile), tile)
                out_ref[:, :, here] = value.reshape(out_ref.shape[0], out_ref.shape[1], tile)

        @pl.when(p < steps)
        def _():
            store(sent_ref)

        @pl.when(p >= steps)
        def _():
            store(kept_ref)

        @pl.when(p + buffers < 2 * steps)
        def _():
            copy(p + buffers).start()

        return carry

    lax.fori_loop(0, 2 * steps, one, 0)
    if makes:
        other_copy.wait()
        made_ref[...] = (2 * other_ref[...] - 1).astype(jnp.bfloat16)


def project(x, signs, who, scale, quarters, by_column, first, count, tile, other=None, after=()):
    width = x.shape[1]
    piece = count // quarters
    order, split = 0, 0
    makes = other is not None
    if by_column:
        shape = (quarters, R // quarters, count)
        if (R // quarters) % 16:
            rows = jnp.arange(R, dtype=jnp.int32)
            signs = jnp.take(signs, rows ^ (who[1] * (R // quarters)), axis=0)
        else:
            order = quarters
    else:
        tile = min(tile, piece)
        split = piece // tile
        shape = (quarters, R, piece)
    shapes = [jax.ShapeDtypeStruct(shape, jnp.bfloat16), jax.ShapeDtypeStruct(shape, jnp.float32)]
    scratch = [pltpu.VMEM(signs.shape, signs.dtype)]
    if makes:
        shapes.append(jax.ShapeDtypeStruct(other.shape, jnp.bfloat16))
        scratch.append(pltpu.VMEM(other.shape, other.dtype))
    buffers = min(BUFFERS, 2 * (count // tile))
    operands = [x, signs] + ([other] if makes else []) + list(after)
    return pl.pallas_call(
        functools.partial(project_kernel, scale, first, split, order, int(makes), len(after)),
        in_specs=[pl.BlockSpec(memory_space=pltpu.SMEM)] + [pl.BlockSpec(memory_space=pl.ANY)] * len(operands),
        out_specs=[pl.BlockSpec(memory_space=pltpu.VMEM)] * len(shapes),
        scratch_shapes=scratch
        + [
            pltpu.VMEM(signs.shape, jnp.bfloat16),
            pltpu.VMEM((buffers, tile, width), jnp.bfloat16),
            pltpu.SemaphoreType.DMA((2,)),
            pltpu.SemaphoreType.DMA((buffers,)),
        ],
        out_shape=shapes,
        compiler_params=pltpu.CompilerParams(vmem_limit_bytes=FULL if makes else VMEM),
        cost_estimate=pl.CostEstimate(flops=4 * count * width * R, bytes_accessed=4 * count * width, transcendentals=0),
        name="project",
    )(who, *operands)


def fetch_all(sources, targets, sems):
    copies = [pltpu.make_async_copy(source, target, sems.at[k]) for k, (source, target) in enumerate(zip(sources, targets))]
    for copy in copies:
        copy.start()
    return copies


def merge_kernel(quarters, bases, pairs, carried, waits, *refs):
    count = bases + 2 * pairs
    sources, refs = refs[:count + carried], refs[count + carried + waits:]
    outs, carries, refs = refs[:quarters], refs[quarters:quarters + carried], refs[quarters + carried:]
    targets, sems = refs[:-1], refs[-1]
    copies = fetch_all(sources, targets, sems)
    for copy in copies:
        copy.wait()
    for k, carry_ref in enumerate(carries):
        carry_ref[...] = targets[count + k][...]
    for d, out_ref in enumerate(outs):
        at = 0
        if bases:
            at = targets[d].shape[1]
            out_ref[:, :at] = targets[d][...]
        for c in range(bases, count, 2):
            kept_ref, got_ref = targets[c], targets[c + 1]
            width = kept_ref.shape[2]
            out_ref[:, at:at + width] = (kept_ref[d] + got_ref[d].astype(jnp.float32)).astype(out_ref.dtype)
            at = at + width


def merge(base, arrays, after, carry=()):
    quarters, rows = arrays[0].shape[:2]
    tokens = sum(array.shape[2] for array in arrays[::2]) + (base[0].shape[1] if base else 0)
    operands = list(base) + list(arrays) + list(carry)
    return pl.pallas_call(
        functools.partial(merge_kernel, quarters, len(base), len(arrays) // 2, len(carry), len(after)),
        in_specs=[pl.BlockSpec(memory_space=pl.ANY)] * (len(operands) + len(after)),
        out_specs=[pl.BlockSpec(memory_space=pltpu.VMEM)] * (quarters + len(carry)),
        out_shape=[jax.ShapeDtypeStruct((rows, tokens), jnp.bfloat16 if d else jnp.float32) for d in range(quarters)]
        + [jax.ShapeDtypeStruct(array.shape, array.dtype) for array in carry],
        scratch_shapes=[pltpu.VMEM(operand.shape, operand.dtype) for operand in operands] + [pltpu.SemaphoreType.DMA((len(operands),))],
        compiler_params=pltpu.CompilerParams(vmem_limit_bytes=VMEM // 6),
        cost_estimate=pl.CostEstimate(flops=quarters * rows * tokens, bytes_accessed=8 * quarters * rows * tokens, transcendentals=0),
        name="merge",
    )(*operands, *after)


def total_kernel(count, waits, *refs):
    sources, out_ref, targets, sems = refs[:count], refs[count + waits], refs[count + waits + 1:-1], refs[-1]
    for copy in fetch_all(sources, targets, sems):
        copy.wait()
    total = targets[0][...]
    for target in targets[1:]:
        total = total + target[...].astype(jnp.float32)
    out_ref[...] = total.astype(out_ref.dtype)


def total_of(parts, after):
    return pl.pallas_call(
        functools.partial(total_kernel, len(parts), len(after)),
        in_specs=[pl.BlockSpec(memory_space=pl.ANY)] * (len(parts) + len(after)),
        out_specs=pl.BlockSpec(memory_space=pltpu.VMEM),
        out_shape=jax.ShapeDtypeStruct(parts[0].shape, jnp.bfloat16),
        scratch_shapes=[pltpu.VMEM(part.shape, part.dtype) for part in parts] + [pltpu.SemaphoreType.DMA((len(parts),))],
        compiler_params=pltpu.CompilerParams(vmem_limit_bytes=VMEM // 6),
        cost_estimate=pl.CostEstimate(flops=parts[0].size * len(parts), bytes_accessed=2 * parts[0].size * len(parts), transcendentals=0),
        name="total",
    )(*parts, *after)


def pack_kernel(quarters, waits, *refs):
    count = quarters + 2
    sources, refs = refs[:count], refs[count + waits:]
    own_g_ref, own_a_ref, outs, refs = refs[0], refs[1], refs[2:quarters + 1], refs[quarters + 1:]
    targets, sems = refs[:-1], refs[-1]
    for copy in fetch_all(sources, targets, sems):
        copy.wait()
    total = targets[0][...]
    for target in targets[1:quarters]:
        total = total + target[...].astype(jnp.float32)
    own = total.astype(jnp.bfloat16)
    own_g_ref[...] = own
    kept_ref, got_ref = targets[quarters], targets[quarters + 1]
    own_a_ref[...] = kept_ref[0] + got_ref[0].astype(jnp.float32)
    rows, at = kept_ref.shape[1], own.shape[1]
    width = kept_ref.shape[2] * rows // R
    for d, out_ref in enumerate(outs, 1):
        out_ref[:, :at] = own
        for f in range(R // rows):
            here = slice(f * width, (f + 1) * width)
            out_ref[f * rows:(f + 1) * rows, at:] = (kept_ref[d, :, here] + got_ref[d, :, here].astype(jnp.float32)).astype(jnp.bfloat16)


def pack(parts, kept, got, after):
    quarters, rows, tokens = kept.shape
    operands = list(parts) + [kept, got]
    packed = jax.ShapeDtypeStruct((R, parts[0].shape[1] + tokens * rows // R), jnp.bfloat16)
    shapes = [jax.ShapeDtypeStruct(parts[0].shape, jnp.bfloat16), jax.ShapeDtypeStruct((rows, tokens), jnp.float32)]
    shapes = shapes + [packed] * (quarters - 1)
    return pl.pallas_call(
        functools.partial(pack_kernel, quarters, len(after)),
        in_specs=[pl.BlockSpec(memory_space=pl.ANY)] * (len(operands) + len(after)),
        out_specs=[pl.BlockSpec(memory_space=pltpu.VMEM)] * len(shapes),
        out_shape=shapes,
        scratch_shapes=[pltpu.VMEM(operand.shape, operand.dtype) for operand in operands] + [pltpu.SemaphoreType.DMA((len(operands),))],
        compiler_params=pltpu.CompilerParams(vmem_limit_bytes=VMEM // 6),
        cost_estimate=pl.CostEstimate(flops=4 * kept.size, bytes_accessed=8 * kept.size, transcendentals=0),
        name="pack",
    )(*operands, *after)


def sketch_rows(half, first, row_ref, col_ref, ids_ref, member_ref, spread_refs, sink):
    columns, tokens = row_ref.shape
    owned = ids_ref.shape[1] // 2
    width = math.gcd(tokens, 512)
    numbers = lax.broadcasted_iota(jnp.int32, (SEQ_DEV, 1), 0)
    ids = ids_ref[:, pl.ds(pl.multiple_of(half * owned + first, 128), tokens)]
    member_ref[...] = (ids == numbers).astype(jnp.bfloat16)
    rows = spread_refs[0].shape[0] // R
    for g in range(columns // rows):
        spread_ref = spread_refs[g % 2]
        for at in range(0, tokens, width):
            right = col_ref[:, first + at:first + at + width].astype(jnp.float32)
            for r in range(rows):
                row = row_ref[g * rows + r:g * rows + r + 1, at:at + width]
                spread_ref[r * R:(r + 1) * R, at:at + width] = (row * right).astype(jnp.bfloat16)
        part = lax.dot_general(member_ref[...], spread_ref[...], LAST, preferred_element_type=jnp.float32)
        sink(slice(g * rows * R, (g + 1) * rows * R), part)


def sketch_kernel(quarters, packed, who_ref, *refs):
    count = quarters + 2 if packed else 2 * quarters + 1
    sources, base_ref, col_ref, targets = refs[:count], refs[count], refs[count + 1], refs[count + 2:2 * count + 2]
    sems, row_ref, member_ref, spread_0, spread_1 = refs[2 * count + 2:]
    half, quarter = who_ref[0], who_ref[1]
    for copy in fetch_all(sources, targets, sems):
        copy.wait()
    ids_ref, own_ref, right_refs = targets[0], targets[1], targets[2:2 + quarters]
    piece = right_refs[0].shape[1]
    for d, right_ref in enumerate(right_refs):
        here = pl.ds(pl.multiple_of((quarter ^ d) * piece, piece), piece)
        col_ref[:, here] = right_ref[:, :piece]
    if packed:
        rows, tokens = row_ref.shape
        width = tokens * rows // R
        for f in range(R // rows):
            here = slice(f * width, (f + 1) * width)
            total = own_ref[:, here]
            for right_ref in right_refs[1:]:
                total = total + right_ref[f * rows:(f + 1) * rows, piece:].astype(jnp.float32)
            row_ref[:, here] = total
    else:
        row_ref[...] = sum([ref[...].astype(jnp.float32) for ref in targets[2 + quarters:]], own_ref[...])

    def sink(here, part):
        base_ref[:, here] = part

    sketch_rows(half, 0, row_ref, col_ref, ids_ref, member_ref, (spread_0, spread_1), sink)


def score_kernel(lefts, first, who_ref, *refs):
    count = lefts + 7
    sources, out_ref, targets = refs[:count], refs[count], refs[count + 1:2 * count + 1]
    sems, sketch_ref, row_ref, member_ref, spread_0, spread_1 = refs[2 * count + 1:]
    copies = fetch_all(sources, targets, sems)
    half, data = who_ref[0], who_ref[2]
    ids_ref, col_ref, base_ref, left_refs, query_refs = targets[0], targets[1], targets[2], targets[3:-4], targets[-4:]
    for copy in copies[:-4]:
        copy.wait()
    row_ref[...] = sum([ref[...].astype(jnp.float32) for ref in left_refs[1:]], left_refs[0][...])

    def sink(here, part):
        sketch_ref[:, here] = base_ref[:, here] + part

    sketch_rows(half, first, row_ref, col_ref, ids_ref, member_ref, (spread_0, spread_1), sink)
    entries = sketch_ref[...]
    high = entries.astype(jnp.bfloat16)
    low = (entries - high.astype(jnp.float32)).astype(jnp.bfloat16)
    both = jnp.concatenate([high, low], axis=0)
    middle = both.shape[1] // 2
    swapped = half == 1
    near = jnp.where(swapped, both[:, middle:], both[:, :middle])
    far = jnp.where(swapped, both[:, :middle], both[:, middle:])
    for copy in copies[-4:]:
        copy.wait()
    rows = query_refs[0].shape[0]
    for side in range(2):
        part = lax.dot_general(near, query_refs[2 * side][...], LAST, preferred_element_type=jnp.float32)
        part = part + lax.dot_general(far, query_refs[2 * side + 1][...], LAST, preferred_element_type=jnp.float32)
        out_ref[:, pl.ds(pl.multiple_of((data ^ side) * rows, rows), rows)] = part[:SEQ_DEV] + part[SEQ_DEV:]


def call_sketch(kernel, who, operands, columns, tokens, shapes, extra, name):
    rows = min(4, columns)
    return pl.pallas_call(
        kernel,
        in_specs=[pl.BlockSpec(memory_space=pltpu.SMEM)] + [pl.BlockSpec(memory_space=pl.ANY)] * len(operands),
        out_specs=[pl.BlockSpec(memory_space=pltpu.VMEM)] * len(shapes),
        out_shape=shapes,
        scratch_shapes=[pltpu.VMEM(operand.shape, operand.dtype) for operand in operands]
        + [pltpu.SemaphoreType.DMA((len(operands),))]
        + extra
        + [
            pltpu.VMEM((columns, tokens), jnp.float32),
            pltpu.VMEM((SEQ_DEV, tokens), jnp.bfloat16),
            pltpu.VMEM((rows * R, tokens), jnp.bfloat16),
            pltpu.VMEM((rows * R, tokens), jnp.bfloat16),
        ],
        compiler_params=pltpu.CompilerParams(vmem_limit_bytes=VMEM // 3),
        cost_estimate=pl.CostEstimate(flops=2 * tokens * columns * R * SEQ_DEV, bytes_accessed=4 * columns * tokens, transcendentals=0),
        name=name,
    )(who, *operands)


def body(n_tensor, activations, out_grads, proj_in, proj_out, segment_ids, queries):
    quarters = n_tensor // 2
    me = lax.axis_index("tensor").astype(jnp.int32)
    half = me % 2
    who = jnp.stack([half, me // 2, lax.axis_index("dp").astype(jnp.int32)])
    owned = activations.shape[0] // 2
    def swap(array, distance):
        return lax.ppermute(array, "tensor", [(k, k ^ distance) for k in range(n_tensor)])

    def cross(array):
        return lax.ppermute(array, "dp", [(0, 1), (1, 0)])

    far = swap(queries, 1)
    cross_near, cross_far = cross(queries), cross(far)
    every = [queries, far, cross_near, cross_far]

    scale_in, scale_out = FF ** -0.5, D ** -0.5
    sent_g, kept_g, signs = project(out_grads, proj_out.T, who, scale_out, quarters, False, 0, owned, 1024, proj_in.T)
    got_g = swap(sent_g, 1)

    def chunk(eighth, eighths, after):
        first, count = owned * eighth // 8, owned * eighths // 8
        sent, kept = project(activations, signs, who, scale_in, quarters, True, first, count, 512, None, after)
        return sent, [kept, swap(sent, 1)]

    sent_0, chunk_0 = chunk(0, 5, [])
    pair_g = merge([], [kept_g, got_g], [sent_0])
    moved_g = [swap(pair_g[d], 2 * d) for d in range(1, quarters)]
    sent_1, chunk_1 = chunk(5, 3, [pair_g[1], far, cross_near])
    columns = R // quarters
    packed = columns % 16 == 0
    if packed:
        sums = pack([pair_g[0]] + moved_g, chunk_0[0], chunk_0[1], [sent_1, cross_far])
        own_g, own_a = sums[:2]
        right = [own_g] + [swap(sums[d + 1], 2 * d) for d in range(1, quarters)]
        first = [segment_ids, own_a] + right
    else:
        own_g = total_of([pair_g[0]] + moved_g, [sent_1])
        right = [own_g] + [swap(own_g, 2 * d) for d in range(1, quarters)]
        pair_0 = merge([], chunk_0, [])
        first = [segment_ids, pair_0[0]] + right + [swap(pair_0[d], 2 * d) for d in range(1, quarters)]
    pair_1 = merge([], chunk_1, [])
    left = [pair_1[0]] + [swap(pair_1[d], 2 * d) for d in range(1, quarters)]

    early, entries = owned * 5 // 8, columns * R
    shapes = [jax.ShapeDtypeStruct((SEQ_DEV, entries), jnp.float32), jax.ShapeDtypeStruct((R, owned), jnp.bfloat16)]
    base, col = call_sketch(functools.partial(sketch_kernel, quarters, packed), who, first, columns, early, shapes, [], "sketch")
    shapes = [jax.ShapeDtypeStruct((SEQ_DEV, 2 * queries.shape[0]), jnp.float32)]
    extra = [pltpu.VMEM((SEQ_DEV, entries), jnp.float32)]
    rest = [segment_ids, col, base] + left + every
    total = call_sketch(functools.partial(score_kernel, quarters, early), who, rest, columns, owned - early, shapes, extra, "score")[0]
    total = (total + swap(total, 1)).astype(jnp.bfloat16)
    parts = [total] + [swap(total, 2 * d) for d in range(1, quarters)]
    parts = [part.astype(jnp.float32) for part in parts]
    while len(parts) > 1:
        parts = [parts[k] + parts[k + 1] for k in range(0, len(parts), 2)]
    return parts[0]


def solution(mesh):
    return jax.shard_map(
        functools.partial(body, mesh.shape["tensor"]),
        mesh=mesh,
        in_specs=(
            P(("copies", "dp"), "tensor"),
            P(("copies", "dp"), "tensor"),
            P("tensor", None),
            P("tensor", None),
            P(("copies", "dp"), None),
            P(("copies", "dp"), "tensor"),
        ),
        out_specs=P(("copies", "dp"), None),
        check_vma=False,
    )
```

```python
import functools
import math

import jax
import jax.numpy as jnp
from jax import lax
from jax.experimental import pallas as pl
from jax.experimental.pallas import tpu as pltpu
from jax.sharding import PartitionSpec as P

D = 8192
FF = 28672
R = 64
SEQ_DEV = 64
BUFFERS = 4
VMEM = 48 * 1024 * 1024
LAST = (((1,), (1,)), ((), ()))


def project_kernel(scale, first, split, columns, group, waits, who_ref, x_hbm, sign_source, *refs):
    makes = group > 0
    other_source, refs = refs[0], refs[makes + waits:]
    sent_ref, kept_ref, made_ref, refs = refs[0], refs[1], refs[2], refs[2 + makes:]
    bits_ref, other_ref = refs[0], refs[1]
    signs_ref, x_buf, sign_sem, sems = refs[-4:]
    half, quarter = who_ref[0], who_ref[1]
    buffers, tile = x_buf.shape[0], x_buf.shape[1]
    quarters = sent_ref.shape[0]
    steps = quarters * split
    total = steps if columns else 2 * steps
    per_quarter = x_hbm.shape[0] // quarters

    def copy(p):
        mine = (p >= steps).astype(jnp.int32)
        s = p - mine * steps
        row = ((s // split) ^ quarter) * per_quarter + lax.rem(s, split) * tile
        row = row + (first if columns else (half ^ 1 ^ mine) * (per_quarter // 2))
        slot = lax.rem(p, buffers)
        return pltpu.make_async_copy(x_hbm.at[pl.ds(pl.multiple_of(row, tile), tile)], x_buf.at[slot], sems.at[slot])

    sign_copy = pltpu.make_async_copy(sign_source, bits_ref, sign_sem.at[0])
    sign_copy.start()

    def begin(p, carry):
        copy(p).start()
        return carry

    lax.fori_loop(0, buffers, begin, 0)
    if makes:
        other_copy = pltpu.make_async_copy(other_source, other_ref, sign_sem.at[1])
        other_copy.start()
    sign_copy.wait()
    signs_ref[...] = (2 * bits_ref[...] - 1).astype(jnp.bfloat16) if makes else bits_ref[...]

    def one(p, carry):
        copy(p).wait()
        mine = (p >= steps).astype(jnp.int32)
        s = p - mine * steps
        part = lax.dot_general(
            signs_ref[...], x_buf[lax.rem(p, buffers)], LAST, preferred_element_type=jnp.float32
        ) * scale
        place = s // split
        here = pl.ds(pl.multiple_of(lax.rem(s, split) * tile, tile), tile)
        if columns:
            sent_ref[place, :, here] = part[:columns].astype(jnp.bfloat16)
            kept_ref[place, :, here] = part[columns:]
        else:
            @pl.when(p < steps)
            def _():
                sent_ref[place, :, here] = part.astype(jnp.bfloat16)

            @pl.when(p >= steps)
            def _():
                kept_ref[place, :, here] = part

        @pl.when(p + buffers < total)
        def _():
            copy(p + buffers).start()

        return carry

    lax.fori_loop(0, total, one, 0)
    if makes:
        other_copy.wait()
        if group % 8:
            made_ref[...] = (2 * other_ref[...] - 1).astype(jnp.bfloat16)
        else:
            blocks = []
            for k in range(R // group):
                side = half ^ 1 ^ (k // quarters)
                blocks.append(other_ref[pl.ds(pl.multiple_of((2 * (k % quarters) + side) * group, 8), group), :])
            for k in range(0, len(blocks), 2):
                pair = jnp.concatenate(blocks[k:k + 2], axis=0)
                made_ref[k * group:(k + 2) * group, :] = (2 * pair - 1).astype(jnp.bfloat16)


def project(x, signs, who, scale, quarters, columns, first, count, tile, other=None, after=()):
    width = x.shape[1]
    makes = other is not None
    group = 0
    tile = min(tile, count)
    rows = columns if columns else R
    if makes:
        group = R // (2 * quarters)
        if group % 8:
            order = jnp.arange(R, dtype=jnp.int32)
            side = who[0] ^ 1 ^ (order // (R // 2))
            order = order % (R // 2)
            other = jnp.take(other, (2 * (order // group) + side) * group + order % group, axis=0)
    shape = (quarters, rows, count)
    shapes = [jax.ShapeDtypeStruct(shape, jnp.bfloat16), jax.ShapeDtypeStruct(shape, jnp.float32)]
    scratch = [pltpu.VMEM(signs.shape, signs.dtype)]
    if makes:
        shapes.append(jax.ShapeDtypeStruct(other.shape, jnp.bfloat16))
        scratch.append(pltpu.VMEM(other.shape, other.dtype))
    split = count // tile
    blocks = quarters * split * (1 if columns else 2)
    buffers = min(BUFFERS, blocks)
    operands = [x, signs] + ([other] if makes else []) + list(after)
    return pl.pallas_call(
        functools.partial(project_kernel, scale, first, split, columns, group, len(after)),
        in_specs=[pl.BlockSpec(memory_space=pltpu.SMEM)] + [pl.BlockSpec(memory_space=pl.ANY)] * len(operands),
        out_specs=[pl.BlockSpec(memory_space=pltpu.VMEM)] * len(shapes),
        scratch_shapes=scratch
        + [
            pltpu.VMEM(signs.shape, jnp.bfloat16),
            pltpu.VMEM((buffers, tile, width), jnp.bfloat16),
            pltpu.SemaphoreType.DMA((2,)),
            pltpu.SemaphoreType.DMA((buffers,)),
        ],
        out_shape=shapes,
        compiler_params=pltpu.CompilerParams(vmem_limit_bytes=VMEM),
        cost_estimate=pl.CostEstimate(flops=2 * blocks * tile * width * R, bytes_accessed=2 * blocks * tile * width, transcendentals=0),
        name="project",
    )(who, *operands)


def fetch_all(sources, targets, sems):
    copies = [pltpu.make_async_copy(source, target, sems.at[k]) for k, (source, target) in enumerate(zip(sources, targets))]
    for copy in copies:
        copy.start()
    return copies


def merge_kernel(quarters, bases, pairs, carried, waits, *refs):
    count = bases + 2 * pairs
    sources, refs = refs[:count + carried], refs[count + carried + waits:]
    outs, carries, refs = refs[:quarters], refs[quarters:quarters + carried], refs[quarters + carried:]
    targets, sems = refs[:-1], refs[-1]
    copies = fetch_all(sources, targets, sems)
    for copy in copies:
        copy.wait()
    for k, carry_ref in enumerate(carries):
        carry_ref[...] = targets[count + k][...]
    for d, out_ref in enumerate(outs):
        at = 0
        if bases:
            at = targets[d].shape[1]
            out_ref[:, :at] = targets[d][...]
        for c in range(bases, count, 2):
            kept_ref, got_ref = targets[c], targets[c + 1]
            width = kept_ref.shape[2]
            out_ref[:, at:at + width] = (kept_ref[d] + got_ref[d].astype(jnp.float32)).astype(out_ref.dtype)
            at = at + width


def merge(base, arrays, after, carry=()):
    quarters, rows = arrays[0].shape[:2]
    tokens = sum(array.shape[2] for array in arrays[::2]) + (base[0].shape[1] if base else 0)
    operands = list(base) + list(arrays) + list(carry)
    return pl.pallas_call(
        functools.partial(merge_kernel, quarters, len(base), len(arrays) // 2, len(carry), len(after)),
        in_specs=[pl.BlockSpec(memory_space=pl.ANY)] * (len(operands) + len(after)),
        out_specs=[pl.BlockSpec(memory_space=pltpu.VMEM)] * (quarters + len(carry)),
        out_shape=[jax.ShapeDtypeStruct((rows, tokens), jnp.bfloat16 if d else jnp.float32) for d in range(quarters)]
        + [jax.ShapeDtypeStruct(array.shape, array.dtype) for array in carry],
        scratch_shapes=[pltpu.VMEM(operand.shape, operand.dtype) for operand in operands] + [pltpu.SemaphoreType.DMA((len(operands),))],
        compiler_params=pltpu.CompilerParams(vmem_limit_bytes=VMEM // 6),
        cost_estimate=pl.CostEstimate(flops=quarters * rows * tokens, bytes_accessed=8 * quarters * rows * tokens, transcendentals=0),
        name="merge",
    )(*operands, *after)


def total_kernel(count, waits, *refs):
    sources, out_ref, targets, sems = refs[:count], refs[count + waits], refs[count + waits + 1:-1], refs[-1]
    for copy in fetch_all(sources, targets, sems):
        copy.wait()
    total = targets[0][...]
    for target in targets[1:]:
        total = total + target[...].astype(jnp.float32)
    out_ref[...] = total.astype(out_ref.dtype)


def total_of(parts, after):
    return pl.pallas_call(
        functools.partial(total_kernel, len(parts), len(after)),
        in_specs=[pl.BlockSpec(memory_space=pl.ANY)] * (len(parts) + len(after)),
        out_specs=pl.BlockSpec(memory_space=pltpu.VMEM),
        out_shape=jax.ShapeDtypeStruct(parts[0].shape, jnp.bfloat16),
        scratch_shapes=[pltpu.VMEM(part.shape, part.dtype) for part in parts] + [pltpu.SemaphoreType.DMA((len(parts),))],
        compiler_params=pltpu.CompilerParams(vmem_limit_bytes=VMEM // 6),
        cost_estimate=pl.CostEstimate(flops=parts[0].size * len(parts), bytes_accessed=2 * parts[0].size * len(parts), transcendentals=0),
        name="total",
    )(*parts, *after)


def stack_kernel(count, waits, *refs):
    sources, out_ref, sems = refs[:count], refs[count + waits], refs[-1]
    rows = sources[0].shape[0]
    targets = [out_ref.at[pl.ds(k * rows, rows)] for k in range(count)]
    for copy in fetch_all(sources, targets, sems):
        copy.wait()


def stack(arrays, after):
    rows, width = arrays[0].shape
    return pl.pallas_call(
        functools.partial(stack_kernel, len(arrays), len(after)),
        in_specs=[pl.BlockSpec(memory_space=pl.ANY)] * (len(arrays) + len(after)),
        out_specs=pl.BlockSpec(memory_space=pltpu.VMEM),
        out_shape=jax.ShapeDtypeStruct((len(arrays) * rows, width), arrays[0].dtype),
        scratch_shapes=[pltpu.SemaphoreType.DMA((len(arrays),))],
        compiler_params=pltpu.CompilerParams(vmem_limit_bytes=VMEM // 6),
        cost_estimate=pl.CostEstimate(flops=0, bytes_accessed=0, transcendentals=0),
        name="stack",
    )(*arrays, *after)


def sketch_rows(quarter, first, row_ref, col_ref, ids_ref, member_ref, spread_refs, sink):
    columns, tokens = row_ref.shape
    width = math.gcd(tokens, 512)
    numbers = lax.broadcasted_iota(jnp.int32, (SEQ_DEV, 1), 0)
    ids = ids_ref[:, pl.ds(pl.multiple_of(quarter * col_ref.shape[1] + first, 128), tokens)]
    member_ref[...] = (ids == numbers).astype(jnp.bfloat16)
    rows = spread_refs[0].shape[0] // R
    for g in range(columns // rows):
        spread_ref = spread_refs[g % 2]
        for at in range(0, tokens, width):
            right = col_ref[:, first + at:first + at + width].astype(jnp.float32)
            for r in range(rows):
                row = row_ref[g * rows + r:g * rows + r + 1, at:at + width]
                spread_ref[r * R:(r + 1) * R, at:at + width] = (row * right).astype(jnp.bfloat16)
        part = lax.dot_general(member_ref[...], spread_ref[...], LAST, preferred_element_type=jnp.float32)
        sink(slice(g * rows * R, (g + 1) * rows * R), part)


def sketch_kernel(lefts, who_ref, *refs):
    count = lefts + 3
    sources, base_ref, col_ref, targets = refs[:count], refs[count], refs[count + 1], refs[count + 2:2 * count + 2]
    sems, row_ref, member_ref, spread_0, spread_1 = refs[2 * count + 2:]
    half, quarter = who_ref[0], who_ref[1]
    for copy in fetch_all(sources, targets, sems):
        copy.wait()
    piece = targets[1].shape[1]
    for k in range(2):
        col_ref[:, pl.ds(pl.multiple_of((half ^ k) * piece, piece), piece)] = targets[1 + k][...]
    row_ref[...] = sum([ref[...].astype(jnp.float32) for ref in targets[4:]], targets[3][...])

    def sink(here, part):
        base_ref[:, here] = part

    sketch_rows(quarter, 0, row_ref, col_ref, targets[0], member_ref, (spread_0, spread_1), sink)


def score_kernel(lefts, asks, first, who_ref, *refs):
    count = lefts + 3 + asks
    sources, out_ref, targets = refs[:count], refs[count], refs[count + 1:2 * count + 1]
    sems, refs = refs[2 * count + 1], refs[2 * count + 2:]
    row_ref, member_ref, spread_0, spread_1 = refs[-4:]
    copies = fetch_all(sources, targets, sems)
    quarter, data = who_ref[1], who_ref[2]
    ids_ref, col_ref, base_ref, left_refs = targets[0], targets[1], targets[2], targets[3:3 + lefts]
    for copy in copies[:3 + lefts]:
        copy.wait()
    row_ref[...] = sum([ref[...].astype(jnp.float32) for ref in left_refs[1:]], left_refs[0][...])
    sketch_ref = refs[0] if asks else out_ref

    def sink(here, part):
        sketch_ref[:, here] = base_ref[:, here] + part

    sketch_rows(quarter, first, row_ref, col_ref, ids_ref, member_ref, (spread_0, spread_1), sink)
    if asks:
        both_ref, query_refs = refs[1], targets[3 + lefts:]
        entries = sketch_ref[...]
        high = entries.astype(jnp.bfloat16)
        both_ref[:SEQ_DEV, :] = high
        both_ref[SEQ_DEV:, :] = (entries - high.astype(jnp.float32)).astype(jnp.bfloat16)
        for copy in copies[3 + lefts:]:
            copy.wait()
        rows, wide = query_refs[0].shape
        for side in range(2):
            total = jnp.zeros((2 * SEQ_DEV, rows), jnp.float32)
            for d in range(lefts):
                query = query_refs[lefts][d * rows:(d + 1) * rows, :] if side else query_refs[d][...]
                near = both_ref[:, pl.ds(pl.multiple_of((quarter ^ d) * wide, wide), wide)]
                total = total + lax.dot_general(near, query, LAST, preferred_element_type=jnp.float32)
            here = pl.ds(pl.multiple_of((data ^ side) * rows, rows), rows)
            out_ref[:, here] = total[:SEQ_DEV] + total[SEQ_DEV:]


def plain_scores(who, entries, asked, crossed):
    quarters = len(asked)
    own = jnp.stack(asked)
    other = crossed.reshape(own.shape)
    both = jnp.where(who[2] == 0, jnp.concatenate([own, other], 1), jnp.concatenate([other, own], 1))
    both = jnp.take(both, jnp.arange(quarters, dtype=jnp.int32) ^ who[1], axis=0)
    both = both.transpose(1, 0, 2).reshape(both.shape[1], -1)
    rounded = lax.reduce_precision(entries, 8, 7)
    low = (entries - rounded).astype(jnp.bfloat16)
    total = lax.dot_general(rounded.astype(jnp.bfloat16), both, LAST, preferred_element_type=jnp.float32)
    return total + lax.dot_general(low, both, LAST, preferred_element_type=jnp.float32)


def call_sketch(kernel, who, operands, columns, tokens, shapes, extra, name):
    rows = min(4, columns)
    return pl.pallas_call(
        kernel,
        in_specs=[pl.BlockSpec(memory_space=pltpu.SMEM)] + [pl.BlockSpec(memory_space=pl.ANY)] * len(operands),
        out_specs=[pl.BlockSpec(memory_space=pltpu.VMEM)] * len(shapes),
        out_shape=shapes,
        scratch_shapes=[pltpu.VMEM(operand.shape, operand.dtype) for operand in operands]
        + [pltpu.SemaphoreType.DMA((len(operands),))]
        + extra
        + [
            pltpu.VMEM((columns, tokens), jnp.float32),
            pltpu.VMEM((SEQ_DEV, tokens), jnp.bfloat16),
            pltpu.VMEM((rows * R, tokens), jnp.bfloat16),
            pltpu.VMEM((rows * R, tokens), jnp.bfloat16),
        ],
        compiler_params=pltpu.CompilerParams(vmem_limit_bytes=VMEM // 3),
        cost_estimate=pl.CostEstimate(flops=2 * tokens * columns * R * SEQ_DEV, bytes_accessed=4 * columns * tokens, transcendentals=0),
        name=name,
    )(who, *operands)


def body(n_tensor, activations, out_grads, proj_in, proj_out, segment_ids, queries):
    quarters = n_tensor // 2
    me = lax.axis_index("tensor").astype(jnp.int32)
    half = me % 2
    who = jnp.stack([half, me // 2, lax.axis_index("dp").astype(jnp.int32)])
    owned = activations.shape[0] // quarters
    early = owned * 3 // 4 if owned % 2048 == 0 else owned // 2
    columns = R // 2

    def swap(array, distance):
        return lax.ppermute(array, "tensor", [(k, k ^ distance) for k in range(n_tensor)])

    def along(arrays):
        return [swap(arrays[d], 2 * d) for d in range(1, quarters)]

    asked = [queries] + along([queries] * quarters)

    scale_in, scale_out = FF ** -0.5, D ** -0.5
    sent_g, kept_g, signs = project(out_grads, proj_out.T, who, scale_out, quarters, 0, 0, owned // 2, 1024, proj_in.T)
    got_g = swap(sent_g, 1)

    def chunk(first, count, after):
        sent, kept = project(activations, signs, who, scale_in, quarters, columns, first, count, 512, None, after)
        return sent, [kept, swap(sent, 1)]

    sent_0, chunk_0 = chunk(0, early, [])
    crossed = lax.ppermute(stack(asked, [sent_0, got_g]), "dp", [(0, 1), (1, 0)])
    pair_g = merge([], [kept_g, got_g], [sent_0])
    moved_g = along(pair_g)
    sent_1, chunk_1 = chunk(early, owned - early, [pair_g[1]])
    own_g = total_of([pair_g[0]] + moved_g, [sent_1, crossed])
    other_g = swap(own_g, 1)
    pair_0 = merge([], chunk_0, [sent_1])
    left_0 = [pair_0[0]] + along(pair_0)
    pair_1 = merge([], chunk_1, [])
    left_1 = [pair_1[0]] + along(pair_1)

    entries = columns * R
    shapes = [jax.ShapeDtypeStruct((SEQ_DEV, entries), jnp.float32), jax.ShapeDtypeStruct((R, owned), jnp.bfloat16)]
    first = [segment_ids, own_g, other_g] + left_0
    base, col = call_sketch(functools.partial(sketch_kernel, quarters), who, first, columns, early, shapes, [], "sketch")
    rest = [segment_ids, col, base] + left_1
    asks = 0 if queries.shape[1] % 128 else quarters + 1
    kernel = functools.partial(score_kernel, quarters, asks, early)
    if not asks:
        shapes = [jax.ShapeDtypeStruct((SEQ_DEV, entries), jnp.float32)]
        total = call_sketch(kernel, who, rest, columns, owned - early, shapes, [], "sketch_rest")[0]
        total = plain_scores(who, total, asked, crossed)
    else:
        shapes = [jax.ShapeDtypeStruct((SEQ_DEV, 2 * queries.shape[0]), jnp.float32)]
        extra = [pltpu.VMEM((SEQ_DEV, entries), jnp.float32), pltpu.VMEM((2 * SEQ_DEV, entries), jnp.bfloat16)]
        rest = rest + asked + [crossed]
        total = call_sketch(kernel, who, rest, columns, owned - early, shapes, extra, "score")[0]
    total = (total + swap(total, 1)).astype(jnp.bfloat16)
    parts = [total] + [swap(total, 2 * d) for d in range(1, quarters)]
    parts = [part.astype(jnp.float32) for part in parts]
    while len(parts) > 1:
        parts = [parts[k] + parts[k + 1] for k in range(0, len(parts), 2)]
    return parts[0]


def solution(mesh):
    return jax.shard_map(
        functools.partial(body, mesh.shape["tensor"]),
        mesh=mesh,
        in_specs=(
            P(("copies", "dp"), "tensor"),
            P(("copies", "dp"), "tensor"),
            P("tensor", None),
            P("tensor", None),
            P(("copies", "dp"), None),
            P(("copies", "dp"), "tensor"),
        ),
        out_specs=P(("copies", "dp"), None),
        check_vma=False,
    )
```

```python
import functools

import jax
import jax.numpy as jnp
from jax import lax
from jax.experimental import pallas as pl
from jax.experimental.pallas import tpu as pltpu
from jax.sharding import PartitionSpec as P

D = 8192
FF = 28672
R = 64
SEQ_DEV = 64
BUFFERS = 4
VMEM = 48 * 1024 * 1024
LAST = (((1,), (1,)), ((), ()))


def project_kernel(scale, order, first, split, who_ref, x_hbm, bits_hbm, *refs):
    sent_ref, kept_ref, bits_ref, signs_ref, x_buf, bits_sem, sems = refs[-7:]
    half, quarter = who_ref[0], who_ref[1]
    buffers, tile = x_buf.shape[0], x_buf.shape[1]
    steps = sent_ref.size // R // tile

    def copy(s, mine):
        slot = lax.rem(s + mine * steps, buffers)
        row = pl.multiple_of((half ^ 1 ^ mine) * (x_hbm.shape[0] // 2) + first + s * tile, tile)
        return pltpu.make_async_copy(x_hbm.at[pl.ds(row, tile)], x_buf.at[slot], sems.at[slot])

    bits_copy = pltpu.make_async_copy(bits_hbm, bits_ref, bits_sem)
    bits_copy.start()
    ahead = min(buffers, steps)
    for s in range(ahead):
        copy(s, 0).start()
    bits_copy.wait()
    for q in range(max(order, 1)):
        rows = R // max(order, 1)
        at = pl.multiple_of((q ^ quarter) * rows, rows) if order else 0
        signs_ref[q * rows:(q + 1) * rows, :] = (2 * bits_ref[pl.ds(at, rows), :] - 1).astype(jnp.bfloat16)

    for mine, out_ref in enumerate((sent_ref, kept_ref)):
        def one(s, carry):
            copy(s, mine).wait()
            slot = lax.rem(s + mine * steps, buffers)
            part = lax.dot_general(signs_ref[...], x_buf[slot], LAST, preferred_element_type=jnp.float32) * scale
            part = part.astype(out_ref.dtype)
            if split:
                here = pl.ds(pl.multiple_of(lax.rem(s, split) * tile, tile), tile)
                out_ref[(s // split) ^ quarter, :, here] = part
            else:
                here = pl.ds(pl.multiple_of(s * tile, tile), tile)
                out_ref[:, :, here] = part.reshape(out_ref.shape[0], out_ref.shape[1], tile)

            @pl.when(s + ahead < steps)
            def _():
                copy(s + ahead, mine).start()

            if not mine:
                @pl.when(s + ahead >= steps)
                def _():
                    copy(s + ahead - steps, 1).start()

            return carry

        lax.fori_loop(0, steps, one, 0)


def project(x, bits, who, scale, quarters, by_column, first, count, tile, after=()):
    width = x.shape[1]
    piece = count // quarters
    order, split = 0, 0
    if not by_column:
        tile = min(tile, piece)
        split = piece // tile
        shape = (quarters, R, piece)
    else:
        shape = (quarters, R // quarters, count)
        if (R // quarters) % 8:
            rows = jnp.arange(R, dtype=jnp.int32)
            bits = jnp.take(bits, rows ^ (who[1] * (R // quarters)), axis=0)
        else:
            order = quarters
    whole = pl.BlockSpec(memory_space=pltpu.VMEM)
    buffers = min(BUFFERS, count // tile)
    return pl.pallas_call(
        functools.partial(project_kernel, scale, order, first, split),
        in_specs=[pl.BlockSpec(memory_space=pltpu.SMEM)] + [pl.BlockSpec(memory_space=pl.ANY)] * (2 + len(after)),
        out_specs=[whole, whole],
        scratch_shapes=[
            pltpu.VMEM((R, width), jnp.int32),
            pltpu.VMEM((R, width), jnp.bfloat16),
            pltpu.VMEM((buffers, tile, width), jnp.bfloat16),
            pltpu.SemaphoreType.DMA,
            pltpu.SemaphoreType.DMA((buffers,)),
        ],
        out_shape=[jax.ShapeDtypeStruct(shape, jnp.bfloat16), jax.ShapeDtypeStruct(shape, jnp.float32)],
        compiler_params=pltpu.CompilerParams(vmem_limit_bytes=VMEM),
        cost_estimate=pl.CostEstimate(flops=4 * count * width * R, bytes_accessed=4 * count * width, transcendentals=0),
        name="project",
    )(who, x, bits, *after)


def fetch_all(sources, targets, sems):
    copies = [pltpu.make_async_copy(source, target, sems.at[k]) for k, (source, target) in enumerate(zip(sources, targets))]
    for copy in copies:
        copy.start()
    return copies


def merge_kernel(chunks, *refs):
    sources, outs = refs[:2 * chunks], refs[2 * chunks:-2 * chunks - 1]
    targets, sems = refs[-2 * chunks - 1:-1], refs[-1]
    copies = fetch_all(sources, targets, sems)
    at = 0
    for c in range(chunks):
        kept_ref, got_ref = targets[2 * c], targets[2 * c + 1]
        copies[2 * c].wait()
        copies[2 * c + 1].wait()
        width = kept_ref.shape[2]
        for d, out_ref in enumerate(outs):
            out_ref[:, at:at + width] = (kept_ref[d] + got_ref[d].astype(jnp.float32)).astype(out_ref.dtype)
        at = at + width


def merge(arrays):
    quarters, rows = arrays[0].shape[:2]
    tokens = sum(array.shape[2] for array in arrays[::2])
    whole = pl.BlockSpec(memory_space=pltpu.VMEM)
    return pl.pallas_call(
        functools.partial(merge_kernel, len(arrays) // 2),
        in_specs=[pl.BlockSpec(memory_space=pl.ANY)] * len(arrays),
        out_specs=[whole] * quarters,
        out_shape=[jax.ShapeDtypeStruct((rows, tokens), jnp.bfloat16 if d else jnp.float32) for d in range(quarters)],
        scratch_shapes=[pltpu.VMEM(array.shape, array.dtype) for array in arrays] + [pltpu.SemaphoreType.DMA((len(arrays),))],
        compiler_params=pltpu.CompilerParams(vmem_limit_bytes=VMEM // 6),
        cost_estimate=pl.CostEstimate(flops=quarters * rows * tokens, bytes_accessed=8 * quarters * rows * tokens, transcendentals=0),
        name="merge",
    )(*arrays)


def score_kernel(quarters, width, who_ref, *refs):
    count = 2 * quarters + 5
    sources, out_ref, targets = refs[:count], refs[count], refs[count + 1:2 * count + 1]
    sems, row_ref, col_ref, member_ref, sketch_ref = refs[2 * count + 1:-2]
    spread_refs = refs[-2:]
    copies = fetch_all(sources, targets, sems)
    left_refs, right_refs = targets[:quarters], targets[quarters:2 * quarters]
    ids_ref, query_refs = targets[2 * quarters], targets[2 * quarters + 1:]
    half, quarter, data = who_ref[0], who_ref[1], who_ref[2]
    for copy in copies[:2 * quarters + 1]:
        copy.wait()
    total = left_refs[0][...]
    for left_ref in left_refs[1:]:
        total = total + left_ref[...].astype(jnp.float32)
    row_ref[...] = total
    piece = right_refs[0].shape[1]
    for d, right_ref in enumerate(right_refs):
        col_ref[:, pl.ds(pl.multiple_of((quarter ^ d) * piece, piece), piece)] = right_ref[...].astype(jnp.float32)
    numbers = lax.broadcasted_iota(jnp.int32, (SEQ_DEV, 1), 0)
    owned = col_ref.shape[1]
    ids = ids_ref[:, pl.ds(pl.multiple_of(half * owned, 128), owned)]
    member_ref[...] = (ids == numbers).astype(jnp.bfloat16)
    rows = spread_refs[0].shape[0] // R
    for g in range(row_ref.shape[0] // rows):
        spread_ref = spread_refs[g % 2]
        for at in range(0, owned, width):
            right = col_ref[:, at:at + width]
            for r in range(rows):
                row = row_ref[g * rows + r:g * rows + r + 1, at:at + width]
                spread_ref[r * R:(r + 1) * R, at:at + width] = (row * right).astype(jnp.bfloat16)
        sketch_ref[:, g * rows * R:(g + 1) * rows * R] = lax.dot_general(
            member_ref[...], spread_ref[...], LAST, preferred_element_type=jnp.float32
        )
    entries = sketch_ref[...]
    high = entries.astype(jnp.bfloat16)
    low = (entries - high.astype(jnp.float32)).astype(jnp.bfloat16)
    both = jnp.concatenate([high, low], axis=0)
    middle = both.shape[1] // 2
    swapped = half == 1
    near = jnp.where(swapped, both[:, middle:], both[:, :middle])
    far = jnp.where(swapped, both[:, :middle], both[:, middle:])
    for copy in copies[2 * quarters + 1:]:
        copy.wait()
    rows = query_refs[0].shape[0]
    for side in range(2):
        part = lax.dot_general(near, query_refs[2 * side][...], LAST, preferred_element_type=jnp.float32)
        part = part + lax.dot_general(far, query_refs[2 * side + 1][...], LAST, preferred_element_type=jnp.float32)
        out_ref[:, pl.ds(pl.multiple_of((data ^ side) * rows, rows), rows)] = part[:SEQ_DEV] + part[SEQ_DEV:]


def score(who, left, right, ids, queries):
    operands = left + right + [ids] + queries
    columns, tokens = left[0].shape
    rows = min(4, columns)
    shape = (SEQ_DEV, 2 * queries[0].shape[0])
    return pl.pallas_call(
        functools.partial(score_kernel, len(left), min(512, tokens)),
        in_specs=[pl.BlockSpec(memory_space=pltpu.SMEM)] + [pl.BlockSpec(memory_space=pl.ANY)] * len(operands),
        out_specs=pl.BlockSpec(memory_space=pltpu.VMEM),
        out_shape=jax.ShapeDtypeStruct(shape, jnp.float32),
        scratch_shapes=[pltpu.VMEM(operand.shape, operand.dtype) for operand in operands]
        + [
            pltpu.SemaphoreType.DMA((len(operands),)),
            pltpu.VMEM((columns, tokens), jnp.float32),
            pltpu.VMEM((R, tokens), jnp.float32),
            pltpu.VMEM((SEQ_DEV, tokens), jnp.bfloat16),
            pltpu.VMEM((SEQ_DEV, columns * R), jnp.float32),
            pltpu.VMEM((rows * R, tokens), jnp.bfloat16),
            pltpu.VMEM((rows * R, tokens), jnp.bfloat16),
        ],
        compiler_params=pltpu.CompilerParams(vmem_limit_bytes=VMEM // 3),
        cost_estimate=pl.CostEstimate(flops=2 * tokens * columns * R * SEQ_DEV, bytes_accessed=4 * columns * tokens, transcendentals=0),
        name="score",
    )(who, *operands)


def body(n_tensor, activations, out_grads, proj_in, proj_out, segment_ids, queries):
    quarters = n_tensor // 2
    me = lax.axis_index("tensor").astype(jnp.int32)
    half = me % 2
    who = jnp.stack([half, me // 2, lax.axis_index("dp").astype(jnp.int32)])
    owned = activations.shape[0] // 2
    early = owned * 5 // 8

    def swap(array, distance):
        return lax.ppermute(array, "tensor", [(k, k ^ distance) for k in range(n_tensor)])

    def cross(array):
        return lax.ppermute(array, "dp", [(0, 1), (1, 0)])

    far = swap(queries, 1)
    cross_near, cross_far = cross(queries), cross(far)
    every = [queries, far, cross_near, cross_far]

    bits_in, bits_out = proj_in.T, proj_out.T
    scale_in, scale_out = FF ** -0.5, D ** -0.5
    sent_g, kept_g = project(out_grads, bits_out, who, scale_out, quarters, False, 0, owned, 1024)
    got_g = swap(sent_g, 1)
    sent_0, kept_0 = project(activations, bits_in, who, scale_in, quarters, True, 0, early, 512)
    got_0 = swap(sent_0, 1)
    pair_g = [kept_g[d] + got_g[d].astype(jnp.float32) for d in range(quarters)]
    pair_g = [pair_g[0]] + [pair.astype(jnp.bfloat16) for pair in pair_g[1:]]
    moved_g = [swap(pair_g[d], 2 * d) for d in range(1, quarters)]
    sent_1, kept_1 = project(activations, bits_in, who, scale_in, quarters, True, early, owned - early, 512, [pair_g[1], far, cross_near])
    got_1 = swap(sent_1, 1)
    own_g = sum([moved.astype(jnp.float32) for moved in moved_g], pair_g[0]).astype(jnp.bfloat16)
    right = [own_g] + [swap(own_g, 2 * d) for d in range(1, quarters)]
    pair_a = merge([kept_0, got_0, kept_1, got_1])
    left = [pair_a[0]] + [swap(pair_a[d], 2 * d) for d in range(1, quarters)]

    total = score(who, left, right, segment_ids, every)
    total = (total + swap(total, 1)).astype(jnp.bfloat16)
    parts = [total] + [swap(total, 2 * d) for d in range(1, quarters)]
    parts = [part.astype(jnp.float32) for part in parts]
    while len(parts) > 1:
        parts = [parts[k] + parts[k + 1] for k in range(0, len(parts), 2)]
    return parts[0]


def solution(mesh):
    return jax.shard_map(
        functools.partial(body, mesh.shape["tensor"]),
        mesh=mesh,
        in_specs=(
            P(("copies", "dp"), "tensor"),
            P(("copies", "dp"), "tensor"),
            P("tensor", None),
            P("tensor", None),
            P(("copies", "dp"), None),
            P(("copies", "dp"), "tensor"),
        ),
        out_specs=P(("copies", "dp"), None),
        check_vma=False,
    )
```

```python
import functools

import jax
import jax.numpy as jnp
from jax import lax
from jax.experimental import pallas as pl
from jax.experimental.pallas import tpu as pltpu
from jax.sharding import PartitionSpec as P

D = 8192
FF = 28672
R = 64
SEQ_DEV = 64
BUFFERS = 4
VMEM = 48 * 1024 * 1024
LAST = (((1,), (1,)), ((), ()))


def project_kernel(scale, order, first, split, who_ref, x_hbm, bits_hbm, *refs):
    sent_ref, kept_ref, bits_ref, signs_ref, x_buf, bits_sem, sems = refs[-7:]
    half, quarter = who_ref[0], who_ref[1]
    buffers, tile = x_buf.shape[0], x_buf.shape[1]
    steps = sent_ref.size // R // tile

    def copy(s, mine):
        slot = lax.rem(s + mine * steps, buffers)
        row = pl.multiple_of((half ^ 1 ^ mine) * (x_hbm.shape[0] // 2) + first + s * tile, tile)
        return pltpu.make_async_copy(x_hbm.at[pl.ds(row, tile)], x_buf.at[slot], sems.at[slot])

    bits_copy = pltpu.make_async_copy(bits_hbm, bits_ref, bits_sem)
    bits_copy.start()
    ahead = min(buffers, steps)
    for s in range(ahead):
        copy(s, 0).start()
    bits_copy.wait()
    for q in range(max(order, 1)):
        rows = R // max(order, 1)
        at = pl.multiple_of((q ^ quarter) * rows, rows) if order else 0
        signs_ref[q * rows:(q + 1) * rows, :] = (2 * bits_ref[pl.ds(at, rows), :] - 1).astype(jnp.bfloat16)

    for mine, out_ref in enumerate((sent_ref, kept_ref)):
        def one(s, carry):
            copy(s, mine).wait()
            slot = lax.rem(s + mine * steps, buffers)
            part = lax.dot_general(signs_ref[...], x_buf[slot], LAST, preferred_element_type=jnp.float32) * scale
            part = part.astype(out_ref.dtype)
            if split:
                here = pl.ds(pl.multiple_of(lax.rem(s, split) * tile, tile), tile)
                out_ref[(s // split) ^ quarter, :, here] = part
            else:
                here = pl.ds(pl.multiple_of(s * tile, tile), tile)
                out_ref[:, :, here] = part.reshape(out_ref.shape[0], out_ref.shape[1], tile)

            @pl.when(s + ahead < steps)
            def _():
                copy(s + ahead, mine).start()

            if not mine:
                @pl.when(s + ahead >= steps)
                def _():
                    copy(s + ahead - steps, 1).start()

            return carry

        lax.fori_loop(0, steps, one, 0)


def project(x, bits, who, scale, quarters, by_column, first, count, tile, after=()):
    width = x.shape[1]
    piece = count // quarters
    order, split = 0, 0
    if not by_column:
        tile = min(tile, piece)
        split = piece // tile
        shape = (quarters, R, piece)
    else:
        shape = (quarters, R // quarters, count)
        if (R // quarters) % 8:
            rows = jnp.arange(R, dtype=jnp.int32)
            bits = jnp.take(bits, rows ^ (who[1] * (R // quarters)), axis=0)
        else:
            order = quarters
    whole = pl.BlockSpec(memory_space=pltpu.VMEM)
    buffers = min(BUFFERS, count // tile)
    return pl.pallas_call(
        functools.partial(project_kernel, scale, order, first, split),
        in_specs=[pl.BlockSpec(memory_space=pltpu.SMEM)] + [pl.BlockSpec(memory_space=pl.ANY)] * (2 + len(after)),
        out_specs=[whole, whole],
        scratch_shapes=[
            pltpu.VMEM((R, width), jnp.int32),
            pltpu.VMEM((R, width), jnp.bfloat16),
            pltpu.VMEM((buffers, tile, width), jnp.bfloat16),
            pltpu.SemaphoreType.DMA,
            pltpu.SemaphoreType.DMA((buffers,)),
        ],
        out_shape=[jax.ShapeDtypeStruct(shape, jnp.bfloat16), jax.ShapeDtypeStruct(shape, jnp.float32)],
        compiler_params=pltpu.CompilerParams(vmem_limit_bytes=VMEM),
        cost_estimate=pl.CostEstimate(flops=4 * count * width * R, bytes_accessed=4 * count * width, transcendentals=0),
        name="project",
    )(who, x, bits, *after)


def fetch_all(sources, targets, sems):
    copies = [pltpu.make_async_copy(source, target, sems.at[k]) for k, (source, target) in enumerate(zip(sources, targets))]
    for copy in copies:
        copy.start()
    return copies


def merge_kernel(chunks, *refs):
    sources, outs = refs[:2 * chunks], refs[2 * chunks:-2 * chunks - 1]
    targets, sems = refs[-2 * chunks - 1:-1], refs[-1]
    copies = fetch_all(sources, targets, sems)
    at = 0
    for c in range(chunks):
        kept_ref, got_ref = targets[2 * c], targets[2 * c + 1]
        copies[2 * c].wait()
        copies[2 * c + 1].wait()
        width = kept_ref.shape[2]
        for d, out_ref in enumerate(outs):
            out_ref[:, at:at + width] = (kept_ref[d] + got_ref[d].astype(jnp.float32)).astype(out_ref.dtype)
        at = at + width


def merge(arrays):
    quarters, rows = arrays[0].shape[:2]
    tokens = sum(array.shape[2] for array in arrays[::2])
    whole = pl.BlockSpec(memory_space=pltpu.VMEM)
    return pl.pallas_call(
        functools.partial(merge_kernel, len(arrays) // 2),
        in_specs=[pl.BlockSpec(memory_space=pl.ANY)] * len(arrays),
        out_specs=[whole] * quarters,
        out_shape=[jax.ShapeDtypeStruct((rows, tokens), jnp.bfloat16 if d else jnp.float32) for d in range(quarters)],
        scratch_shapes=[pltpu.VMEM(array.shape, array.dtype) for array in arrays] + [pltpu.SemaphoreType.DMA((len(arrays),))],
        compiler_params=pltpu.CompilerParams(vmem_limit_bytes=VMEM // 6),
        cost_estimate=pl.CostEstimate(flops=quarters * rows * tokens, bytes_accessed=8 * quarters * rows * tokens, transcendentals=0),
        name="merge",
    )(*arrays)


def score_kernel(quarters, width, who_ref, *refs):
    count = 2 * quarters + 5
    sources, out_ref, targets = refs[:count], refs[count], refs[count + 1:2 * count + 1]
    sems, row_ref, col_ref, member_ref, sketch_ref = refs[2 * count + 1:-2]
    spread_refs = refs[-2:]
    copies = fetch_all(sources, targets, sems)
    left_refs, right_refs = targets[:quarters], targets[quarters:2 * quarters]
    ids_ref, query_refs = targets[2 * quarters], targets[2 * quarters + 1:]
    half, quarter, data = who_ref[0], who_ref[1], who_ref[2]
    for copy in copies[:2 * quarters + 1]:
        copy.wait()
    total = left_refs[0][...]
    for left_ref in left_refs[1:]:
        total = total + left_ref[...].astype(jnp.float32)
    row_ref[...] = total
    piece = right_refs[0].shape[1]
    for d, right_ref in enumerate(right_refs):
        col_ref[:, pl.ds(pl.multiple_of((quarter ^ d) * piece, piece), piece)] = right_ref[...].astype(jnp.float32)
    numbers = lax.broadcasted_iota(jnp.int32, (SEQ_DEV, 1), 0)
    owned = col_ref.shape[1]
    ids = ids_ref[:, pl.ds(pl.multiple_of(half * owned, 128), owned)]
    member_ref[...] = (ids == numbers).astype(jnp.bfloat16)
    rows = spread_refs[0].shape[0] // R
    for g in range(row_ref.shape[0] // rows):
        spread_ref = spread_refs[g % 2]
        for at in range(0, owned, width):
            right = col_ref[:, at:at + width]
            for r in range(rows):
                row = row_ref[g * rows + r:g * rows + r + 1, at:at + width]
                spread_ref[r * R:(r + 1) * R, at:at + width] = (row * right).astype(jnp.bfloat16)
        sketch_ref[:, g * rows * R:(g + 1) * rows * R] = lax.dot_general(
            member_ref[...], spread_ref[...], LAST, preferred_element_type=jnp.float32
        )
    entries = sketch_ref[...]
    high = entries.astype(jnp.bfloat16)
    low = (entries - high.astype(jnp.float32)).astype(jnp.bfloat16)
    both = jnp.concatenate([high, low], axis=0)
    middle = both.shape[1] // 2
    swapped = half == 1
    near = jnp.where(swapped, both[:, middle:], both[:, :middle])
    far = jnp.where(swapped, both[:, :middle], both[:, middle:])
    for copy in copies[2 * quarters + 1:]:
        copy.wait()
    rows = query_refs[0].shape[0]
    for side in range(2):
        part = lax.dot_general(near, query_refs[2 * side][...], LAST, preferred_element_type=jnp.float32)
        part = part + lax.dot_general(far, query_refs[2 * side + 1][...], LAST, preferred_element_type=jnp.float32)
        out_ref[:, pl.ds(pl.multiple_of((data ^ side) * rows, rows), rows)] = part[:SEQ_DEV] + part[SEQ_DEV:]


def score(who, left, right, ids, queries):
    operands = left + right + [ids] + queries
    columns, tokens = left[0].shape
    rows = min(4, columns)
    shape = (SEQ_DEV, 2 * queries[0].shape[0])
    return pl.pallas_call(
        functools.partial(score_kernel, len(left), min(512, tokens)),
        in_specs=[pl.BlockSpec(memory_space=pltpu.SMEM)] + [pl.BlockSpec(memory_space=pl.ANY)] * len(operands),
        out_specs=pl.BlockSpec(memory_space=pltpu.VMEM),
        out_shape=jax.ShapeDtypeStruct(shape, jnp.float32),
        scratch_shapes=[pltpu.VMEM(operand.shape, operand.dtype) for operand in operands]
        + [
            pltpu.SemaphoreType.DMA((len(operands),)),
            pltpu.VMEM((columns, tokens), jnp.float32),
            pltpu.VMEM((R, tokens), jnp.float32),
            pltpu.VMEM((SEQ_DEV, tokens), jnp.bfloat16),
            pltpu.VMEM((SEQ_DEV, columns * R), jnp.float32),
            pltpu.VMEM((rows * R, tokens), jnp.bfloat16),
            pltpu.VMEM((rows * R, tokens), jnp.bfloat16),
        ],
        compiler_params=pltpu.CompilerParams(vmem_limit_bytes=VMEM // 3),
        cost_estimate=pl.CostEstimate(flops=2 * tokens * columns * R * SEQ_DEV, bytes_accessed=4 * columns * tokens, transcendentals=0),
        name="score",
    )(who, *operands)


def body(n_tensor, activations, out_grads, proj_in, proj_out, segment_ids, queries):
    quarters = n_tensor // 2
    me = lax.axis_index("tensor").astype(jnp.int32)
    half = me % 2
    who = jnp.stack([half, me // 2, lax.axis_index("dp").astype(jnp.int32)])
    owned = activations.shape[0] // 2
    early = owned * 5 // 8

    def swap(array, distance):
        return lax.ppermute(array, "tensor", [(k, k ^ distance) for k in range(n_tensor)])

    def cross(array):
        return lax.ppermute(array, "dp", [(0, 1), (1, 0)])

    far = swap(queries, 1)
    cross_near, cross_far = cross(queries), cross(far)
    every = [queries, far, cross_near, cross_far]

    bits_in, bits_out = proj_in.T, proj_out.T
    scale_in, scale_out = FF ** -0.5, D ** -0.5
    sent_g, kept_g = project(out_grads, bits_out, who, scale_out, quarters, False, 0, owned, 1024)
    got_g = swap(sent_g, 1)
    sent_0, kept_0 = project(activations, bits_in, who, scale_in, quarters, True, 0, early, 512)
    got_0 = swap(sent_0, 1)
    pair_g = [kept_g[d] + got_g[d].astype(jnp.float32) for d in range(quarters)]
    pair_g = [pair_g[0]] + [pair.astype(jnp.bfloat16) for pair in pair_g[1:]]
    moved_g = [swap(pair_g[d], 2 * d) for d in range(1, quarters)]
    sent_1, kept_1 = project(activations, bits_in, who, scale_in, quarters, True, early, owned - early, 512, [pair_g[1], far, cross_near])
    got_1 = swap(sent_1, 1)
    own_g = sum([moved.astype(jnp.float32) for moved in moved_g], pair_g[0]).astype(jnp.bfloat16)
    pieces = {0: own_g}
    step = quarters // 2
    while step:
        pieces.update({d ^ step: swap(piece, 2 * step) for d, piece in list(pieces.items())})
        step = step // 2
    right = [pieces[d] for d in range(quarters)]
    pair_a = merge([kept_0, got_0, kept_1, got_1])
    left = [pair_a[0]] + [swap(pair_a[d], 2 * d) for d in range(1, quarters)]

    total = score(who, left, right, segment_ids, every)
    total = (total + swap(total, 1)).astype(jnp.bfloat16)
    parts = [total] + [swap(total, 2 * d) for d in range(1, quarters)]
    parts = [part.astype(jnp.float32) for part in parts]
    while len(parts) > 1:
        parts = [parts[k] + parts[k + 1] for k in range(0, len(parts), 2)]
    return parts[0]


def solution(mesh):
    return jax.shard_map(
        functools.partial(body, mesh.shape["tensor"]),
        mesh=mesh,
        in_specs=(
            P(("copies", "dp"), "tensor"),
            P(("copies", "dp"), "tensor"),
            P("tensor", None),
            P("tensor", None),
            P(("copies", "dp"), None),
            P(("copies", "dp"), "tensor"),
        ),
        out_specs=P(("copies", "dp"), None),
        check_vma=False,
    )
```

```python
import functools

import jax
import jax.numpy as jnp
from jax import lax
from jax.experimental import pallas as pl
from jax.experimental.pallas import tpu as pltpu
from jax.sharding import PartitionSpec as P

D = 8192
FF = 28672
R = 64
SEQ_DEV = 64
BUFFERS = 4
VMEM = 48 * 1024 * 1024
LAST = (((1,), (1,)), ((), ()))


def project_kernel(scale, order, first, split, who_ref, x_hbm, bits_hbm, *refs):
    sent_ref, kept_ref, bits_ref, signs_ref, x_buf, bits_sem, sems = refs[-7:]
    half, quarter = who_ref[0], who_ref[1]
    buffers, tile = x_buf.shape[0], x_buf.shape[1]
    steps = sent_ref.size // R // tile

    def copy(s, mine):
        slot = lax.rem(s + mine * steps, buffers)
        row = pl.multiple_of((half ^ 1 ^ mine) * (x_hbm.shape[0] // 2) + first + s * tile, tile)
        return pltpu.make_async_copy(x_hbm.at[pl.ds(row, tile)], x_buf.at[slot], sems.at[slot])

    bits_copy = pltpu.make_async_copy(bits_hbm, bits_ref, bits_sem)
    bits_copy.start()
    ahead = min(buffers, steps)
    for s in range(ahead):
        copy(s, 0).start()
    bits_copy.wait()
    for q in range(max(order, 1)):
        rows = R // max(order, 1)
        at = pl.multiple_of((q ^ quarter) * rows, rows) if order else 0
        signs_ref[q * rows:(q + 1) * rows, :] = (2 * bits_ref[pl.ds(at, rows), :] - 1).astype(jnp.bfloat16)

    for mine, out_ref in enumerate((sent_ref, kept_ref)):
        def one(s, carry):
            copy(s, mine).wait()
            slot = lax.rem(s + mine * steps, buffers)
            part = lax.dot_general(signs_ref[...], x_buf[slot], LAST, preferred_element_type=jnp.float32) * scale
            part = part.astype(out_ref.dtype)
            if split:
                here = pl.ds(pl.multiple_of(lax.rem(s, split) * tile, tile), tile)
                out_ref[(s // split) ^ quarter, :, here] = part
            else:
                here = pl.ds(pl.multiple_of(s * tile, tile), tile)
                out_ref[:, :, here] = part.reshape(out_ref.shape[0], out_ref.shape[1], tile)

            @pl.when(s + ahead < steps)
            def _():
                copy(s + ahead, mine).start()

            if not mine:
                @pl.when(s + ahead >= steps)
                def _():
                    copy(s + ahead - steps, 1).start()

            return carry

        lax.fori_loop(0, steps, one, 0)


def project(x, bits, who, scale, quarters, by_column, first, count, tile, after=()):
    width = x.shape[1]
    piece = count // quarters
    order, split = 0, 0
    if not by_column:
        tile = min(tile, piece)
        split = piece // tile
        shape = (quarters, R, piece)
    else:
        shape = (quarters, R // quarters, count)
        if (R // quarters) % 8:
            rows = jnp.arange(R, dtype=jnp.int32)
            bits = jnp.take(bits, rows ^ (who[1] * (R // quarters)), axis=0)
        else:
            order = quarters
    whole = pl.BlockSpec(memory_space=pltpu.VMEM)
    buffers = min(BUFFERS, count // tile)
    return pl.pallas_call(
        functools.partial(project_kernel, scale, order, first, split),
        in_specs=[pl.BlockSpec(memory_space=pltpu.SMEM)] + [pl.BlockSpec(memory_space=pl.ANY)] * (2 + len(after)),
        out_specs=[whole, whole],
        scratch_shapes=[
            pltpu.VMEM((R, width), jnp.int32),
            pltpu.VMEM((R, width), jnp.bfloat16),
            pltpu.VMEM((buffers, tile, width), jnp.bfloat16),
            pltpu.SemaphoreType.DMA,
            pltpu.SemaphoreType.DMA((buffers,)),
        ],
        out_shape=[jax.ShapeDtypeStruct(shape, jnp.bfloat16), jax.ShapeDtypeStruct(shape, jnp.float32)],
        compiler_params=pltpu.CompilerParams(vmem_limit_bytes=VMEM),
        cost_estimate=pl.CostEstimate(flops=4 * count * width * R, bytes_accessed=4 * count * width, transcendentals=0),
        name="project",
    )(who, x, bits, *after)


def fetch_all(sources, targets, sems):
    copies = [pltpu.make_async_copy(source, target, sems.at[k]) for k, (source, target) in enumerate(zip(sources, targets))]
    for copy in copies:
        copy.start()
    return copies


def merge_kernel(chunks, *refs):
    sources, outs = refs[:2 * chunks], refs[2 * chunks:-2 * chunks - 1]
    targets, sems = refs[-2 * chunks - 1:-1], refs[-1]
    copies = fetch_all(sources, targets, sems)
    at = 0
    for c in range(chunks):
        kept_ref, got_ref = targets[2 * c], targets[2 * c + 1]
        copies[2 * c].wait()
        copies[2 * c + 1].wait()
        width = kept_ref.shape[2]
        for d, out_ref in enumerate(outs):
            out_ref[:, at:at + width] = (kept_ref[d] + got_ref[d].astype(jnp.float32)).astype(out_ref.dtype)
        at = at + width


def merge(arrays):
    quarters, rows = arrays[0].shape[:2]
    tokens = sum(array.shape[2] for array in arrays[::2])
    whole = pl.BlockSpec(memory_space=pltpu.VMEM)
    return pl.pallas_call(
        functools.partial(merge_kernel, len(arrays) // 2),
        in_specs=[pl.BlockSpec(memory_space=pl.ANY)] * len(arrays),
        out_specs=[whole] * quarters,
        out_shape=[jax.ShapeDtypeStruct((rows, tokens), jnp.bfloat16 if d else jnp.float32) for d in range(quarters)],
        scratch_shapes=[pltpu.VMEM(array.shape, array.dtype) for array in arrays] + [pltpu.SemaphoreType.DMA((len(arrays),))],
        compiler_params=pltpu.CompilerParams(vmem_limit_bytes=VMEM // 6),
        cost_estimate=pl.CostEstimate(flops=quarters * rows * tokens, bytes_accessed=8 * quarters * rows * tokens, transcendentals=0),
        name="merge",
    )(*arrays)


def score_kernel(quarters, width, who_ref, *refs):
    count = 2 * quarters + 5
    sources, out_ref, targets = refs[:count], refs[count], refs[count + 1:2 * count + 1]
    sems, row_ref, col_ref, member_ref, sketch_ref = refs[2 * count + 1:-2]
    spread_refs = refs[-2:]
    copies = fetch_all(sources, targets, sems)
    left_refs, right_refs = targets[:quarters], targets[quarters:2 * quarters]
    ids_ref, query_refs = targets[2 * quarters], targets[2 * quarters + 1:]
    half, quarter, data = who_ref[0], who_ref[1], who_ref[2]
    for copy in copies[:2 * quarters + 1]:
        copy.wait()
    total = left_refs[0][...]
    for left_ref in left_refs[1:]:
        total = total + left_ref[...].astype(jnp.float32)
    row_ref[...] = total
    piece = right_refs[0].shape[1]
    for d, right_ref in enumerate(right_refs):
        col_ref[:, pl.ds(pl.multiple_of((quarter ^ d) * piece, piece), piece)] = right_ref[...].astype(jnp.float32)
    numbers = lax.broadcasted_iota(jnp.int32, (SEQ_DEV, 1), 0)
    owned = col_ref.shape[1]
    ids = ids_ref[:, pl.ds(pl.multiple_of(half * owned, 128), owned)]
    member_ref[...] = (ids == numbers).astype(jnp.bfloat16)
    rows = spread_refs[0].shape[0] // R
    for g in range(row_ref.shape[0] // rows):
        spread_ref = spread_refs[g % 2]
        for at in range(0, owned, width):
            right = col_ref[:, at:at + width]
            for r in range(rows):
                row = row_ref[g * rows + r:g * rows + r + 1, at:at + width]
                spread_ref[r * R:(r + 1) * R, at:at + width] = (row * right).astype(jnp.bfloat16)
        sketch_ref[:, g * rows * R:(g + 1) * rows * R] = lax.dot_general(
            member_ref[...], spread_ref[...], LAST, preferred_element_type=jnp.float32
        )
    entries = sketch_ref[...]
    high = entries.astype(jnp.bfloat16)
    low = (entries - high.astype(jnp.float32)).astype(jnp.bfloat16)
    both = jnp.concatenate([high, low], axis=0)
    middle = both.shape[1] // 2
    swapped = half == 1
    near = jnp.where(swapped, both[:, middle:], both[:, :middle])
    far = jnp.where(swapped, both[:, :middle], both[:, middle:])
    for copy in copies[2 * quarters + 1:]:
        copy.wait()
    rows = query_refs[0].shape[0]
    for side in range(2):
        part = lax.dot_general(near, query_refs[2 * side][...], LAST, preferred_element_type=jnp.float32)
        part = part + lax.dot_general(far, query_refs[2 * side + 1][...], LAST, preferred_element_type=jnp.float32)
        out_ref[:, pl.ds(pl.multiple_of((data ^ side) * rows, rows), rows)] = part[:SEQ_DEV] + part[SEQ_DEV:]


def score(who, left, right, ids, queries):
    operands = left + right + [ids] + queries
    columns, tokens = left[0].shape
    rows = min(4, columns)
    shape = (SEQ_DEV, 2 * queries[0].shape[0])
    return pl.pallas_call(
        functools.partial(score_kernel, len(left), min(512, tokens)),
        in_specs=[pl.BlockSpec(memory_space=pltpu.SMEM)] + [pl.BlockSpec(memory_space=pl.ANY)] * len(operands),
        out_specs=pl.BlockSpec(memory_space=pltpu.VMEM),
        out_shape=jax.ShapeDtypeStruct(shape, jnp.float32),
        scratch_shapes=[pltpu.VMEM(operand.shape, operand.dtype) for operand in operands]
        + [
            pltpu.SemaphoreType.DMA((len(operands),)),
            pltpu.VMEM((columns, tokens), jnp.float32),
            pltpu.VMEM((R, tokens), jnp.float32),
            pltpu.VMEM((SEQ_DEV, tokens), jnp.bfloat16),
            pltpu.VMEM((SEQ_DEV, columns * R), jnp.float32),
            pltpu.VMEM((rows * R, tokens), jnp.bfloat16),
            pltpu.VMEM((rows * R, tokens), jnp.bfloat16),
        ],
        compiler_params=pltpu.CompilerParams(vmem_limit_bytes=VMEM // 3),
        cost_estimate=pl.CostEstimate(flops=2 * tokens * columns * R * SEQ_DEV, bytes_accessed=4 * columns * tokens, transcendentals=0),
        name="score",
    )(who, *operands)


def body(n_tensor, activations, out_grads, proj_in, proj_out, segment_ids, queries):
    quarters = n_tensor // 2
    me = lax.axis_index("tensor").astype(jnp.int32)
    half = me % 2
    who = jnp.stack([half, me // 2, lax.axis_index("dp").astype(jnp.int32)])
    owned = activations.shape[0] // 2
    early = owned * 5 // 8

    def swap(array, distance):
        return lax.ppermute(array, "tensor", [(k, k ^ distance) for k in range(n_tensor)])

    def along(arrays):
        moved = {d: swap(arrays[d], 2 * d) for d in range(quarters - 1, 0, -1)}
        return [moved[d] for d in range(1, quarters)]

    def cross(array):
        return lax.ppermute(array, "dp", [(0, 1), (1, 0)])

    far = swap(queries, 1)
    cross_near, cross_far = cross(queries), cross(far)
    every = [queries, far, cross_near, cross_far]

    bits_in, bits_out = proj_in.T, proj_out.T
    scale_in, scale_out = FF ** -0.5, D ** -0.5
    sent_g, kept_g = project(out_grads, bits_out, who, scale_out, quarters, False, 0, owned, 1024)
    got_g = swap(sent_g, 1)
    sent_0, kept_0 = project(activations, bits_in, who, scale_in, quarters, True, 0, early, 512)
    got_0 = swap(sent_0, 1)
    pair_g = [kept_g[d] + got_g[d].astype(jnp.float32) for d in range(quarters)]
    pair_g = [pair_g[0]] + [pair.astype(jnp.bfloat16) for pair in pair_g[1:]]
    moved_g = along(pair_g)
    sent_1, kept_1 = project(activations, bits_in, who, scale_in, quarters, True, early, owned - early, 512, [pair_g[1], far, cross_near])
    got_1 = swap(sent_1, 1)
    own_g = sum([moved.astype(jnp.float32) for moved in moved_g], pair_g[0]).astype(jnp.bfloat16)
    pieces = {0: own_g}
    step = quarters // 2
    while step:
        pieces.update({d ^ step: swap(piece, 2 * step) for d, piece in list(pieces.items())})
        step = step // 2
    right = [pieces[d] for d in range(quarters)]
    pair_a = merge([kept_0, got_0, kept_1, got_1])
    left = [pair_a[0]] + along(pair_a)[::-1]

    total = score(who, left, right, segment_ids, every)
    total = (total + swap(total, 1)).astype(jnp.bfloat16)
    parts = [total] + along([total] * quarters)
    parts = [part.astype(jnp.float32) for part in parts[::-1]]
    while len(parts) > 1:
        parts = [parts[k] + parts[k + 1] for k in range(0, len(parts), 2)]
    return parts[0]


def solution(mesh):
    return jax.shard_map(
        functools.partial(body, mesh.shape["tensor"]),
        mesh=mesh,
        in_specs=(
            P(("copies", "dp"), "tensor"),
            P(("copies", "dp"), "tensor"),
            P("tensor", None),
            P("tensor", None),
            P(("copies", "dp"), None),
            P(("copies", "dp"), "tensor"),
        ),
        out_specs=P(("copies", "dp"), None),
        check_vma=False,
    )
```

```python
import functools

import jax
import jax.numpy as jnp
from jax import lax
from jax.experimental import pallas as pl
from jax.experimental.pallas import tpu as pltpu
from jax.sharding import PartitionSpec as P

D = 8192
FF = 28672
R = 64
SEQ_DEV = 64
BUFFERS = 4
VMEM = 48 * 1024 * 1024
LAST = (((1,), (1,)), ((), ()))


def project_kernel(scale, order, first, split, who_ref, x_hbm, bits_hbm, *refs):
    sent_ref, kept_ref, bits_ref, signs_ref, x_buf, bits_sem, sems = refs[-7:]
    half, quarter = who_ref[0], who_ref[1]
    buffers, tile = x_buf.shape[0], x_buf.shape[1]
    steps = sent_ref.size // R // tile

    def copy(s, mine):
        slot = lax.rem(s + mine * steps, buffers)
        row = pl.multiple_of((half ^ 1 ^ mine) * (x_hbm.shape[0] // 2) + first + s * tile, tile)
        return pltpu.make_async_copy(x_hbm.at[pl.ds(row, tile)], x_buf.at[slot], sems.at[slot])

    bits_copy = pltpu.make_async_copy(bits_hbm, bits_ref, bits_sem)
    bits_copy.start()
    ahead = min(buffers, steps)
    for s in range(ahead):
        copy(s, 0).start()
    bits_copy.wait()
    for q in range(max(order, 1)):
        rows = R // max(order, 1)
        at = pl.multiple_of((q ^ quarter) * rows, rows) if order else 0
        signs_ref[q * rows:(q + 1) * rows, :] = (2 * bits_ref[pl.ds(at, rows), :] - 1).astype(jnp.bfloat16)

    for mine, out_ref in enumerate((sent_ref, kept_ref)):
        def one(s, carry):
            copy(s, mine).wait()
            slot = lax.rem(s + mine * steps, buffers)
            part = lax.dot_general(signs_ref[...], x_buf[slot], LAST, preferred_element_type=jnp.float32) * scale
            part = part.astype(out_ref.dtype)
            if split:
                here = pl.ds(pl.multiple_of(lax.rem(s, split) * tile, tile), tile)
                out_ref[(s // split) ^ quarter, :, here] = part
            else:
                here = pl.ds(pl.multiple_of(s * tile, tile), tile)
                out_ref[:, :, here] = part.reshape(out_ref.shape[0], out_ref.shape[1], tile)

            @pl.when(s + ahead < steps)
            def _():
                copy(s + ahead, mine).start()

            if not mine:
                @pl.when(s + ahead >= steps)
                def _():
                    copy(s + ahead - steps, 1).start()

            return carry

        lax.fori_loop(0, steps, one, 0)


def project(x, bits, who, scale, quarters, by_column, first, count, tile, after=()):
    width = x.shape[1]
    piece = count // quarters
    order, split = 0, 0
    if not by_column:
        tile = min(tile, piece)
        split = piece // tile
        shape = (quarters, R, piece)
    else:
        shape = (quarters, R // quarters, count)
        if (R // quarters) % 8:
            rows = jnp.arange(R, dtype=jnp.int32)
            bits = jnp.take(bits, rows ^ (who[1] * (R // quarters)), axis=0)
        else:
            order = quarters
    whole = pl.BlockSpec(memory_space=pltpu.VMEM)
    buffers = min(BUFFERS, count // tile)
    return pl.pallas_call(
        functools.partial(project_kernel, scale, order, first, split),
        in_specs=[pl.BlockSpec(memory_space=pltpu.SMEM)] + [pl.BlockSpec(memory_space=pl.ANY)] * (2 + len(after)),
        out_specs=[whole, whole],
        scratch_shapes=[
            pltpu.VMEM((R, width), jnp.int32),
            pltpu.VMEM((R, width), jnp.bfloat16),
            pltpu.VMEM((buffers, tile, width), jnp.bfloat16),
            pltpu.SemaphoreType.DMA,
            pltpu.SemaphoreType.DMA((buffers,)),
        ],
        out_shape=[jax.ShapeDtypeStruct(shape, jnp.bfloat16), jax.ShapeDtypeStruct(shape, jnp.float32)],
        compiler_params=pltpu.CompilerParams(vmem_limit_bytes=VMEM),
        cost_estimate=pl.CostEstimate(flops=4 * count * width * R, bytes_accessed=4 * count * width, transcendentals=0),
        name="project",
    )(who, x, bits, *after)


def fetch_all(sources, targets, sems):
    copies = [pltpu.make_async_copy(source, target, sems.at[k]) for k, (source, target) in enumerate(zip(sources, targets))]
    for copy in copies:
        copy.start()
    return copies


def merge_kernel(chunks, *refs):
    sources, outs = refs[:2 * chunks], refs[2 * chunks:-2 * chunks - 1]
    targets, sems = refs[-2 * chunks - 1:-1], refs[-1]
    copies = fetch_all(sources, targets, sems)
    at = 0
    for c in range(chunks):
        kept_ref, got_ref = targets[2 * c], targets[2 * c + 1]
        copies[2 * c].wait()
        copies[2 * c + 1].wait()
        width = kept_ref.shape[2]
        for d, out_ref in enumerate(outs):
            out_ref[:, at:at + width] = (kept_ref[d] + got_ref[d].astype(jnp.float32)).astype(out_ref.dtype)
        at = at + width


def merge(arrays):
    quarters, rows = arrays[0].shape[:2]
    tokens = sum(array.shape[2] for array in arrays[::2])
    whole = pl.BlockSpec(memory_space=pltpu.VMEM)
    return pl.pallas_call(
        functools.partial(merge_kernel, len(arrays) // 2),
        in_specs=[pl.BlockSpec(memory_space=pl.ANY)] * len(arrays),
        out_specs=[whole] * quarters,
        out_shape=[jax.ShapeDtypeStruct((rows, tokens), jnp.bfloat16 if d else jnp.float32) for d in range(quarters)],
        scratch_shapes=[pltpu.VMEM(array.shape, array.dtype) for array in arrays] + [pltpu.SemaphoreType.DMA((len(arrays),))],
        compiler_params=pltpu.CompilerParams(vmem_limit_bytes=VMEM // 6),
        cost_estimate=pl.CostEstimate(flops=quarters * rows * tokens, bytes_accessed=8 * quarters * rows * tokens, transcendentals=0),
        name="merge",
    )(*arrays)


def score_kernel(quarters, width, who_ref, *refs):
    count = 2 * quarters + 5
    sources, out_ref, targets = refs[:count], refs[count], refs[count + 1:2 * count + 1]
    sems, row_ref, col_ref, member_ref, sketch_ref = refs[2 * count + 1:-2]
    spread_refs = refs[-2:]
    copies = fetch_all(sources, targets, sems)
    left_refs, right_refs = targets[:quarters], targets[quarters:2 * quarters]
    ids_ref, query_refs = targets[2 * quarters], targets[2 * quarters + 1:]
    half, quarter, data = who_ref[0], who_ref[1], who_ref[2]
    for copy in copies[:2 * quarters + 1]:
        copy.wait()
    total = left_refs[0][...]
    for left_ref in left_refs[1:]:
        total = total + left_ref[...].astype(jnp.float32)
    row_ref[...] = total
    piece = right_refs[0].shape[1]
    for d, right_ref in enumerate(right_refs):
        col_ref[:, pl.ds(pl.multiple_of((quarter ^ d) * piece, piece), piece)] = right_ref[...].astype(jnp.float32)
    numbers = lax.broadcasted_iota(jnp.int32, (SEQ_DEV, 1), 0)
    owned = col_ref.shape[1]
    ids = ids_ref[:, pl.ds(pl.multiple_of(half * owned, 128), owned)]
    member_ref[...] = (ids == numbers).astype(jnp.bfloat16)
    columns = row_ref.shape[0]
    blocks = owned // width
    sketch_ref[...] = jnp.zeros(sketch_ref.shape, jnp.float32)

    def fill(spread_ref, block):
        here = pl.ds(pl.multiple_of(block * width, width), width)
        right = col_ref[:, here]
        for r in range(columns):
            spread_ref[r * R:(r + 1) * R, :] = (row_ref[r:r + 1, here] * right).astype(jnp.bfloat16)

    def add(spread_ref, block):
        here = pl.ds(pl.multiple_of(block * width, width), width)
        sketch_ref[...] += lax.dot_general(member_ref[:, here], spread_ref[...], LAST, preferred_element_type=jnp.float32)

    def two(k, carry):
        fill(spread_refs[1], 2 * k + 1)
        add(spread_refs[0], 2 * k)
        fill(spread_refs[0], jnp.minimum(2 * k + 2, blocks - 1))
        add(spread_refs[1], 2 * k + 1)
        return carry

    fill(spread_refs[0], 0)
    lax.fori_loop(0, blocks // 2, two, 0)
    entries = sketch_ref[...]
    high = entries.astype(jnp.bfloat16)
    low = (entries - high.astype(jnp.float32)).astype(jnp.bfloat16)
    both = jnp.concatenate([high, low], axis=0)
    middle = both.shape[1] // 2
    swapped = half == 1
    near = jnp.where(swapped, both[:, middle:], both[:, :middle])
    far = jnp.where(swapped, both[:, :middle], both[:, middle:])
    for copy in copies[2 * quarters + 1:]:
        copy.wait()
    rows = query_refs[0].shape[0]
    for side in range(2):
        part = lax.dot_general(near, query_refs[2 * side][...], LAST, preferred_element_type=jnp.float32)
        part = part + lax.dot_general(far, query_refs[2 * side + 1][...], LAST, preferred_element_type=jnp.float32)
        out_ref[:, pl.ds(pl.multiple_of((data ^ side) * rows, rows), rows)] = part[:SEQ_DEV] + part[SEQ_DEV:]


def score(who, left, right, ids, queries):
    operands = left + right + [ids] + queries
    columns, tokens = left[0].shape
    width = min(512, tokens // 2)
    shape = (SEQ_DEV, 2 * queries[0].shape[0])
    return pl.pallas_call(
        functools.partial(score_kernel, len(left), width),
        in_specs=[pl.BlockSpec(memory_space=pltpu.SMEM)] + [pl.BlockSpec(memory_space=pl.ANY)] * len(operands),
        out_specs=pl.BlockSpec(memory_space=pltpu.VMEM),
        out_shape=jax.ShapeDtypeStruct(shape, jnp.float32),
        scratch_shapes=[pltpu.VMEM(operand.shape, operand.dtype) for operand in operands]
        + [
            pltpu.SemaphoreType.DMA((len(operands),)),
            pltpu.VMEM((columns, tokens), jnp.float32),
            pltpu.VMEM((R, tokens), jnp.float32),
            pltpu.VMEM((SEQ_DEV, tokens), jnp.bfloat16),
            pltpu.VMEM((SEQ_DEV, columns * R), jnp.float32),
            pltpu.VMEM((columns * R, width), jnp.bfloat16),
            pltpu.VMEM((columns * R, width), jnp.bfloat16),
        ],
        compiler_params=pltpu.CompilerParams(vmem_limit_bytes=VMEM // 3),
        cost_estimate=pl.CostEstimate(flops=2 * tokens * columns * R * SEQ_DEV, bytes_accessed=4 * columns * tokens, transcendentals=0),
        name="score",
    )(who, *operands)


def body(n_tensor, activations, out_grads, proj_in, proj_out, segment_ids, queries):
    quarters = n_tensor // 2
    me = lax.axis_index("tensor").astype(jnp.int32)
    half = me % 2
    who = jnp.stack([half, me // 2, lax.axis_index("dp").astype(jnp.int32)])
    owned = activations.shape[0] // 2
    early = owned * 5 // 8

    def swap(array, distance):
        return lax.ppermute(array, "tensor", [(k, k ^ distance) for k in range(n_tensor)])

    def along(arrays):
        moved = {d: swap(arrays[d], 2 * d) for d in range(quarters - 1, 0, -1)}
        return [moved[d] for d in range(1, quarters)]

    def cross(array):
        return lax.ppermute(array, "dp", [(0, 1), (1, 0)])

    far = swap(queries, 1)
    cross_near, cross_far = cross(queries), cross(far)
    every = [queries, far, cross_near, cross_far]

    bits_in, bits_out = proj_in.T, proj_out.T
    scale_in, scale_out = FF ** -0.5, D ** -0.5
    sent_g, kept_g = project(out_grads, bits_out, who, scale_out, quarters, False, 0, owned, 1024)
    got_g = swap(sent_g, 1)
    sent_0, kept_0 = project(activations, bits_in, who, scale_in, quarters, True, 0, early, 512)
    got_0 = swap(sent_0, 1)
    pair_g = [kept_g[d] + got_g[d].astype(jnp.float32) for d in range(quarters)]
    pair_g = [pair_g[0]] + [pair.astype(jnp.bfloat16) for pair in pair_g[1:]]
    moved_g = along(pair_g)
    sent_1, kept_1 = project(activations, bits_in, who, scale_in, quarters, True, early, owned - early, 512, [pair_g[1], far, cross_near])
    got_1 = swap(sent_1, 1)
    own_g = sum([moved.astype(jnp.float32) for moved in moved_g], pair_g[0]).astype(jnp.bfloat16)
    pieces = {0: own_g}
    step = quarters // 2
    while step:
        pieces.update({d ^ step: swap(piece, 2 * step) for d, piece in list(pieces.items())})
        step = step // 2
    right = [pieces[d] for d in range(quarters)]
    pair_a = merge([kept_0, got_0, kept_1, got_1])
    left = [pair_a[0]] + along(pair_a)[::-1]

    total = score(who, left, right, segment_ids, every)
    total = (total + swap(total, 1)).astype(jnp.bfloat16)
    parts = [total] + along([total] * quarters)
    parts = [part.astype(jnp.float32) for part in parts[::-1]]
    while len(parts) > 1:
        parts = [parts[k] + parts[k + 1] for k in range(0, len(parts), 2)]
    return parts[0]


def solution(mesh):
    return jax.shard_map(
        functools.partial(body, mesh.shape["tensor"]),
        mesh=mesh,
        in_specs=(
            P(("copies", "dp"), "tensor"),
            P(("copies", "dp"), "tensor"),
            P("tensor", None),
            P("tensor", None),
            P(("copies", "dp"), None),
            P(("copies", "dp"), "tensor"),
        ),
        out_specs=P(("copies", "dp"), None),
        check_vma=False,
    )
```

```python
import functools

import jax
import jax.numpy as jnp
from jax import lax
from jax.experimental import pallas as pl
from jax.experimental.pallas import tpu as pltpu
from jax.sharding import PartitionSpec as P

D = 8192
FF = 28672
R = 64
SEQ_DEV = 64
BUFFERS = 6
VMEM = 48 * 1024 * 1024
LAST = (((1,), (1,)), ((), ()))


def project_kernel(scale, order, first, split, who_ref, x_hbm, bits_hbm, *refs):
    sent_ref, kept_ref, bits_ref, signs_ref, x_buf, bits_sem, sems = refs[-7:]
    half, quarter = who_ref[0], who_ref[1]
    buffers, tile = x_buf.shape[0], x_buf.shape[1]
    steps = sent_ref.size // R // tile

    def copy(s, mine):
        slot = lax.rem(s + mine * steps, buffers)
        row = pl.multiple_of((half ^ 1 ^ mine) * (x_hbm.shape[0] // 2) + first + s * tile, tile)
        return pltpu.make_async_copy(x_hbm.at[pl.ds(row, tile)], x_buf.at[slot], sems.at[slot])

    bits_copy = pltpu.make_async_copy(bits_hbm, bits_ref, bits_sem)
    bits_copy.start()
    ahead = min(buffers, steps)
    for s in range(ahead):
        copy(s, 0).start()
    bits_copy.wait()
    for q in range(max(order, 1)):
        rows = R // max(order, 1)
        at = pl.multiple_of((q ^ quarter) * rows, rows) if order else 0
        signs_ref[q * rows:(q + 1) * rows, :] = (2 * bits_ref[pl.ds(at, rows), :] - 1).astype(jnp.bfloat16)

    for mine, out_ref in enumerate((sent_ref, kept_ref)):
        def one(s, carry):
            copy(s, mine).wait()
            slot = lax.rem(s + mine * steps, buffers)
            part = lax.dot_general(signs_ref[...], x_buf[slot], LAST, preferred_element_type=jnp.float32) * scale
            part = part.astype(out_ref.dtype)
            if split:
                here = pl.ds(pl.multiple_of(lax.rem(s, split) * tile, tile), tile)
                out_ref[(s // split) ^ quarter, :, here] = part
            else:
                here = pl.ds(pl.multiple_of(s * tile, tile), tile)
                out_ref[:, :, here] = part.reshape(out_ref.shape[0], out_ref.shape[1], tile)

            @pl.when(s + ahead < steps)
            def _():
                copy(s + ahead, mine).start()

            if not mine:
                @pl.when(s + ahead >= steps)
                def _():
                    copy(s + ahead - steps, 1).start()

            return carry

        lax.fori_loop(0, steps, one, 0)


def project(x, bits, who, scale, quarters, by_column, first, count, tile, after=()):
    width = x.shape[1]
    piece = count // quarters
    order, split = 0, 0
    if not by_column:
        tile = min(tile, piece)
        split = piece // tile
        shape = (quarters, R, piece)
    else:
        shape = (quarters, R // quarters, count)
        if (R // quarters) % 8:
            rows = jnp.arange(R, dtype=jnp.int32)
            bits = jnp.take(bits, rows ^ (who[1] * (R // quarters)), axis=0)
        else:
            order = quarters
    whole = pl.BlockSpec(memory_space=pltpu.VMEM)
    buffers = min(BUFFERS, count // tile)
    return pl.pallas_call(
        functools.partial(project_kernel, scale, order, first, split),
        in_specs=[pl.BlockSpec(memory_space=pltpu.SMEM)] + [pl.BlockSpec(memory_space=pl.ANY)] * (2 + len(after)),
        out_specs=[whole, whole],
        scratch_shapes=[
            pltpu.VMEM((R, width), jnp.int32),
            pltpu.VMEM((R, width), jnp.bfloat16),
            pltpu.VMEM((buffers, tile, width), jnp.bfloat16),
            pltpu.SemaphoreType.DMA,
            pltpu.SemaphoreType.DMA((buffers,)),
        ],
        out_shape=[jax.ShapeDtypeStruct(shape, jnp.bfloat16), jax.ShapeDtypeStruct(shape, jnp.float32)],
        compiler_params=pltpu.CompilerParams(vmem_limit_bytes=VMEM),
        cost_estimate=pl.CostEstimate(flops=4 * count * width * R, bytes_accessed=4 * count * width, transcendentals=0),
        name="project",
    )(who, x, bits, *after)


def fetch_all(sources, targets, sems):
    copies = [pltpu.make_async_copy(source, target, sems.at[k]) for k, (source, target) in enumerate(zip(sources, targets))]
    for copy in copies:
        copy.start()
    return copies


def merge_kernel(chunks, *refs):
    sources, outs = refs[:2 * chunks], refs[2 * chunks:-2 * chunks - 1]
    targets, sems = refs[-2 * chunks - 1:-1], refs[-1]
    copies = fetch_all(sources, targets, sems)
    at = 0
    for c in range(chunks):
        kept_ref, got_ref = targets[2 * c], targets[2 * c + 1]
        copies[2 * c].wait()
        copies[2 * c + 1].wait()
        width = kept_ref.shape[2]
        for d, out_ref in enumerate(outs):
            out_ref[:, at:at + width] = (kept_ref[d] + got_ref[d].astype(jnp.float32)).astype(out_ref.dtype)
        at = at + width


def merge(arrays):
    quarters, rows = arrays[0].shape[:2]
    tokens = sum(array.shape[2] for array in arrays[::2])
    whole = pl.BlockSpec(memory_space=pltpu.VMEM)
    return pl.pallas_call(
        functools.partial(merge_kernel, len(arrays) // 2),
        in_specs=[pl.BlockSpec(memory_space=pl.ANY)] * len(arrays),
        out_specs=[whole] * quarters,
        out_shape=[jax.ShapeDtypeStruct((rows, tokens), jnp.bfloat16 if d else jnp.float32) for d in range(quarters)],
        scratch_shapes=[pltpu.VMEM(array.shape, array.dtype) for array in arrays] + [pltpu.SemaphoreType.DMA((len(arrays),))],
        compiler_params=pltpu.CompilerParams(vmem_limit_bytes=VMEM // 6),
        cost_estimate=pl.CostEstimate(flops=quarters * rows * tokens, bytes_accessed=8 * quarters * rows * tokens, transcendentals=0),
        name="merge",
    )(*arrays)


def score_kernel(quarters, width, who_ref, *refs):
    count = 2 * quarters + 5
    sources, out_ref, targets = refs[:count], refs[count], refs[count + 1:2 * count + 1]
    sems, row_ref, col_ref, member_ref, sketch_ref = refs[2 * count + 1:-2]
    spread_refs = refs[-2:]
    copies = fetch_all(sources, targets, sems)
    left_refs, right_refs = targets[:quarters], targets[quarters:2 * quarters]
    ids_ref, query_refs = targets[2 * quarters], targets[2 * quarters + 1:]
    half, quarter, data = who_ref[0], who_ref[1], who_ref[2]
    for copy in copies[:2 * quarters + 1]:
        copy.wait()
    total = left_refs[0][...]
    for left_ref in left_refs[1:]:
        total = total + left_ref[...].astype(jnp.float32)
    row_ref[...] = total
    piece = right_refs[0].shape[1]
    for d, right_ref in enumerate(right_refs):
        col_ref[:, pl.ds(pl.multiple_of((quarter ^ d) * piece, piece), piece)] = right_ref[...].astype(jnp.float32)
    numbers = lax.broadcasted_iota(jnp.int32, (SEQ_DEV, 1), 0)
    owned = col_ref.shape[1]
    ids = ids_ref[:, pl.ds(pl.multiple_of(half * owned, 128), owned)]
    member_ref[...] = (ids == numbers).astype(jnp.bfloat16)
    rows = spread_refs[0].shape[0] // R
    for g in range(row_ref.shape[0] // rows):
        spread_ref = spread_refs[g % 2]
        for at in range(0, owned, width):
            right = col_ref[:, at:at + width]
            for r in range(rows):
                row = row_ref[g * rows + r:g * rows + r + 1, at:at + width]
                spread_ref[r * R:(r + 1) * R, at:at + width] = (row * right).astype(jnp.bfloat16)
        sketch_ref[:, g * rows * R:(g + 1) * rows * R] = lax.dot_general(
            member_ref[...], spread_ref[...], LAST, preferred_element_type=jnp.float32
        )
    entries = sketch_ref[...]
    high = entries.astype(jnp.bfloat16)
    low = (entries - high.astype(jnp.float32)).astype(jnp.bfloat16)
    both = jnp.concatenate([high, low], axis=0)
    middle = both.shape[1] // 2
    swapped = half == 1
    near = jnp.where(swapped, both[:, middle:], both[:, :middle])
    far = jnp.where(swapped, both[:, :middle], both[:, middle:])
    for copy in copies[2 * quarters + 1:]:
        copy.wait()
    rows = query_refs[0].shape[0]
    for side in range(2):
        part = lax.dot_general(near, query_refs[2 * side][...], LAST, preferred_element_type=jnp.float32)
        part = part + lax.dot_general(far, query_refs[2 * side + 1][...], LAST, preferred_element_type=jnp.float32)
        out_ref[:, pl.ds(pl.multiple_of((data ^ side) * rows, rows), rows)] = part[:SEQ_DEV] + part[SEQ_DEV:]


def score(who, left, right, ids, queries):
    operands = left + right + [ids] + queries
    columns, tokens = left[0].shape
    rows = min(4, columns)
    shape = (SEQ_DEV, 2 * queries[0].shape[0])
    return pl.pallas_call(
        functools.partial(score_kernel, len(left), min(512, tokens)),
        in_specs=[pl.BlockSpec(memory_space=pltpu.SMEM)] + [pl.BlockSpec(memory_space=pl.ANY)] * len(operands),
        out_specs=pl.BlockSpec(memory_space=pltpu.VMEM),
        out_shape=jax.ShapeDtypeStruct(shape, jnp.float32),
        scratch_shapes=[pltpu.VMEM(operand.shape, operand.dtype) for operand in operands]
        + [
            pltpu.SemaphoreType.DMA((len(operands),)),
            pltpu.VMEM((columns, tokens), jnp.float32),
            pltpu.VMEM((R, tokens), jnp.float32),
            pltpu.VMEM((SEQ_DEV, tokens), jnp.bfloat16),
            pltpu.VMEM((SEQ_DEV, columns * R), jnp.float32),
            pltpu.VMEM((rows * R, tokens), jnp.bfloat16),
            pltpu.VMEM((rows * R, tokens), jnp.bfloat16),
        ],
        compiler_params=pltpu.CompilerParams(vmem_limit_bytes=VMEM // 3),
        cost_estimate=pl.CostEstimate(flops=2 * tokens * columns * R * SEQ_DEV, bytes_accessed=4 * columns * tokens, transcendentals=0),
        name="score",
    )(who, *operands)


def body(n_tensor, activations, out_grads, proj_in, proj_out, segment_ids, queries):
    quarters = n_tensor // 2
    me = lax.axis_index("tensor").astype(jnp.int32)
    half = me % 2
    who = jnp.stack([half, me // 2, lax.axis_index("dp").astype(jnp.int32)])
    owned = activations.shape[0] // 2
    early = owned * 5 // 8

    def swap(array, distance):
        return lax.ppermute(array, "tensor", [(k, k ^ distance) for k in range(n_tensor)])

    def along(arrays):
        moved = {d: swap(arrays[d], 2 * d) for d in range(quarters - 1, 0, -1)}
        return [moved[d] for d in range(1, quarters)]

    def cross(array):
        return lax.ppermute(array, "dp", [(0, 1), (1, 0)])

    far = swap(queries, 1)
    cross_near, cross_far = cross(queries), cross(far)
    every = [queries, far, cross_near, cross_far]

    bits_in, bits_out = proj_in.T, proj_out.T
    scale_in, scale_out = FF ** -0.5, D ** -0.5
    sent_g, kept_g = project(out_grads, bits_out, who, scale_out, quarters, False, 0, owned, 1024)
    got_g = swap(sent_g, 1)
    sent_0, kept_0 = project(activations, bits_in, who, scale_in, quarters, True, 0, early, 512)
    got_0 = swap(sent_0, 1)
    pair_g = [kept_g[d] + got_g[d].astype(jnp.float32) for d in range(quarters)]
    pair_g = [pair_g[0]] + [pair.astype(jnp.bfloat16) for pair in pair_g[1:]]
    moved_g = along(pair_g)
    sent_1, kept_1 = project(activations, bits_in, who, scale_in, quarters, True, early, owned - early, 512, [pair_g[1], far, cross_near])
    got_1 = swap(sent_1, 1)
    own_g = sum([moved.astype(jnp.float32) for moved in moved_g], pair_g[0]).astype(jnp.bfloat16)
    pieces = {0: own_g}
    step = quarters // 2
    while step:
        pieces.update({d ^ step: swap(piece, 2 * step) for d, piece in list(pieces.items())})
        step = step // 2
    right = [pieces[d] for d in range(quarters)]
    pair_a = merge([kept_0, got_0, kept_1, got_1])
    left = [pair_a[0]] + along(pair_a)[::-1]

    total = score(who, left, right, segment_ids, every)
    total = (total + swap(total, 1)).astype(jnp.bfloat16)
    parts = [total] + along([total] * quarters)
    parts = [part.astype(jnp.float32) for part in parts[::-1]]
    while len(parts) > 1:
        parts = [parts[k] + parts[k + 1] for k in range(0, len(parts), 2)]
    return parts[0]


def solution(mesh):
    return jax.shard_map(
        functools.partial(body, mesh.shape["tensor"]),
        mesh=mesh,
        in_specs=(
            P(("copies", "dp"), "tensor"),
            P(("copies", "dp"), "tensor"),
            P("tensor", None),
            P("tensor", None),
            P(("copies", "dp"), None),
            P(("copies", "dp"), "tensor"),
        ),
        out_specs=P(("copies", "dp"), None),
        check_vma=False,
    )
```
